32 devices in a mesh: shard: 8 (over z, y), rep: 4 (over x, core).
Axes of the slice: x: 2, y: 2, z: 4, core: 2. Of those that a mesh axis runs over, the one named last changes fastest.
Arguments:
- tokens: bfloat16 [16, 1024, 1024], P('rep', 'shard'), may hold values from -6 to 6
- attn_gain: bfloat16 [1024], replicated, may hold values from 0.5 to 1.5
- w_query: bfloat16 [1024, 512], P('shard'), may hold values from -0.1875 to 0.1875
- w_key: bfloat16 [1024, 512], P('shard'), may hold values from -0.1875 to 0.1875
- w_value: bfloat16 [1024, 1024], P('shard'), may hold values from -0.1875 to 0.1875
- w_outgate: bfloat16 [1024, 1024], P('shard'), may hold values from -0.1875 to 0.1875
- w_rank_in: bfloat16 [1024, 16], P('shard'), may hold values from -0.1875 to 0.1875
- w_rank_out: bfloat16 [512, 16], P('shard'), may hold values from -1.5 to 1.5
- fgate_bias: bfloat16 [512], replicated, may hold values from -1 to 11
- head_gain: bfloat16 [256], replicated, may hold values from 0.5 to 1.5
- w_output: bfloat16 [1024, 1024], P('shard'), may hold values from -0.1875 to 0.1875
- ffn_gain: bfloat16 [1024], replicated, may hold values from 0.5 to 1.5
- w_gate: bfloat16 [1024, 2816], P('shard'), may hold values from -0.1875 to 0.1875
- w_up: bfloat16 [1024, 2816], P('shard'), may hold values from -0.1875 to 0.1875
- w_down: bfloat16 [2816, 1024], P('shard'), may hold values from -0.109375 to 0.109375
- out_grad: bfloat16 [16, 1024, 1024], P('rep', 'shard'), may hold values from -6 to 6
Outputs:
- block_out: bfloat16 [16, 1024, 1024], P('rep', 'shard')
- tokens_grad: bfloat16 [16, 1024, 1024], P('rep', 'shard')
- attn_gain_grad: float32 [1024], replicated
- w_query_grad: float32 [1024, 512], P('shard')
- w_key_grad: float32 [1024, 512], P('shard')
- w_value_grad: float32 [1024, 1024], P('shard')
- w_outgate_grad: float32 [1024, 1024], P('shard')
- w_rank_in_grad: float32 [1024, 16], P('shard')
- w_rank_out_grad: float32 [512, 16], P('shard')
- fgate_bias_grad: float32 [512], replicated
- head_gain_grad: float32 [256], replicated
- w_output_grad: float32 [1024, 1024], P('shard')
- ffn_gain_grad: float32 [1024], replicated
- w_gate_grad: float32 [1024, 2816], P('shard')
- w_up_grad: float32 [1024, 2816], P('shard')
- w_down_grad: float32 [2816, 1024], P('shard')
The draws below stay inside these ranges and needn't reach their ends.
All inputs are finite; a program needn't handle non-finite values.
Results may differ from the reference program's by a relative error of at most 0.009.
The reference program's roundings to bfloat16 on the way count: a program that leaves them out, or rounds other values in their place, can miss the bound.
Values may be sent and summed in bfloat16 or wider, within the bound.
No kernel may reach another device: no remote copies, remote signals or barrier semaphores. Data moves between devices by JAX's collectives and lax.ppermute only.
A program may use at most 384 MiB of HBM per device.

```python
import jax
import jax.numpy as jnp
from jax import lax

D = 1024
HEADS = 4
KD = 512
VD = 1024
RANK = 16
FF = 2816
SPAN = 64
DK = 128
DV = 256
LENGTH = 1024
SEQ_ALL = 16


def draw_fgate_bias(key, part):
    chooser, fast_key, middle_key, slow_key = jax.random.split(jax.random.fold_in(key, 7), 4)
    picks = jax.random.randint(chooser, (KD,), 0, 3)
    fast_values = jax.random.uniform(fast_key, (KD,), jnp.float32, -1.0, 3.0)
    middle_values = jax.random.uniform(middle_key, (KD,), jnp.float32, 3.0, 6.0)
    slow_values = jax.random.uniform(slow_key, (KD,), jnp.float32, 8.0, 11.0)
    chosen = jnp.where(picks == 0, fast_values, jnp.where(picks == 1, middle_values, slow_values))
    return chosen.astype(jnp.bfloat16)


def draw_tokens(key, part):
    key = jax.random.fold_in(key, 11)
    noise_key, level_key, direction_key = jax.random.split(key, 3)
    noise = jnp.clip(jax.random.normal(noise_key, (SEQ_ALL, LENGTH, D), jnp.float32), -4.0, 4.0)
    direction = jnp.clip(jax.random.normal(direction_key, (D,), jnp.float32), -2.0, 2.0)
    levels = jax.random.uniform(level_key, (SEQ_ALL, LENGTH // SPAN), jnp.float32, -1.0, 1.0)
    levels = jnp.repeat(levels, SPAN, axis=1)
    values = noise + levels[:, :, None] * direction[None, None, :]
    return jnp.clip(values, -6.0, 6.0).astype(jnp.bfloat16)


def block_levels(own_key, shape, shards, low, top_value):
    gain = 1.0
    for position, blocks in shards:
        heights = jax.random.uniform(jax.random.fold_in(jax.random.fold_in(own_key, 6), position), (blocks,), jnp.float32, low / len(shards), top_value / len(shards))
        gain = gain * jnp.repeat(jnp.exp(heights), shape[position] // blocks).reshape((-1,) + (1,) * (len(shape) - 1 - position))
    return gain


def bell_draw(stream_key, dims, width, bound, cuts=(), kind=jnp.bfloat16):
    entries = jax.random.normal(stream_key, dims, jnp.float32) * width
    if len(cuts) > 0:
        entries = block_levels(stream_key, dims, cuts, -0.22, 0.18) * entries
    return jnp.clip(entries, min=-bound, max=bound).astype(kind)


def setup_inputs(seed: int = 0) -> dict:
    keys = jax.random.split(jax.random.key(seed), 17)
    tokens = draw_tokens(jax.random.fold_in(keys[16], 71), 0)
    attn_gain = jnp.clip(1.0 + 0.1 * jax.random.normal(keys[1], (D,), jnp.float32), 0.5, 1.5).astype(jnp.bfloat16)
    w_query = bell_draw(keys[2], (D, KD), D ** -0.5, 0.1875, ((0, 8),))
    w_key = bell_draw(keys[3], (D, KD), D ** -0.5, 0.1875, ((0, 8),))
    w_value = bell_draw(keys[4], (D, VD), D ** -0.5, 0.1875, ((0, 8),))
    w_outgate = bell_draw(keys[5], (D, VD), D ** -0.5, 0.1875, ((0, 8),))
    w_rank_in = bell_draw(keys[6], (D, RANK), D ** -0.5, 0.1875, ((0, 8),))
    w_rank_out = bell_draw(keys[7], (KD, RANK), RANK ** -0.5, 1.5, ((0, 8),))
    fgate_bias = draw_fgate_bias(jax.random.fold_in(keys[16], 71), 0)
    head_gain = jnp.clip(1.0 + 0.1 * jax.random.normal(keys[9], (DV,), jnp.float32), 0.5, 1.5).astype(jnp.bfloat16)
    w_output = bell_draw(keys[10], (VD, D), VD ** -0.5, 0.1875, ((0, 8),))
    ffn_gain = jnp.clip(1.0 + 0.1 * jax.random.normal(keys[11], (D,), jnp.float32), 0.5, 1.5).astype(jnp.bfloat16)
    w_gate = bell_draw(keys[12], (D, FF), D ** -0.5, 0.1875, ((0, 8),))
    w_up = bell_draw(keys[13], (D, FF), D ** -0.5, 0.1875, ((0, 8),))
    w_down = bell_draw(keys[14], (FF, D), FF ** -0.5, 0.109375, ((0, 8),))
    out_grad = bell_draw(keys[15], (SEQ_ALL, LENGTH, D), 1.0, 6.0, ((0, 4), (1, 8)))
    return {"tokens": tokens, "attn_gain": attn_gain, "w_query": w_query, "w_key": w_key, "w_value": w_value, "w_outgate": w_outgate, "w_rank_in": w_rank_in, "w_rank_out": w_rank_out, "fgate_bias": fgate_bias, "head_gain": head_gain, "w_output": w_output, "ffn_gain": ffn_gain, "w_gate": w_gate, "w_up": w_up, "w_down": w_down, "out_grad": out_grad}


PRECISE = lax.Precision.HIGHEST
EPSILON = 1e-06
GATE_NORM = 16.0

@jax.custom_vjp
def low(v):
    return lax.optimization_barrier(v.astype(jnp.bfloat16)).astype(jnp.float32)

@jax.custom_vjp
def low_back(v):
    return v

def low_keep(v):
    return (low(v), None)

def low_pass(kept, grad):
    return (grad,)

def back_keep(v):
    return (v, None)

def back_low(kept, grad):
    return (low(grad),)
low.defvjp(low_keep, low_pass)
low_back.defvjp(back_keep, back_low)

def matmul_high(left_side, right_side):
    return jnp.dot(left_side, right_side, precision=PRECISE, preferred_element_type=jnp.float32)

def root_norm(values, gain_row):
    return values * lax.rsqrt(lax.optimization_barrier(jnp.mean(values * values, axis=-1, keepdims=True)) + EPSILON) * gain_row

def block_step(carried, blocks):
    queries, key_rows, value_rows, decays = blocks
    cumulated = jnp.cumsum(decays, axis=0)
    closing = cumulated[-1]
    causal_mask = jnp.arange(SPAN, dtype=jnp.int32)[:, None] >= jnp.arange(SPAN, dtype=jnp.int32)[None, :]
    differences = cumulated[:, None] - cumulated[None, :]
    differences = jnp.where(causal_mask[:, :, None, None], differences, jnp.zeros_like(differences))
    weights = jnp.exp(differences)
    scores = jnp.einsum('thc,shc,tshc->hts', queries, key_rows, weights, precision=PRECISE)
    scores = jnp.where(causal_mask[None], scores, jnp.zeros_like(scores))
    query_scaled = queries * jnp.exp(cumulated)
    key_tail = key_rows * jnp.exp(closing[None] - cumulated)
    mixed_rows = jnp.einsum('hts,she->the', scores, value_rows, precision=PRECISE)
    mixed_rows = mixed_rows + jnp.einsum('thc,hce->the', query_scaled, carried, precision=PRECISE)
    carried = jnp.exp(closing)[:, :, None] * carried + jnp.einsum('shc,she->hce', key_tail, value_rows, precision=PRECISE)
    return (carried, mixed_rows)

def sequence_mixing(queries, key_rows, value_rows, decays):
    blocks = LENGTH // SPAN
    shaped = (queries.reshape(blocks, SPAN, HEADS, DK), key_rows.reshape(blocks, SPAN, HEADS, DK), value_rows.reshape(blocks, SPAN, HEADS, DV), decays.reshape(blocks, SPAN, HEADS, DK))
    initial = jnp.zeros((HEADS, DK, DV), dtype=queries.dtype)
    final_state, outputs = lax.scan(jax.checkpoint(block_step), initial, shaped)
    return outputs.reshape(LENGTH, HEADS, DV)

def block_forward(params, inputs):
    attn_gain, w_query, w_key, w_value, w_outgate, w_rank_in, w_rank_out, fgate_bias, head_gain, w_output, ffn_gain, w_gate, w_up, w_down = params
    normed = low(root_norm(inputs, attn_gain))
    queries = low_back(low(matmul_high(normed, w_query)))
    key_rows = low_back(low(matmul_high(normed, w_key)))
    value_rows = low_back(low(matmul_high(normed, w_value)))
    out_gate = low_back(matmul_high(normed, w_outgate))
    rank_rows = low_back(low(matmul_high(normed, w_rank_in)))
    logits = low_back(matmul_high(rank_rows, w_rank_out.T) + fgate_bias)
    decays = jax.nn.log_sigmoid(logits) / GATE_NORM
    mixed_rows = sequence_mixing(queries, key_rows, value_rows, decays)
    heads_normed = root_norm(mixed_rows, head_gain)
    gated = low((heads_normed * jax.nn.silu(out_gate.reshape(LENGTH, HEADS, DV))).reshape(LENGTH, VD))
    residual = inputs + low_back(matmul_high(gated, w_output))
    normed_ffn = low(root_norm(residual, ffn_gain))
    gate_rows = low_back(matmul_high(normed_ffn, w_gate))
    up_rows = low_back(matmul_high(normed_ffn, w_up))
    hidden = low(jax.nn.silu(gate_rows) * up_rows)
    return residual + matmul_high(hidden, w_down)

def reference(tokens, attn_gain, w_query, w_key, w_value, w_outgate, w_rank_in, w_rank_out, fgate_bias, head_gain, w_output, ffn_gain, w_gate, w_up, w_down, out_grad):
    raw_params = (attn_gain, w_query, w_key, w_value, w_outgate, w_rank_in, w_rank_out, fgate_bias, head_gain, w_output, ffn_gain, w_gate, w_up, w_down)
    params = tuple((weight_array.astype(jnp.float32) for weight_array in raw_params))

    def accumulate(totals, sequence):
        sequence_tokens, sequence_grad = sequence
        result_rows, pullback = jax.vjp(block_forward, params, sequence_tokens.astype(jnp.float32))
        param_grads, input_grad = pullback(sequence_grad.astype(jnp.float32))
        totals = jax.tree.map(jnp.add, totals, param_grads)
        return (totals, (result_rows.astype(jnp.bfloat16), input_grad.astype(jnp.bfloat16)))
    zeros_tree = tuple((jnp.zeros(weight_array.shape, dtype=jnp.float32) for weight_array in params))
    totals, (outputs, input_grads) = lax.scan(accumulate, zeros_tree, (tokens, out_grad))
    return (outputs, input_grads, totals[0], totals[1], totals[2], totals[3], totals[4], totals[5], totals[6], totals[7], totals[8], totals[9], totals[10], totals[11], totals[12], totals[13])
```

```python
import jax
import jax.numpy as jnp
from jax import lax
import numpy as np
from jax.experimental import pallas as pl
from jax.experimental.pallas import tpu as pltpu
from jax.sharding import Mesh
from jax.sharding import PartitionSpec as P

HEADS = 4
KD = 512
VD = 1024
SPAN = 64
DK = 128
DV = 256


PRECISE = lax.Precision.HIGHEST
EPSILON = 1e-06
GATE_NORM = 16.0


def entering(part, axis, combine, identity, reverse):
    count = lax.axis_size(axis)
    place = lax.axis_index(axis)
    ahead = count - 1 - place if reverse else place
    gathered = jax.tree.map(lambda a: lax.all_gather(a, axis), part)
    state = jax.tree.map(lambda a, e: jnp.zeros_like(a) + jnp.asarray(e, a.dtype), part, identity)

    def one(hop, state):
        source = count - 1 - hop if reverse else hop
        return combine(
            state, jax.tree.map(lambda a: lax.dynamic_index_in_dim(a, source, 0, False), gathered)
        )

    return lax.fori_loop(0, ahead, one, state)


def product(left_side, right_side):
    return jnp.dot(left_side, right_side, preferred_element_type=jnp.float32)


def times_transpose(left_side, right_side):
    return lax.dot_general(
        left_side, right_side, (((1,), (1,)), ((), ())), preferred_element_type=jnp.float32
    )


def outer_sum(left_side, right_side):
    return lax.dot_general(
        left_side, right_side, (((0,), (0,)), ((), ())), preferred_element_type=jnp.float32
    )


def root_norm(values, gain_row):
    return (
        values * lax.rsqrt(jnp.mean(values * values, axis=-1, keepdims=True) + EPSILON) * gain_row
    )


def gated_heads(mixed_rows, gain_row, out_gate):
    heads_normed = root_norm(mixed_rows, gain_row)
    return (heads_normed * jax.nn.silu(out_gate.reshape(mixed_rows.shape))).reshape(out_gate.shape)


def silu_product(gate_rows, up_rows):
    return jax.nn.silu(gate_rows) * up_rows


def forget_log(logits):
    return jax.nn.log_sigmoid(logits) / GATE_NORM


def chain_link(earlier, later):
    return (earlier[0] * later[0], later[0][..., None] * earlier[1] + later[1])


def local_mixing(queries, key_rows, value_rows, decays, start_state):
    cumulated = jnp.cumsum(decays, axis=2)
    closing = cumulated[:, :, -1]
    causal_mask = jnp.arange(SPAN)[:, None] >= jnp.arange(SPAN)[None, :]
    differences = cumulated[:, :, :, None] - cumulated[:, :, None, :]
    differences = jnp.where(causal_mask[:, :, None, None], differences, 0.0)
    weights = jnp.exp(differences)
    scores = jnp.einsum("bntha,bnsha,bntsha->bnhts", queries, key_rows, weights, precision=PRECISE)
    scores = jnp.where(causal_mask, scores, 0.0)
    query_scaled = queries * jnp.exp(cumulated)
    key_tail = key_rows * jnp.exp(closing[:, :, None] - cumulated)
    inner = jnp.einsum("bnhts,bnshe->bnthe", scores, value_rows, precision=PRECISE)
    pieces = jnp.einsum("bnsha,bnshe->nbhae", key_tail, value_rows, precision=PRECISE)
    rates = jnp.exp(jnp.moveaxis(closing, 1, 0))

    def advance(carried, item):
        piece, rate = item
        return (rate[..., None] * carried + piece, carried)

    final_state, starts = lax.scan(advance, start_state, (pieces, rates))
    carried_part = jnp.einsum("bntha,nbhae->bnthe", query_scaled, starts, precision=PRECISE)
    return (inner + carried_part, final_state)


def wide_body(
    tokens,
    attn_gain,
    w_query,
    w_key,
    w_value,
    w_outgate,
    w_rank_in,
    w_rank_out,
    fgate_bias,
    head_gain,
    w_output,
    ffn_gain,
    w_gate,
    w_up,
    w_down,
    out_grad,
):
    seqs, tok_dev, width = tokens.shape
    blocks = tok_dev // SPAN
    count = seqs * tok_dev
    gathered = (
        lax.all_gather(w_query, "shard", axis=0, tiled=True),
        lax.all_gather(w_key, "shard", axis=0, tiled=True),
        lax.all_gather(w_value, "shard", axis=0, tiled=True),
        lax.all_gather(w_outgate, "shard", axis=0, tiled=True),
        lax.all_gather(w_rank_in, "shard", axis=0, tiled=True),
        lax.all_gather(w_rank_out, "shard", axis=0, tiled=True),
        lax.all_gather(w_output, "shard", axis=0, tiled=True),
        lax.all_gather(w_gate, "shard", axis=0, tiled=True),
        lax.all_gather(w_up, "shard", axis=0, tiled=True),
        lax.all_gather(w_down, "shard", axis=0, tiled=True),
    )
    (
        query_full,
        key_full,
        value_full,
        outgate_full,
        rank_in_full,
        rank_out_full,
        output_full,
        gate_full,
        up_full,
        down_full,
    ) = gathered
    inputs = tokens.reshape(count, width).astype(jnp.float32)
    normed, norm_back = jax.vjp(root_norm, inputs, attn_gain.astype(jnp.float32))
    normed_low = normed.astype(jnp.bfloat16)
    queries = product(normed_low, query_full).astype(jnp.bfloat16)
    key_rows = product(normed_low, key_full).astype(jnp.bfloat16)
    value_rows = product(normed_low, value_full).astype(jnp.bfloat16)
    out_gate = product(normed_low, outgate_full)
    rank_rows = product(normed_low, rank_in_full).astype(jnp.bfloat16)
    logits = times_transpose(rank_rows, rank_out_full) + fgate_bias.astype(jnp.float32)
    decays, gate_back = jax.vjp(forget_log, logits)
    shape_key = (seqs, blocks, SPAN, HEADS, DK)
    shape_value = (seqs, blocks, SPAN, HEADS, DV)
    query_blocks = queries.astype(jnp.float32).reshape(shape_key)
    key_blocks = key_rows.astype(jnp.float32).reshape(shape_key)
    value_blocks = value_rows.astype(jnp.float32).reshape(shape_value)
    decay_blocks = decays.reshape(shape_key)
    cumulated = jnp.cumsum(decay_blocks, axis=2)
    block_total = cumulated[:, :, -1]
    running = jnp.cumsum(block_total, axis=1)
    preceding = running - block_total
    device_total = running[:, -1]
    tail_keys = key_blocks * jnp.exp(
        device_total[:, None, None] - preceding[:, :, None] - cumulated
    )
    local_end = jnp.einsum("bntha,bnthe->bhae", tail_keys, value_blocks, precision=PRECISE)
    total_rate = jnp.exp(device_total)
    unit_rate = jnp.ones_like(total_rate)
    scanned = entering(
        (total_rate, local_end), "shard", chain_link, (unit_rate, jnp.zeros_like(local_end)), False
    )
    (mixed, final_state), mix_back = jax.vjp(
        local_mixing, query_blocks, key_blocks, value_blocks, decay_blocks, scanned[1]
    )
    mixed_rows = mixed.reshape(count, HEADS, DV)
    gated, gated_back = jax.vjp(gated_heads, mixed_rows, head_gain.astype(jnp.float32), out_gate)
    gated_low = gated.astype(jnp.bfloat16)
    residual = inputs + product(gated_low, output_full)
    normed_ffn, ffn_norm_back = jax.vjp(root_norm, residual, ffn_gain.astype(jnp.float32))
    ffn_input = normed_ffn.astype(jnp.bfloat16)
    gate_rows = product(ffn_input, gate_full)
    up_rows = product(ffn_input, up_full)
    hidden, act_back = jax.vjp(silu_product, gate_rows, up_rows)
    hidden_low = hidden.astype(jnp.bfloat16)
    block_out = (residual + product(hidden_low, down_full)).astype(jnp.bfloat16)
    grad_rows = out_grad.reshape(count, width)
    down_grad = outer_sum(hidden_low, grad_rows)
    hidden_grad = times_transpose(grad_rows, down_full)
    gate_grad, up_grad = act_back(hidden_grad)
    gate_grad_low = gate_grad.astype(jnp.bfloat16)
    up_grad_low = up_grad.astype(jnp.bfloat16)
    gate_w_grad = outer_sum(ffn_input, gate_grad_low)
    up_w_grad = outer_sum(ffn_input, up_grad_low)
    ffn_input_grad = times_transpose(gate_grad_low, gate_full) + times_transpose(
        up_grad_low, up_full
    )
    residual_part, ffn_gain_grad = ffn_norm_back(ffn_input_grad)
    residual_grad = grad_rows.astype(jnp.float32) + residual_part
    branch_grad = residual_grad.astype(jnp.bfloat16)
    output_w_grad = outer_sum(gated_low, branch_grad)
    gated_grad = times_transpose(branch_grad, output_full)
    mixed_grad, head_gain_grad, out_gate_grad = gated_back(gated_grad)
    mixed_grad_blocks = mixed_grad.reshape(shape_value)
    early_queries = query_blocks * jnp.exp(preceding[:, :, None] + cumulated)
    back_part = jnp.einsum("bntha,bnthe->bhae", early_queries, mixed_grad_blocks, precision=PRECISE)
    rescanned = entering(
        (total_rate, back_part), "shard", chain_link, (unit_rate, jnp.zeros_like(back_part)), True
    )
    pulled = mix_back((mixed_grad_blocks, rescanned[1]))
    query_grad_low = pulled[0].reshape(count, KD).astype(jnp.bfloat16)
    key_grad_low = pulled[1].reshape(count, KD).astype(jnp.bfloat16)
    value_grad_low = pulled[2].reshape(count, VD).astype(jnp.bfloat16)
    logit_grad = gate_back(pulled[3].reshape(count, KD))[0]
    logit_grad_low = logit_grad.astype(jnp.bfloat16)
    out_gate_low = out_gate_grad.astype(jnp.bfloat16)
    bias_grad = jnp.sum(logit_grad_low.astype(jnp.float32), axis=0)
    rank_out_grad = outer_sum(logit_grad_low, rank_rows)
    rank_grad_low = product(logit_grad_low, rank_out_full).astype(jnp.bfloat16)
    rank_in_grad = outer_sum(normed_low, rank_grad_low)
    query_w_grad = outer_sum(normed_low, query_grad_low)
    key_w_grad = outer_sum(normed_low, key_grad_low)
    value_w_grad = outer_sum(normed_low, value_grad_low)
    outgate_w_grad = outer_sum(normed_low, out_gate_low)
    normed_grad = (
        times_transpose(query_grad_low, query_full)
        + times_transpose(key_grad_low, key_full)
        + times_transpose(value_grad_low, value_full)
        + times_transpose(out_gate_low, outgate_full)
        + times_transpose(rank_grad_low, rank_in_full)
    )
    input_part, attn_gain_grad = norm_back(normed_grad)
    tokens_grad = (residual_grad + input_part).astype(jnp.bfloat16).reshape(tokens.shape)
    matrices = (
        query_w_grad,
        key_w_grad,
        value_w_grad,
        outgate_w_grad,
        rank_in_grad,
        rank_out_grad,
        output_w_grad,
        gate_w_grad,
        up_w_grad,
        down_grad,
    )
    owned = (
        lax.psum_scatter(matrices[0], "shard", scatter_dimension=0, tiled=True),
        lax.psum_scatter(matrices[1], "shard", scatter_dimension=0, tiled=True),
        lax.psum_scatter(matrices[2], "shard", scatter_dimension=0, tiled=True),
        lax.psum_scatter(matrices[3], "shard", scatter_dimension=0, tiled=True),
        lax.psum_scatter(matrices[4], "shard", scatter_dimension=0, tiled=True),
        lax.psum_scatter(matrices[5], "shard", scatter_dimension=0, tiled=True),
        lax.psum_scatter(matrices[6], "shard", scatter_dimension=0, tiled=True),
        lax.psum_scatter(matrices[7], "shard", scatter_dimension=0, tiled=True),
        lax.psum_scatter(matrices[8], "shard", scatter_dimension=0, tiled=True),
        lax.psum_scatter(matrices[9], "shard", scatter_dimension=0, tiled=True),
    )
    owned = lax.psum(
        (
            owned[0],
            owned[1],
            owned[2],
            owned[3],
            owned[4],
            owned[5],
            owned[6],
            owned[7],
            owned[8],
            owned[9],
        ),
        "rep",
    )
    small = lax.psum((attn_gain_grad, bias_grad, head_gain_grad, ffn_gain_grad), ("shard", "rep"))
    return (
        block_out.reshape(tokens.shape),
        tokens_grad,
        small[0],
        owned[0],
        owned[1],
        owned[2],
        owned[3],
        owned[4],
        owned[5],
        small[1],
        small[2],
        owned[6],
        small[3],
        owned[7],
        owned[8],
        owned[9],
    )


CHUNK = 128
LEVELS = (64, 32, 16, 8, 4, 2, 1)
PAIR = 2
AXES = ("shard", "x", "core")
BF16 = jnp.bfloat16
F32 = jnp.float32


def level_tables():
    rows = np.arange(CHUNK)
    t, u = rows[:, None], rows[None, :]
    sums = [(u <= t), (u > t)]
    masks = [(t == u)]
    for size in LEVELS:
        same = (t // (2 * size)) == (u // (2 * size))
        late_t = (t % (2 * size)) >= size
        late_u = (u % (2 * size)) >= size
        sums.append(
            same & ((late_t & late_u & (u <= t)) | (~late_t & ~late_u & (u > t)))
        )
        masks.append(same & late_t & ~late_u)
    sums = np.concatenate(sums, 0).astype(np.float32)
    masks = np.stack(masks, 0).astype(np.float32)
    upper = (u >= t).astype(np.float32)
    return (
        np.concatenate([sums, sums], 1),
        masks,
        np.concatenate([upper, upper], 1),
    )


def dot_nn(a, b):
    return lax.dot_general(a, b, (((1,), (0,)), ((), ())), preferred_element_type=F32)


def dot_nt(a, b):
    return lax.dot_general(a, b, (((1,), (1,)), ((), ())), preferred_element_type=F32)


def dot_tn(a, b):
    return lax.dot_general(a, b, (((0,), (0,)), ((), ())), preferred_element_type=F32)


def split(a):
    high = a.astype(BF16)
    return high, (a - high.astype(F32)).astype(BF16)


def fine(dot, a, b):
    ah, al = split(a)
    bh, bl = split(b)
    return dot(ah, bh) + (dot(ah, bl) + dot(al, bh))


def half_fine(dot, a, b):
    ah, al = split(a)
    return dot(ah, b) + dot(al, b)


def summed(table, values):
    high = values.astype(BF16)
    rest = (values - high.astype(F32)).astype(BF16)
    return dot_nn(table, jnp.concatenate([high, rest], 0))


def log_decay(logits):
    return (jnp.minimum(logits, 0.0) - jnp.log(1.0 + jnp.exp(-jnp.abs(logits)))) / GATE_NORM


def sigmoid(z):
    return 1.0 / (1.0 + jnp.exp(-z))


def mix_forward_kernel(
    order, q_ref, k_ref, v_ref, lg_ref, og_ref, gain_ref, sums_ref, mask_ref,
    gated_ref, mixed_ref, states_ref, state
):
    @pl.when(pl.program_id(0) == 0)
    def _():
        state[...] = jnp.zeros_like(state)

    factors = jnp.exp(summed(sums_ref[...], log_decay(lg_ref[...])))
    for head in range(PAIR):
        kc = slice(head * DK, (head + 1) * DK)
        vc = slice(head * DV, (head + 1) * DV)
        q_low, k_low, v_low = q_ref[:, kc], k_ref[:, kc], v_ref[:, vc]
        q, k = q_low.astype(F32), k_low.astype(F32)
        scores = mask_ref[0] * dot_nt(q_low, k_low)
        for level in range(len(LEVELS)):
            e = factors[(level + 2) * CHUNK : (level + 3) * CHUNK, kc]
            scores += mask_ref[level + 1] * fine(dot_nt, q * e, k * e)
        before = factors[:CHUNK, kc]
        after = factors[CHUNK : 2 * CHUNK, kc]
        carried = state[head]
        states_ref[0, head] = carried
        mixed = half_fine(dot_nn, scores, v_low) + fine(dot_nt, q * before, carried)
        k_high, k_rest = split(k * after)
        state[head] = carried * before[CHUNK - 1 :] + (
            dot_tn(v_low, k_high) + dot_tn(v_low, k_rest)
        )
        mixed_ref[:, vc] = mixed
        normed = mixed * lax.rsqrt(jnp.mean(mixed * mixed, axis=1, keepdims=True) + EPSILON)
        og = og_ref[:, vc]
        gated_ref[:, vc] = (normed * gain_ref[...] * (og * sigmoid(og))).astype(BF16)


def mix_backward_kernel(
    order, q_ref, k_ref, v_ref, lg_ref, og_ref, mixed_ref, dg_ref, states_ref, gain_ref,
    sums_ref, mask_ref, upper_ref,
    dall_ref, dlog_ref, hgain_ref, bias_ref, dstate, carry
):
    @pl.when(pl.program_id(0) == 0)
    def _():
        dstate[...] = jnp.zeros_like(dstate)
        carry[...] = jnp.zeros_like(carry)
        hgain_ref[...] = jnp.zeros_like(hgain_ref)
        bias_ref[...] = jnp.zeros_like(bias_ref)

    logits = lg_ref[...]
    factors = jnp.exp(summed(sums_ref[...], log_decay(logits)))
    gain = gain_ref[...]
    flows = []
    for head in range(PAIR):
        kc = slice(head * DK, (head + 1) * DK)
        vc = slice(head * DV, (head + 1) * DV)
        og, m, dg = og_ref[:, vc], mixed_ref[:, vc], dg_ref[:, vc]
        sig = sigmoid(og)
        r = lax.rsqrt(jnp.mean(m * m, axis=1, keepdims=True) + EPSILON)
        n = m * r
        dn = dg * (og * sig)
        hgain_ref[...] += jnp.sum(dn * n, axis=0, keepdims=True)
        u = gain * dn
        dm = r * (u - n * jnp.mean(u * n, axis=1, keepdims=True))
        dog = dg * (n * gain) * (sig * (1.0 + og * (1.0 - sig)))
        dall_ref[:, 2 * PAIR * DK + PAIR * DV + head * DV : 2 * PAIR * DK + PAIR * DV + (head + 1) * DV] = dog.astype(BF16)
        dm_low = dm.astype(BF16)
        q_low, k_low, v_low = q_ref[:, kc], k_ref[:, kc], v_ref[:, vc]
        q, k = q_low.astype(F32), k_low.astype(F32)
        dm_rest = (dm - dm_low.astype(F32)).astype(BF16)
        da = dot_nt(dm_low, v_low) + dot_nt(dm_rest, v_low)
        before = factors[:CHUNK, kc]
        after = factors[CHUNK : 2 * CHUNK, kc]
        carried = states_ref[0, head]
        ds = dstate[head]
        ds_low = ds.astype(BF16)
        q_in = (q * before).astype(BF16)
        k_out = (k * after).astype(BF16)
        scores = mask_ref[0] * dot_nt(q_low, k_low)
        part = (mask_ref[0] * da).astype(BF16)
        dq = dot_nn(part, k_low) + before * dot_nn(dm_low, carried.astype(BF16))
        dk = dot_tn(part, q_low) + after * dot_nn(v_low, ds_low)
        for level in range(len(LEVELS)):
            e = factors[(level + 2) * CHUNK : (level + 3) * CHUNK, kc]
            q_e, k_e = (q * e).astype(BF16), (k * e).astype(BF16)
            scores += mask_ref[level + 1] * dot_nt(q_e, k_e)
            part = (mask_ref[level + 1] * da).astype(BF16)
            dq += e * dot_nn(part, k_e)
            dk += e * dot_tn(part, q_e)
        dv = dot_tn(scores.astype(BF16), dm_low) + dot_nt(k_out, ds_low)
        dall_ref[:, kc] = dq.astype(BF16)
        dall_ref[:, PAIR * DK + head * DK : PAIR * DK + (head + 1) * DK] = dk.astype(BF16)
        dall_ref[:, 2 * PAIR * DK + head * DV : 2 * PAIR * DK + (head + 1) * DV] = dv.astype(BF16)
        ds = ds * before[CHUNK - 1 :] + dot_tn(dm_low, q_in)
        dstate[head] = ds
        flows.append(q * dq - k * dk)
        carried_flow = jnp.sum(carried * ds, axis=0, keepdims=True)
        flows.append(carried_flow)
    flow = jnp.concatenate([flows[0], flows[2]], 1)
    d_decay = summed(upper_ref[...], flow) + carry[...]
    carry[...] = jnp.concatenate([flows[1], flows[3]], 1)
    dlog = (d_decay * (sigmoid(-logits) * (1.0 / GATE_NORM))).astype(BF16)
    dlog_ref[...] = dlog
    bias_ref[...] += jnp.sum(dlog.astype(F32), axis=0, keepdims=True)


def mix_forward(order, q, k, v, logits, og, gain, sums, masks):
    rows = q.shape[0]
    steps = rows // CHUNK
    ck, cv = PAIR * DK, PAIR * DV

    def row_block(width):
        return pl.BlockSpec((CHUNK, width), lambda g, o: (o[g], 0))

    def whole(a):
        return pl.BlockSpec(a.shape, lambda g, o: (0,) * a.ndim)

    return pl.pallas_call(
        mix_forward_kernel,
        grid_spec=pltpu.PrefetchScalarGridSpec(
            num_scalar_prefetch=1,
            grid=(steps,),
            in_specs=[row_block(ck), row_block(ck), row_block(cv), row_block(ck), row_block(cv),
                      whole(gain), whole(sums), whole(masks)],
            out_specs=[row_block(cv), row_block(cv),
                       pl.BlockSpec((1, PAIR, DV, DK), lambda g, o: (g, 0, 0, 0))],
            scratch_shapes=[pltpu.VMEM((PAIR, DV, DK), F32)],
        ),
        out_shape=[jax.ShapeDtypeStruct((rows, cv), BF16), jax.ShapeDtypeStruct((rows, cv), F32),
                   jax.ShapeDtypeStruct((steps, PAIR, DV, DK), F32)],
        compiler_params=pltpu.CompilerParams(vmem_limit_bytes=40 * 1024 * 1024),
        name="mix_forward",
    )(order, q, k, v, logits, og, gain, sums, masks)


def mix_backward(order, q, k, v, logits, og, mixed, d_gated, states, gain, sums, masks, upper):
    rows = q.shape[0]
    steps = rows // CHUNK
    ck, cv = PAIR * DK, PAIR * DV

    def row_block(width):
        return pl.BlockSpec((CHUNK, width), lambda g, o: (o[steps - 1 - g], 0))

    def whole(a):
        return pl.BlockSpec(a.shape, lambda g, o: (0,) * a.ndim)

    return pl.pallas_call(
        mix_backward_kernel,
        grid_spec=pltpu.PrefetchScalarGridSpec(
            num_scalar_prefetch=1,
            grid=(steps,),
            in_specs=[row_block(ck), row_block(ck), row_block(cv), row_block(ck), row_block(cv),
                      row_block(cv), row_block(cv),
                      pl.BlockSpec((1, PAIR, DV, DK), lambda g, o: (steps - 1 - g, 0, 0, 0)),
                      whole(gain), whole(sums), whole(masks), whole(upper)],
            out_specs=[row_block(2 * ck + 2 * cv), row_block(ck),
                       pl.BlockSpec((1, DV), lambda g, o: (0, 0)),
                       pl.BlockSpec((1, ck), lambda g, o: (0, 0))],
            scratch_shapes=[pltpu.VMEM((PAIR, DV, DK), F32), pltpu.VMEM((1, ck), F32)],
        ),
        out_shape=[jax.ShapeDtypeStruct((rows, 2 * ck + 2 * cv), BF16), jax.ShapeDtypeStruct((rows, ck), BF16),
                   jax.ShapeDtypeStruct((1, DV), F32), jax.ShapeDtypeStruct((1, ck), F32)],
        compiler_params=pltpu.CompilerParams(vmem_limit_bytes=40 * 1024 * 1024),
        name="mix_backward",
    )(order, q, k, v, logits, og, mixed, d_gated, states, gain, sums, masks, upper)


def device_of(shard, x, core, xs):
    return (shard * xs + x) * 2 + core


def core_swap(a):
    return lax.ppermute(a, "core", [(0, 1), (1, 0)])


def x_swap(a):
    return lax.ppermute(a, "x", [(0, 1), (1, 0)])


def by_core(mine, other, axis):
    first = lax.axis_index("core") == 0
    return jnp.concatenate(
        [jnp.where(first, mine, other), jnp.where(first, other, mine)], axis
    )


def swap_rows(a):
    half = a.shape[0] // 2
    return jnp.concatenate([a[half:], a[:half]], 0)


def core_half(a, axis):
    half = a.shape[axis] // 2
    return lax.dynamic_slice_in_dim(a, lax.axis_index("core") * half, half, axis)


def body(
    tokens,
    attn_gain,
    w_query,
    w_key,
    w_value,
    w_outgate,
    w_rank_in,
    w_rank_out,
    fgate_bias,
    head_gain,
    w_output,
    ffn_gain,
    w_gate,
    w_up,
    w_down,
    out_grad,
):
    seqs, tok_dev, width = tokens.shape
    shards = lax.axis_size("shard")
    xs = lax.axis_size("x")
    core = lax.axis_index("core")
    place = lax.axis_index("shard")
    piece = place % seqs

    def to_chip(step):
        pairs = []
        for j in range(shards):
            for x in range(xs):
                for c in range(2):
                    target = c * seqs + (step + j % seqs) % seqs
                    pairs.append(
                        (device_of(j, x, c, xs), device_of(target, x, j // seqs, xs))
                    )
        return pairs

    def rows_in(a):
        return jnp.concatenate(
            [
                lax.ppermute(
                    lax.dynamic_index_in_dim(a, (step + piece) % seqs, 0, False),
                    AXES,
                    to_chip(step),
                )
                for step in range(seqs)
            ],
            0,
        )

    def rows_out(a):
        back = [
            lax.ppermute(
                a[step * tok_dev : (step + 1) * tok_dev],
                AXES,
                [(t, s) for s, t in to_chip(step)],
            )
            for step in range(seqs)
        ]
        twice = jnp.stack(back + back, 0)
        return lax.dynamic_slice_in_dim(twice, (seqs - piece) % seqs, seqs, 0)

    counter = jnp.arange(shards, dtype=jnp.int32)
    order = ((counter // seqs) ^ core) * seqs + (piece - counter) % seqs
    order = order.astype(jnp.int32)
    sums, masks, upper = level_tables()
    sums, masks, upper = jnp.asarray(sums, BF16), jnp.asarray(masks, F32), jnp.asarray(upper, BF16)

    rank_pack = jnp.concatenate(
        [
            w_rank_in,
            jnp.pad(w_rank_out, ((0, w_rank_in.shape[0] - w_rank_out.shape[0]), (0, 0))),
            jnp.zeros((w_rank_in.shape[0], 96), BF16),
        ],
        1,
    )
    ck, cv = PAIR * DK, PAIR * DV
    packed = jnp.concatenate(
        [core_half(w, 1) for w in (w_query, w_key, w_value, w_outgate, w_output)] + [rank_pack], 1
    )
    wide = 2 * ck + 2 * cv
    own = rows_in(tokens)
    attn_full = lax.all_gather(packed, "shard", axis=0, tiled=True)
    ffn_cols = lax.all_gather(
        jnp.concatenate([core_half(w_gate, 1), core_half(w_up, 1)], 1), "shard", axis=0, tiled=True
    )
    down_rows = lax.all_gather(core_half(w_down, 0), "shard", axis=0)
    own_grad = rows_in(out_grad)

    x_low = jnp.concatenate([own, core_swap(own)], 0)
    inputs = x_low.astype(F32)
    r_in = lax.rsqrt(jnp.mean(inputs * inputs, axis=1, keepdims=True) + EPSILON)
    attn_row = attn_gain.astype(F32)
    normed = (inputs * r_in * attn_row).astype(BF16)

    w_qkvo = attn_full[:, :wide]
    rank_in = attn_full[:, wide + cv : wide + cv + 16]
    rank_out = attn_full[:, wide + cv + 16 : wide + cv + 32]
    rank_out = rank_out.reshape(shards, -1, 16)[:, : w_rank_out.shape[0]].reshape(-1, 16)
    rank_out = core_half(rank_out, 0)
    queries = product(normed, w_qkvo[:, :ck]).astype(BF16)
    keys = product(normed, w_qkvo[:, ck : 2 * ck]).astype(BF16)
    values = product(normed, w_qkvo[:, 2 * ck : 2 * ck + cv]).astype(BF16)
    out_gate = product(normed, w_qkvo[:, 2 * ck + cv :])
    rank_rows = product(normed, rank_in).astype(BF16)
    logits = times_transpose(rank_rows, rank_out) + core_half(fgate_bias, 0).astype(F32)
    gain = head_gain.astype(F32)[None]
    gated, mixed, states = mix_forward(
        order, queries, keys, values, logits, out_gate, gain, sums, masks
    )
    gated_full = by_core(gated, swap_rows(core_swap(gated)), 1)
    out_mine = attn_full[:, wide : wide + cv]
    w_out_full = by_core(out_mine, core_swap(out_mine), 1)
    residual = inputs + product(gated_full, w_out_full)
    r_ffn = lax.rsqrt(jnp.mean(residual * residual, axis=1, keepdims=True) + EPSILON)
    ffn_row = ffn_gain.astype(F32)
    ffn_in = (residual * r_ffn * ffn_row).astype(BF16)

    ff_half = w_gate.shape[1] // 2
    group = shards // 2
    mine_down = lax.dynamic_slice_in_dim(down_rows, core * group, group, 0)
    send_down = lax.dynamic_slice_in_dim(down_rows, (1 - core) * group, group, 0)
    other_down = core_swap(send_down)
    w_down_half = by_core(mine_down, other_down, 1).reshape(ff_half, width)
    w_gate_half, w_up_half = ffn_cols[:, :ff_half], ffn_cols[:, ff_half:]

    dy = jnp.concatenate([own_grad, core_swap(own_grad)], 0)
    gate = product(ffn_in, w_gate_half)
    up = product(ffn_in, w_up_half)
    sig = sigmoid(gate)
    act = gate * sig
    hidden = (act * up).astype(BF16)
    d_hidden = times_transpose(dy, w_down_half)
    d_gate = (d_hidden * up * (sig * (1.0 + gate * (1.0 - sig)))).astype(BF16)
    d_up = (d_hidden * act).astype(BF16)
    half_rows = x_low.shape[0] // 2
    block_part = product(hidden, w_down_half)
    block_own = (
        residual[:half_rows] + block_part[:half_rows] + core_swap(block_part[half_rows:])
    ).astype(BF16)
    block_out = rows_out(block_own)

    down_grad = outer_sum(hidden, dy).astype(BF16).reshape(group, 2, -1, width)
    mine_dg = lax.dynamic_index_in_dim(down_grad, core, 1, False)
    other_dg = core_swap(lax.dynamic_index_in_dim(down_grad, 1 - core, 1, False))
    down_grad = by_core(mine_dg, other_dg, 0)
    down_own = lax.psum_scatter(
        down_grad.reshape(-1, width), "shard", scatter_dimension=0, tiled=True
    )
    gateup_grad = jnp.concatenate([outer_sum(ffn_in, d_gate), outer_sum(ffn_in, d_up)], 1)
    gateup_own = lax.psum_scatter(
        gateup_grad.astype(BF16), "shard", scatter_dimension=0, tiled=True
    )

    dn_part = times_transpose(d_gate, w_gate_half) + times_transpose(d_up, w_up_half)
    dn_ffn = dn_part + swap_rows(core_swap(dn_part))
    u = ffn_row * dn_ffn
    d_residual = dy.astype(F32) + r_ffn * (
        u - residual * (r_ffn * r_ffn) * jnp.mean(u * residual, axis=1, keepdims=True)
    )
    ffn_gain_grad = jnp.sum((dn_ffn * residual * r_ffn)[:half_rows], axis=0)
    d_branch = d_residual.astype(BF16)
    out_w_grad = outer_sum(gated_full, core_half(d_branch, 1))
    d_gated = times_transpose(d_branch, core_half(w_out_full, 0))
    d_all, d_logits, hgain_part, bias_part = mix_backward(
        order, queries, keys, values, logits, out_gate, mixed, d_gated, states, gain,
        sums, masks, upper
    )
    rank_out_grad = outer_sum(d_logits, rank_rows)
    rank_part = product(d_logits, rank_out)
    d_rank = (rank_part + swap_rows(core_swap(rank_part))).astype(BF16)
    rank_in_grad = outer_sum(normed[:half_rows], d_rank[:half_rows])
    qkvo_grad = outer_sum(normed, d_all)
    attn_own = lax.psum_scatter(
        jnp.concatenate([qkvo_grad, out_w_grad], 1).astype(BF16),
        "shard",
        scatter_dimension=0,
        tiled=True,
    )
    dn_attn = times_transpose(d_all, w_qkvo)
    dn_own = (
        dn_attn[:half_rows]
        + core_swap(dn_attn[half_rows:])
        + times_transpose(d_rank[:half_rows], rank_in)
    )
    own_in, own_r = inputs[:half_rows], r_in[:half_rows]
    u = attn_row * dn_own
    tok_grad = (
        d_residual[:half_rows]
        + own_r * (u - own_in * (own_r * own_r) * jnp.mean(u * own_in, axis=1, keepdims=True))
    ).astype(BF16)
    tokens_grad = rows_out(tok_grad)
    attn_gain_grad = jnp.sum(dn_own * own_in * own_r, axis=0)

    first = (core == 0).astype(F32)
    bias_both = jnp.concatenate([bias_part[0] * first, bias_part[0] * (1.0 - first)], 0)
    rank_out_both = jnp.concatenate([rank_out_grad * first, rank_out_grad * (1.0 - first)], 0)
    small = lax.psum(
        (attn_gain_grad, bias_both, hgain_part[0], ffn_gain_grad, rank_in_grad, rank_out_both),
        AXES,
    )
    rin_rows, rout_rows = w_rank_in.shape[0], w_rank_out.shape[0]
    rank_in_own = lax.dynamic_slice_in_dim(small[4], place * rin_rows, rin_rows, 0)
    rank_out_own = lax.dynamic_slice_in_dim(small[5], place * rout_rows, rout_rows, 0)

    def settle(a):
        total = a.astype(F32)
        if xs == 2:
            total = total + x_swap(a).astype(F32)
        return total, core_swap(total)

    attn_mine, attn_other = settle(attn_own)
    gu_mine, gu_other = settle(gateup_own)
    down_mine, down_other = settle(down_own)

    def columns(mine, other, start, size):
        return by_core(mine[:, start : start + size], other[:, start : start + size], 1)

    return (
        block_out,
        tokens_grad,
        small[0],
        columns(attn_mine, attn_other, 0, ck),
        columns(attn_mine, attn_other, ck, ck),
        columns(attn_mine, attn_other, 2 * ck, cv),
        columns(attn_mine, attn_other, 2 * ck + cv, cv),
        rank_in_own,
        rank_out_own,
        small[1],
        small[2],
        columns(attn_mine, attn_other, wide, cv),
        small[3],
        columns(gu_mine, gu_other, 0, ff_half),
        columns(gu_mine, gu_other, ff_half, ff_half),
        by_core(down_mine, down_other, 0),
    )


def solution(mesh):
    shards = mesh.shape["shard"]
    reps = mesh.shape["rep"]

    def run(*arrays):
        tokens = arrays[0]
        seqs = tokens.shape[0] // reps
        narrow = reps == 4 and shards == 2 * seqs and tokens.shape[1] // shards == CHUNK
        if narrow:
            grid = Mesh(mesh.devices.reshape(shards, reps // 2, 2), AXES)
            rep = ("x", "core")
        else:
            grid, rep = mesh, "rep"
        rows, cols = P(rep, "shard", None), P("shard", None)
        in_specs = (rows, P()) + (cols,) * 6 + (P(), P(), cols, P()) + (cols,) * 3 + (rows,)
        out_specs = (rows, rows, P()) + (cols,) * 6 + (P(), P(), cols, P()) + (cols,) * 3
        return jax.shard_map(
            body if narrow else wide_body,
            mesh=grid,
            in_specs=in_specs,
            out_specs=out_specs,
            check_vma=False,
        )(*arrays)

    return run
```

```python
import jax
import jax.numpy as jnp
from jax import lax
import numpy as np
from jax.experimental import pallas as pl
from jax.experimental.pallas import tpu as pltpu
from jax.sharding import Mesh
from jax.sharding import PartitionSpec as P

HEADS = 4
KD = 512
VD = 1024
SPAN = 64
DK = 128
DV = 256


PRECISE = lax.Precision.HIGHEST
EPSILON = 1e-06
GATE_NORM = 16.0


def entering(part, axis, combine, identity, reverse):
    count = lax.axis_size(axis)
    place = lax.axis_index(axis)
    ahead = count - 1 - place if reverse else place
    gathered = jax.tree.map(lambda a: lax.all_gather(a, axis), part)
    state = jax.tree.map(lambda a, e: jnp.zeros_like(a) + jnp.asarray(e, a.dtype), part, identity)

    def one(hop, state):
        source = count - 1 - hop if reverse else hop
        return combine(
            state, jax.tree.map(lambda a: lax.dynamic_index_in_dim(a, source, 0, False), gathered)
        )

    return lax.fori_loop(0, ahead, one, state)


def product(left_side, right_side):
    return jnp.dot(left_side, right_side, preferred_element_type=jnp.float32)


def times_transpose(left_side, right_side):
    return lax.dot_general(
        left_side, right_side, (((1,), (1,)), ((), ())), preferred_element_type=jnp.float32
    )


def outer_sum(left_side, right_side):
    return lax.dot_general(
        left_side, right_side, (((0,), (0,)), ((), ())), preferred_element_type=jnp.float32
    )


def root_norm(values, gain_row):
    return (
        values * lax.rsqrt(jnp.mean(values * values, axis=-1, keepdims=True) + EPSILON) * gain_row
    )


def gated_heads(mixed_rows, gain_row, out_gate):
    heads_normed = root_norm(mixed_rows, gain_row)
    return (heads_normed * jax.nn.silu(out_gate.reshape(mixed_rows.shape))).reshape(out_gate.shape)


def silu_product(gate_rows, up_rows):
    return jax.nn.silu(gate_rows) * up_rows


def forget_log(logits):
    return jax.nn.log_sigmoid(logits) / GATE_NORM


def chain_link(earlier, later):
    return (earlier[0] * later[0], later[0][..., None] * earlier[1] + later[1])


def local_mixing(queries, key_rows, value_rows, decays, start_state):
    cumulated = jnp.cumsum(decays, axis=2)
    closing = cumulated[:, :, -1]
    causal_mask = jnp.arange(SPAN)[:, None] >= jnp.arange(SPAN)[None, :]
    differences = cumulated[:, :, :, None] - cumulated[:, :, None, :]
    differences = jnp.where(causal_mask[:, :, None, None], differences, 0.0)
    weights = jnp.exp(differences)
    scores = jnp.einsum("bntha,bnsha,bntsha->bnhts", queries, key_rows, weights, precision=PRECISE)
    scores = jnp.where(causal_mask, scores, 0.0)
    query_scaled = queries * jnp.exp(cumulated)
    key_tail = key_rows * jnp.exp(closing[:, :, None] - cumulated)
    inner = jnp.einsum("bnhts,bnshe->bnthe", scores, value_rows, precision=PRECISE)
    pieces = jnp.einsum("bnsha,bnshe->nbhae", key_tail, value_rows, precision=PRECISE)
    rates = jnp.exp(jnp.moveaxis(closing, 1, 0))

    def advance(carried, item):
        piece, rate = item
        return (rate[..., None] * carried + piece, carried)

    final_state, starts = lax.scan(advance, start_state, (pieces, rates))
    carried_part = jnp.einsum("bntha,nbhae->bnthe", query_scaled, starts, precision=PRECISE)
    return (inner + carried_part, final_state)


def wide_body(
    tokens,
    attn_gain,
    w_query,
    w_key,
    w_value,
    w_outgate,
    w_rank_in,
    w_rank_out,
    fgate_bias,
    head_gain,
    w_output,
    ffn_gain,
    w_gate,
    w_up,
    w_down,
    out_grad,
):
    seqs, tok_dev, width = tokens.shape
    blocks = tok_dev // SPAN
    count = seqs * tok_dev
    gathered = (
        lax.all_gather(w_query, "shard", axis=0, tiled=True),
        lax.all_gather(w_key, "shard", axis=0, tiled=True),
        lax.all_gather(w_value, "shard", axis=0, tiled=True),
        lax.all_gather(w_outgate, "shard", axis=0, tiled=True),
        lax.all_gather(w_rank_in, "shard", axis=0, tiled=True),
        lax.all_gather(w_rank_out, "shard", axis=0, tiled=True),
        lax.all_gather(w_output, "shard", axis=0, tiled=True),
        lax.all_gather(w_gate, "shard", axis=0, tiled=True),
        lax.all_gather(w_up, "shard", axis=0, tiled=True),
        lax.all_gather(w_down, "shard", axis=0, tiled=True),
    )
    (
        query_full,
        key_full,
        value_full,
        outgate_full,
        rank_in_full,
        rank_out_full,
        output_full,
        gate_full,
        up_full,
        down_full,
    ) = gathered
    inputs = tokens.reshape(count, width).astype(jnp.float32)
    normed, norm_back = jax.vjp(root_norm, inputs, attn_gain.astype(jnp.float32))
    normed_low = normed.astype(jnp.bfloat16)
    queries = product(normed_low, query_full).astype(jnp.bfloat16)
    key_rows = product(normed_low, key_full).astype(jnp.bfloat16)
    value_rows = product(normed_low, value_full).astype(jnp.bfloat16)
    out_gate = product(normed_low, outgate_full)
    rank_rows = product(normed_low, rank_in_full).astype(jnp.bfloat16)
    logits = times_transpose(rank_rows, rank_out_full) + fgate_bias.astype(jnp.float32)
    decays, gate_back = jax.vjp(forget_log, logits)
    shape_key = (seqs, blocks, SPAN, HEADS, DK)
    shape_value = (seqs, blocks, SPAN, HEADS, DV)
    query_blocks = queries.astype(jnp.float32).reshape(shape_key)
    key_blocks = key_rows.astype(jnp.float32).reshape(shape_key)
    value_blocks = value_rows.astype(jnp.float32).reshape(shape_value)
    decay_blocks = decays.reshape(shape_key)
    cumulated = jnp.cumsum(decay_blocks, axis=2)
    block_total = cumulated[:, :, -1]
    running = jnp.cumsum(block_total, axis=1)
    preceding = running - block_total
    device_total = running[:, -1]
    tail_keys = key_blocks * jnp.exp(
        device_total[:, None, None] - preceding[:, :, None] - cumulated
    )
    local_end = jnp.einsum("bntha,bnthe->bhae", tail_keys, value_blocks, precision=PRECISE)
    total_rate = jnp.exp(device_total)
    unit_rate = jnp.ones_like(total_rate)
    scanned = entering(
        (total_rate, local_end), "shard", chain_link, (unit_rate, jnp.zeros_like(local_end)), False
    )
    (mixed, final_state), mix_back = jax.vjp(
        local_mixing, query_blocks, key_blocks, value_blocks, decay_blocks, scanned[1]
    )
    mixed_rows = mixed.reshape(count, HEADS, DV)
    gated, gated_back = jax.vjp(gated_heads, mixed_rows, head_gain.astype(jnp.float32), out_gate)
    gated_low = gated.astype(jnp.bfloat16)
    residual = inputs + product(gated_low, output_full)
    normed_ffn, ffn_norm_back = jax.vjp(root_norm, residual, ffn_gain.astype(jnp.float32))
    ffn_input = normed_ffn.astype(jnp.bfloat16)
    gate_rows = product(ffn_input, gate_full)
    up_rows = product(ffn_input, up_full)
    hidden, act_back = jax.vjp(silu_product, gate_rows, up_rows)
    hidden_low = hidden.astype(jnp.bfloat16)
    block_out = (residual + product(hidden_low, down_full)).astype(jnp.bfloat16)
    grad_rows = out_grad.reshape(count, width)
    down_grad = outer_sum(hidden_low, grad_rows)
    hidden_grad = times_transpose(grad_rows, down_full)
    gate_grad, up_grad = act_back(hidden_grad)
    gate_grad_low = gate_grad.astype(jnp.bfloat16)
    up_grad_low = up_grad.astype(jnp.bfloat16)
    gate_w_grad = outer_sum(ffn_input, gate_grad_low)
    up_w_grad = outer_sum(ffn_input, up_grad_low)
    ffn_input_grad = times_transpose(gate_grad_low, gate_full) + times_transpose(
        up_grad_low, up_full
    )
    residual_part, ffn_gain_grad = ffn_norm_back(ffn_input_grad)
    residual_grad = grad_rows.astype(jnp.float32) + residual_part
    branch_grad = residual_grad.astype(jnp.bfloat16)
    output_w_grad = outer_sum(gated_low, branch_grad)
    gated_grad = times_transpose(branch_grad, output_full)
    mixed_grad, head_gain_grad, out_gate_grad = gated_back(gated_grad)
    mixed_grad_blocks = mixed_grad.reshape(shape_value)
    early_queries = query_blocks * jnp.exp(preceding[:, :, None] + cumulated)
    back_part = jnp.einsum("bntha,bnthe->bhae", early_queries, mixed_grad_blocks, precision=PRECISE)
    rescanned = entering(
        (total_rate, back_part), "shard", chain_link, (unit_rate, jnp.zeros_like(back_part)), True
    )
    pulled = mix_back((mixed_grad_blocks, rescanned[1]))
    query_grad_low = pulled[0].reshape(count, KD).astype(jnp.bfloat16)
    key_grad_low = pulled[1].reshape(count, KD).astype(jnp.bfloat16)
    value_grad_low = pulled[2].reshape(count, VD).astype(jnp.bfloat16)
    logit_grad = gate_back(pulled[3].reshape(count, KD))[0]
    logit_grad_low = logit_grad.astype(jnp.bfloat16)
    out_gate_low = out_gate_grad.astype(jnp.bfloat16)
    bias_grad = jnp.sum(logit_grad_low.astype(jnp.float32), axis=0)
    rank_out_grad = outer_sum(logit_grad_low, rank_rows)
    rank_grad_low = product(logit_grad_low, rank_out_full).astype(jnp.bfloat16)
    rank_in_grad = outer_sum(normed_low, rank_grad_low)
    query_w_grad = outer_sum(normed_low, query_grad_low)
    key_w_grad = outer_sum(normed_low, key_grad_low)
    value_w_grad = outer_sum(normed_low, value_grad_low)
    outgate_w_grad = outer_sum(normed_low, out_gate_low)
    normed_grad = (
        times_transpose(query_grad_low, query_full)
        + times_transpose(key_grad_low, key_full)
        + times_transpose(value_grad_low, value_full)
        + times_transpose(out_gate_low, outgate_full)
        + times_transpose(rank_grad_low, rank_in_full)
    )
    input_part, attn_gain_grad = norm_back(normed_grad)
    tokens_grad = (residual_grad + input_part).astype(jnp.bfloat16).reshape(tokens.shape)
    matrices = (
        query_w_grad,
        key_w_grad,
        value_w_grad,
        outgate_w_grad,
        rank_in_grad,
        rank_out_grad,
        output_w_grad,
        gate_w_grad,
        up_w_grad,
        down_grad,
    )
    owned = (
        lax.psum_scatter(matrices[0], "shard", scatter_dimension=0, tiled=True),
        lax.psum_scatter(matrices[1], "shard", scatter_dimension=0, tiled=True),
        lax.psum_scatter(matrices[2], "shard", scatter_dimension=0, tiled=True),
        lax.psum_scatter(matrices[3], "shard", scatter_dimension=0, tiled=True),
        lax.psum_scatter(matrices[4], "shard", scatter_dimension=0, tiled=True),
        lax.psum_scatter(matrices[5], "shard", scatter_dimension=0, tiled=True),
        lax.psum_scatter(matrices[6], "shard", scatter_dimension=0, tiled=True),
        lax.psum_scatter(matrices[7], "shard", scatter_dimension=0, tiled=True),
        lax.psum_scatter(matrices[8], "shard", scatter_dimension=0, tiled=True),
        lax.psum_scatter(matrices[9], "shard", scatter_dimension=0, tiled=True),
    )
    owned = lax.psum(
        (
            owned[0],
            owned[1],
            owned[2],
            owned[3],
            owned[4],
            owned[5],
            owned[6],
            owned[7],
            owned[8],
            owned[9],
        ),
        "rep",
    )
    small = lax.psum((attn_gain_grad, bias_grad, head_gain_grad, ffn_gain_grad), ("shard", "rep"))
    return (
        block_out.reshape(tokens.shape),
        tokens_grad,
        small[0],
        owned[0],
        owned[1],
        owned[2],
        owned[3],
        owned[4],
        owned[5],
        small[1],
        small[2],
        owned[6],
        small[3],
        owned[7],
        owned[8],
        owned[9],
    )


CHUNK = 128
LEVELS = (64, 32, 16, 8, 4, 2, 1)
PAIR = 2
AXES = ("shard", "x", "core")
BF16 = jnp.bfloat16
F32 = jnp.float32


def level_tables():
    rows = np.arange(CHUNK)
    t, u = rows[:, None], rows[None, :]
    sums = [(u <= t), (u > t)]
    masks = [(t == u)]
    for size in LEVELS:
        same = (t // (2 * size)) == (u // (2 * size))
        late_t = (t % (2 * size)) >= size
        late_u = (u % (2 * size)) >= size
        sums.append(
            same & ((late_t & late_u & (u <= t)) | (~late_t & ~late_u & (u > t)))
        )
        masks.append(same & late_t & ~late_u)
    sums = np.concatenate(sums, 0).astype(np.float32)
    masks = np.stack(masks, 0).astype(np.float32)
    upper = (u >= t).astype(np.float32)
    return (
        np.concatenate([sums, sums], 1),
        masks,
        np.concatenate([upper, upper], 1),
    )


def dot_nn(a, b):
    return lax.dot_general(a, b, (((1,), (0,)), ((), ())), preferred_element_type=F32)


def dot_nt(a, b):
    return lax.dot_general(a, b, (((1,), (1,)), ((), ())), preferred_element_type=F32)


def dot_tn(a, b):
    return lax.dot_general(a, b, (((0,), (0,)), ((), ())), preferred_element_type=F32)


def split(a):
    high = a.astype(BF16)
    return high, (a - high.astype(F32)).astype(BF16)


def fine(dot, a, b):
    ah, al = split(a)
    bh, bl = split(b)
    return dot(ah, bh) + (dot(ah, bl) + dot(al, bh))


def half_fine(dot, a, b):
    ah, al = split(a)
    return dot(ah, b) + dot(al, b)


def summed(table, values):
    high = values.astype(BF16)
    rest = (values - high.astype(F32)).astype(BF16)
    return dot_nn(table, jnp.concatenate([high, rest], 0))


def log_decay(logits):
    return (jnp.minimum(logits, 0.0) - jnp.log(1.0 + jnp.exp(-jnp.abs(logits)))) / GATE_NORM


def sigmoid(z):
    return 1.0 / (1.0 + jnp.exp(-z))


def mix_forward_kernel(
    order, q_ref, k_ref, v_ref, lg_ref, og_ref, gain_ref, sums_ref, mask_ref,
    gated_ref, mixed_ref, states_ref, state
):
    @pl.when(pl.program_id(0) == 0)
    def _():
        state[...] = jnp.zeros_like(state)

    factors = jnp.exp(summed(sums_ref[...], log_decay(lg_ref[...])))
    for head in range(PAIR):
        kc = slice(head * DK, (head + 1) * DK)
        vc = slice(head * DV, (head + 1) * DV)
        q_low, k_low, v_low = q_ref[:, kc], k_ref[:, kc], v_ref[:, vc]
        q, k = q_low.astype(F32), k_low.astype(F32)
        scores = mask_ref[0] * dot_nt(q_low, k_low)
        for level in range(len(LEVELS)):
            e = factors[(level + 2) * CHUNK : (level + 3) * CHUNK, kc]
            scores += mask_ref[level + 1] * fine(dot_nt, q * e, k * e)
        before = factors[:CHUNK, kc]
        after = factors[CHUNK : 2 * CHUNK, kc]
        carried = state[head]
        states_ref[0, head] = carried
        mixed = half_fine(dot_nn, scores, v_low) + fine(dot_nt, q * before, carried)
        k_high, k_rest = split(k * after)
        state[head] = carried * before[CHUNK - 1 :] + (
            dot_tn(v_low, k_high) + dot_tn(v_low, k_rest)
        )
        mixed_ref[:, vc] = mixed
        normed = mixed * lax.rsqrt(jnp.mean(mixed * mixed, axis=1, keepdims=True) + EPSILON)
        og = og_ref[:, vc]
        gated_ref[:, vc] = (normed * gain_ref[...] * (og * sigmoid(og))).astype(BF16)


def mix_backward_kernel(
    order, q_ref, k_ref, v_ref, lg_ref, og_ref, mixed_ref, dg_ref, states_ref, gain_ref,
    sums_ref, mask_ref, upper_ref,
    dall_ref, dlog_ref, hgain_ref, bias_ref, dstate, carry
):
    @pl.when(pl.program_id(0) == 0)
    def _():
        dstate[...] = jnp.zeros_like(dstate)
        carry[...] = jnp.zeros_like(carry)
        hgain_ref[...] = jnp.zeros_like(hgain_ref)
        bias_ref[...] = jnp.zeros_like(bias_ref)

    logits = lg_ref[...]
    factors = jnp.exp(summed(sums_ref[...], log_decay(logits)))
    gain = gain_ref[...]
    flows = []
    for head in range(PAIR):
        kc = slice(head * DK, (head + 1) * DK)
        vc = slice(head * DV, (head + 1) * DV)
        og, m, dg = og_ref[:, vc], mixed_ref[:, vc], dg_ref[:, vc]
        sig = sigmoid(og)
        r = lax.rsqrt(jnp.mean(m * m, axis=1, keepdims=True) + EPSILON)
        n = m * r
        dn = dg * (og * sig)
        hgain_ref[...] += jnp.sum(dn * n, axis=0, keepdims=True)
        u = gain * dn
        dm = r * (u - n * jnp.mean(u * n, axis=1, keepdims=True))
        dog = dg * (n * gain) * (sig * (1.0 + og * (1.0 - sig)))
        dall_ref[:, 2 * PAIR * DK + PAIR * DV + head * DV : 2 * PAIR * DK + PAIR * DV + (head + 1) * DV] = dog.astype(BF16)
        dm_low = dm.astype(BF16)
        q_low, k_low, v_low = q_ref[:, kc], k_ref[:, kc], v_ref[:, vc]
        q, k = q_low.astype(F32), k_low.astype(F32)
        dm_rest = (dm - dm_low.astype(F32)).astype(BF16)
        da = dot_nt(dm_low, v_low) + dot_nt(dm_rest, v_low)
        before = factors[:CHUNK, kc]
        after = factors[CHUNK : 2 * CHUNK, kc]
        carried = states_ref[0, head]
        ds = dstate[head]
        ds_low = ds.astype(BF16)
        q_in = (q * before).astype(BF16)
        k_out = (k * after).astype(BF16)
        scores = mask_ref[0] * dot_nt(q_low, k_low)
        part = (mask_ref[0] * da).astype(BF16)
        dq = dot_nn(part, k_low) + before * dot_nn(dm_low, carried.astype(BF16))
        dk = dot_tn(part, q_low) + after * dot_nn(v_low, ds_low)
        for level in range(len(LEVELS)):
            e = factors[(level + 2) * CHUNK : (level + 3) * CHUNK, kc]
            q_e, k_e = (q * e).astype(BF16), (k * e).astype(BF16)
            scores += mask_ref[level + 1] * dot_nt(q_e, k_e)
            part = (mask_ref[level + 1] * da).astype(BF16)
            dq += e * dot_nn(part, k_e)
            dk += e * dot_tn(part, q_e)
        dv = dot_tn(scores.astype(BF16), dm_low) + dot_nt(k_out, ds_low)
        dall_ref[:, kc] = dq.astype(BF16)
        dall_ref[:, PAIR * DK + head * DK : PAIR * DK + (head + 1) * DK] = dk.astype(BF16)
        dall_ref[:, 2 * PAIR * DK + head * DV : 2 * PAIR * DK + (head + 1) * DV] = dv.astype(BF16)
        ds = ds * before[CHUNK - 1 :] + dot_tn(dm_low, q_in)
        dstate[head] = ds
        flows.append(q * dq - k * dk)
        carried_flow = jnp.sum(carried * ds, axis=0, keepdims=True)
        flows.append(carried_flow)
    flow = jnp.concatenate([flows[0], flows[2]], 1)
    d_decay = summed(upper_ref[...], flow) + carry[...]
    carry[...] = jnp.concatenate([flows[1], flows[3]], 1)
    dlog = (d_decay * (sigmoid(-logits) * (1.0 / GATE_NORM))).astype(BF16)
    dlog_ref[...] = dlog
    bias_ref[...] += jnp.sum(dlog.astype(F32), axis=0, keepdims=True)


def mix_forward(order, q, k, v, logits, og, gain, sums, masks):
    rows = q.shape[0]
    steps = rows // CHUNK
    ck, cv = PAIR * DK, PAIR * DV

    def row_block(width):
        return pl.BlockSpec((CHUNK, width), lambda g, o: (o[g], 0))

    def whole(a):
        return pl.BlockSpec(a.shape, lambda g, o: (0,) * a.ndim)

    return pl.pallas_call(
        mix_forward_kernel,
        grid_spec=pltpu.PrefetchScalarGridSpec(
            num_scalar_prefetch=1,
            grid=(steps,),
            in_specs=[row_block(ck), row_block(ck), row_block(cv), row_block(ck), row_block(cv),
                      whole(gain), whole(sums), whole(masks)],
            out_specs=[row_block(cv), row_block(cv),
                       pl.BlockSpec((1, PAIR, DV, DK), lambda g, o: (g, 0, 0, 0))],
            scratch_shapes=[pltpu.VMEM((PAIR, DV, DK), F32)],
        ),
        out_shape=[jax.ShapeDtypeStruct((rows, cv), BF16), jax.ShapeDtypeStruct((rows, cv), F32),
                   jax.ShapeDtypeStruct((steps, PAIR, DV, DK), F32)],
        compiler_params=pltpu.CompilerParams(vmem_limit_bytes=40 * 1024 * 1024),
        name="mix_forward",
    )(order, q, k, v, logits, og, gain, sums, masks)


def mix_backward(order, q, k, v, logits, og, mixed, d_gated, states, gain, sums, masks, upper):
    rows = q.shape[0]
    steps = rows // CHUNK
    ck, cv = PAIR * DK, PAIR * DV

    def row_block(width):
        return pl.BlockSpec((CHUNK, width), lambda g, o: (o[steps - 1 - g], 0))

    def whole(a):
        return pl.BlockSpec(a.shape, lambda g, o: (0,) * a.ndim)

    return pl.pallas_call(
        mix_backward_kernel,
        grid_spec=pltpu.PrefetchScalarGridSpec(
            num_scalar_prefetch=1,
            grid=(steps,),
            in_specs=[row_block(ck), row_block(ck), row_block(cv), row_block(ck), row_block(cv),
                      row_block(cv), row_block(cv),
                      pl.BlockSpec((1, PAIR, DV, DK), lambda g, o: (steps - 1 - g, 0, 0, 0)),
                      whole(gain), whole(sums), whole(masks), whole(upper)],
            out_specs=[row_block(2 * ck + 2 * cv), row_block(ck),
                       pl.BlockSpec((1, DV), lambda g, o: (0, 0)),
                       pl.BlockSpec((1, ck), lambda g, o: (0, 0))],
            scratch_shapes=[pltpu.VMEM((PAIR, DV, DK), F32), pltpu.VMEM((1, ck), F32)],
        ),
        out_shape=[jax.ShapeDtypeStruct((rows, 2 * ck + 2 * cv), BF16), jax.ShapeDtypeStruct((rows, ck), BF16),
                   jax.ShapeDtypeStruct((1, DV), F32), jax.ShapeDtypeStruct((1, ck), F32)],
        compiler_params=pltpu.CompilerParams(vmem_limit_bytes=40 * 1024 * 1024),
        name="mix_backward",
    )(order, q, k, v, logits, og, mixed, d_gated, states, gain, sums, masks, upper)


def device_of(shard, x, core, xs):
    return (shard * xs + x) * 2 + core


def core_swap(a):
    return lax.ppermute(a, "core", [(0, 1), (1, 0)])


def x_swap(a):
    return lax.ppermute(a, "x", [(0, 1), (1, 0)])


def ring_order(shards):
    return list(range(0, shards, 2)) + list(range(shards - 1, 0, -2))


class Ring:
    def __init__(self):
        self.shards, self.xs = lax.axis_size("shard"), lax.axis_size("x")
        self.core = lax.axis_index("core")
        cycle = ring_order(self.shards)
        spot = [cycle.index(s) for s in range(self.shards)]
        self.cycle = jnp.asarray(cycle, jnp.int32)
        self.spot = jnp.asarray(spot, jnp.int32)[lax.axis_index("shard")]
        self.sign = 1 - 2 * self.core
        self.pairs = []
        for s in range(self.shards):
            for x in range(self.xs):
                for c in range(2):
                    step = 1 if c == 0 else -1
                    to = cycle[(spot[s] + step) % self.shards]
                    self.pairs.append(
                        (device_of(s, x, c, self.xs), device_of(to, x, c, self.xs))
                    )

    def behind(self, hops):
        return self.cycle[(self.spot - self.sign * hops) % self.shards]

    def send(self, a):
        return lax.ppermute(a, AXES, self.pairs)

    def gather(self, piece):
        whole = jnp.zeros((self.shards,) + piece.shape, piece.dtype)
        pieces = [piece]
        for _ in range(self.shards - 1):
            pieces.append(self.send(pieces[-1]))
        for hops, a in enumerate(pieces):
            whole = lax.dynamic_update_index_in_dim(whole, a, self.behind(hops), 0)
        return whole, pieces

    def scatter(self, blocks):
        def own(hops):
            return lax.dynamic_index_in_dim(blocks, self.behind(hops), 0, False)

        moving = own(1)
        for hops in range(2, self.shards + 1):
            arrived = self.send(moving)
            moving = (arrived.astype(F32) + own(hops).astype(F32)).astype(BF16)
        return moving


def tree_sum(a):
    shards = lax.axis_size("shard")
    a = a + core_swap(a)
    if lax.axis_size("x") == 2:
        a = a + x_swap(a)
    step = 1
    while step < shards:
        a = a + lax.ppermute(a, "shard", [(s, s ^ step) for s in range(shards)])
        step *= 2
    return a


def by_core(mine, other, axis):
    first = lax.axis_index("core") == 0
    return jnp.concatenate(
        [jnp.where(first, mine, other), jnp.where(first, other, mine)], axis
    )


def swap_rows(a):
    half = a.shape[0] // 2
    return jnp.concatenate([a[half:], a[:half]], 0)


def core_half(a, axis):
    half = a.shape[axis] // 2
    return lax.dynamic_slice_in_dim(a, lax.axis_index("core") * half, half, axis)


def body(
    tokens,
    attn_gain,
    w_query,
    w_key,
    w_value,
    w_outgate,
    w_rank_in,
    w_rank_out,
    fgate_bias,
    head_gain,
    w_output,
    ffn_gain,
    w_gate,
    w_up,
    w_down,
    out_grad,
):
    seqs, tok_dev, width = tokens.shape
    shards = lax.axis_size("shard")
    xs = lax.axis_size("x")
    core = lax.axis_index("core")
    place = lax.axis_index("shard")
    piece = place % seqs

    def to_chip(step):
        pairs = []
        for j in range(shards):
            for x in range(xs):
                for c in range(2):
                    target = c * seqs + (step + j % seqs) % seqs
                    pairs.append(
                        (device_of(j, x, c, xs), device_of(target, x, j // seqs, xs))
                    )
        return pairs

    def rows_in(a):
        return jnp.concatenate(
            [
                lax.ppermute(
                    lax.dynamic_index_in_dim(a, (step + piece) % seqs, 0, False),
                    AXES,
                    to_chip(step),
                )
                for step in range(seqs)
            ],
            0,
        )

    def rows_out(a):
        back = [
            lax.ppermute(
                a[step * tok_dev : (step + 1) * tok_dev],
                AXES,
                [(t, s) for s, t in to_chip(step)],
            )
            for step in range(seqs)
        ]
        twice = jnp.stack(back + back, 0)
        return lax.dynamic_slice_in_dim(twice, (seqs - piece) % seqs, seqs, 0)

    counter = jnp.arange(shards, dtype=jnp.int32)
    order = ((counter // seqs) ^ core) * seqs + (piece - counter) % seqs
    order = order.astype(jnp.int32)
    sums, masks, upper = level_tables()
    sums, masks, upper = jnp.asarray(sums, BF16), jnp.asarray(masks, F32), jnp.asarray(upper, BF16)

    rank_pack = jnp.concatenate(
        [
            w_rank_in,
            jnp.pad(w_rank_out, ((0, w_rank_in.shape[0] - w_rank_out.shape[0]), (0, 0))),
            jnp.zeros((w_rank_in.shape[0], 96), BF16),
        ],
        1,
    )
    ck, cv = PAIR * DK, PAIR * DV
    packed = jnp.concatenate(
        [core_half(w, 1) for w in (w_query, w_key, w_value, w_outgate, w_output)] + [rank_pack], 1
    )
    wide = 2 * ck + 2 * cv
    own = rows_in(tokens)
    ring = Ring()
    attn_full, attn_pieces = ring.gather(packed)
    attn_full = attn_full.reshape(width, -1)
    cols_piece = jnp.concatenate([core_half(w_gate, 1), core_half(w_up, 1)], 1)
    cols_piece, down_piece, grad_in, _ = lax.optimization_barrier(
        (cols_piece, core_half(w_down, 0), out_grad, attn_pieces[-2])
    )
    ffn_cols, _ = ring.gather(cols_piece)
    ffn_cols = ffn_cols.reshape(width, -1)
    down_rows, _ = ring.gather(down_piece)
    own_grad = rows_in(grad_in)

    x_low = jnp.concatenate([own, core_swap(own)], 0)
    inputs = x_low.astype(F32)
    r_in = lax.rsqrt(jnp.mean(inputs * inputs, axis=1, keepdims=True) + EPSILON)
    attn_row = attn_gain.astype(F32)
    normed = (inputs * r_in * attn_row).astype(BF16)

    w_qkvo = attn_full[:, :wide]
    rank_in = attn_full[:, wide + cv : wide + cv + 16]
    rank_out = attn_full[:, wide + cv + 16 : wide + cv + 32]
    rank_out = rank_out.reshape(shards, -1, 16)[:, : w_rank_out.shape[0]].reshape(-1, 16)
    rank_out = core_half(rank_out, 0)
    queries = product(normed, w_qkvo[:, :ck]).astype(BF16)
    keys = product(normed, w_qkvo[:, ck : 2 * ck]).astype(BF16)
    values = product(normed, w_qkvo[:, 2 * ck : 2 * ck + cv]).astype(BF16)
    out_gate = product(normed, w_qkvo[:, 2 * ck + cv :])
    rank_rows = product(normed, rank_in).astype(BF16)
    logits = times_transpose(rank_rows, rank_out) + core_half(fgate_bias, 0).astype(F32)
    gain = head_gain.astype(F32)[None]
    gated, mixed, states = mix_forward(
        order, queries, keys, values, logits, out_gate, gain, sums, masks
    )
    gated_full = by_core(gated, swap_rows(core_swap(gated)), 1)
    out_mine = attn_full[:, wide : wide + cv]
    w_out_full = by_core(out_mine, core_swap(out_mine), 1)
    residual = inputs + product(gated_full, w_out_full)
    r_ffn = lax.rsqrt(jnp.mean(residual * residual, axis=1, keepdims=True) + EPSILON)
    ffn_row = ffn_gain.astype(F32)
    ffn_in = (residual * r_ffn * ffn_row).astype(BF16)

    ff_half = w_gate.shape[1] // 2
    group = shards // 2
    mine_down = lax.dynamic_slice_in_dim(down_rows, core * group, group, 0)
    send_down = lax.dynamic_slice_in_dim(down_rows, (1 - core) * group, group, 0)
    other_down = core_swap(send_down)
    w_down_half = by_core(mine_down, other_down, 1).reshape(ff_half, width)
    w_gate_half, w_up_half = ffn_cols[:, :ff_half], ffn_cols[:, ff_half:]

    dy = jnp.concatenate([own_grad, core_swap(own_grad)], 0)
    gate = product(ffn_in, w_gate_half)
    up = product(ffn_in, w_up_half)
    sig = sigmoid(gate)
    act = gate * sig
    hidden = (act * up).astype(BF16)
    d_hidden = times_transpose(dy, w_down_half)
    d_gate = (d_hidden * up * (sig * (1.0 + gate * (1.0 - sig)))).astype(BF16)
    d_up = (d_hidden * act).astype(BF16)
    half_rows = x_low.shape[0] // 2
    block_part = product(hidden, w_down_half)
    block_own = (
        residual[:half_rows] + block_part[:half_rows] + core_swap(block_part[half_rows:])
    ).astype(BF16)
    block_out = rows_out(block_own)

    down_grad = outer_sum(hidden, dy).astype(BF16).reshape(group, 2, -1, width)
    mine_dg = lax.dynamic_index_in_dim(down_grad, core, 1, False)
    other_dg = core_swap(lax.dynamic_index_in_dim(down_grad, 1 - core, 1, False))
    down_grad = by_core(mine_dg, other_dg, 0)
    down_own = ring.scatter(down_grad)
    gate_own = ring.scatter(outer_sum(ffn_in, d_gate).astype(BF16).reshape(shards, -1, ff_half))
    up_own = ring.scatter(outer_sum(ffn_in, d_up).astype(BF16).reshape(shards, -1, ff_half))

    dn_part = times_transpose(d_gate, w_gate_half) + times_transpose(d_up, w_up_half)
    dn_ffn = dn_part + swap_rows(core_swap(dn_part))
    u = ffn_row * dn_ffn
    d_residual = dy.astype(F32) + r_ffn * (
        u - residual * (r_ffn * r_ffn) * jnp.mean(u * residual, axis=1, keepdims=True)
    )
    ffn_gain_grad = jnp.sum((dn_ffn * residual * r_ffn)[:half_rows], axis=0)
    d_branch = d_residual.astype(BF16)
    out_w_grad = outer_sum(gated_full, core_half(d_branch, 1))
    d_gated = times_transpose(d_branch, core_half(w_out_full, 0))
    d_all, d_logits, hgain_part, bias_part = mix_backward(
        order, queries, keys, values, logits, out_gate, mixed, d_gated, states, gain,
        sums, masks, upper
    )
    rank_out_grad = outer_sum(rank_rows, d_logits)
    rank_part = product(d_logits, rank_out)
    d_rank = (rank_part + swap_rows(core_swap(rank_part))).astype(BF16)
    rank_in_grad = outer_sum(d_rank[:half_rows], normed[:half_rows])
    qkvo_grad = outer_sum(normed, d_all)
    attn_own = ring.scatter(qkvo_grad.astype(BF16).reshape(shards, -1, wide))
    wout_own = ring.scatter(out_w_grad.astype(BF16).reshape(shards, -1, cv))
    dn_attn = times_transpose(d_all, w_qkvo)
    dn_own = (
        dn_attn[:half_rows]
        + core_swap(dn_attn[half_rows:])
        + times_transpose(d_rank[:half_rows], rank_in)
    )
    own_in, own_r = inputs[:half_rows], r_in[:half_rows]
    u = attn_row * dn_own
    tok_grad = (
        d_residual[:half_rows]
        + own_r * (u - own_in * (own_r * own_r) * jnp.mean(u * own_in, axis=1, keepdims=True))
    ).astype(BF16)
    tokens_grad = rows_out(tok_grad)
    attn_gain_grad = jnp.sum(dn_own * own_in * own_r, axis=0)

    first = (core == 0).astype(F32)

    def spread(a):
        return jnp.concatenate([a * first, a * (1.0 - first)], 1)

    rank_out_both = spread(rank_out_grad)
    lanes = 128

    def flat(a):
        return a.reshape(-1, lanes)

    parts = (
        attn_gain_grad[None], spread(bias_part), hgain_part, ffn_gain_grad[None],
        rank_in_grad, rank_out_both,
    )
    small = tree_sum(jnp.concatenate([flat(a) for a in parts], 0))
    pieces, at = [], 0
    for a in parts:
        size = a.size // lanes
        pieces.append(small[at : at + size].reshape(a.shape))
        at += size
    rin_rows, rout_rows = w_rank_in.shape[0], w_rank_out.shape[0]
    rank_in_own = lax.dynamic_slice_in_dim(pieces[4], place * rin_rows, rin_rows, 1).T
    rank_out_own = lax.dynamic_slice_in_dim(pieces[5].T, place * rout_rows, rout_rows, 0)

    def settle(moving):
        total = moving.astype(F32)
        if xs == 2:
            total = total + x_swap(moving).astype(F32)
        return total, core_swap(total)

    attn_mine, attn_other = settle(attn_own)

    def columns(mine, other, start, size):
        return by_core(mine[:, start : start + size], other[:, start : start + size], 1)

    return (
        block_out,
        tokens_grad,
        pieces[0][0],
        columns(attn_mine, attn_other, 0, ck),
        columns(attn_mine, attn_other, ck, ck),
        columns(attn_mine, attn_other, 2 * ck, cv),
        columns(attn_mine, attn_other, 2 * ck + cv, cv),
        rank_in_own,
        rank_out_own,
        pieces[1][0],
        pieces[2][0],
        by_core(*settle(wout_own), 1),
        pieces[3][0],
        by_core(*settle(gate_own), 1),
        by_core(*settle(up_own), 1),
        by_core(*settle(down_own), 0),
    )


def solution(mesh):
    shards = mesh.shape["shard"]
    reps = mesh.shape["rep"]

    def run(*arrays):
        tokens = arrays[0]
        seqs = tokens.shape[0] // reps
        narrow = reps == 4 and shards == 2 * seqs and tokens.shape[1] // shards == CHUNK
        if narrow:
            grid = Mesh(mesh.devices.reshape(shards, reps // 2, 2), AXES)
            rep = ("x", "core")
        else:
            grid, rep = mesh, "rep"
        rows, cols = P(rep, "shard", None), P("shard", None)
        in_specs = (rows, P()) + (cols,) * 6 + (P(), P(), cols, P()) + (cols,) * 3 + (rows,)
        out_specs = (rows, rows, P()) + (cols,) * 6 + (P(), P(), cols, P()) + (cols,) * 3
        return jax.shard_map(
            body if narrow else wide_body,
            mesh=grid,
            in_specs=in_specs,
            out_specs=out_specs,
            check_vma=False,
        )(*arrays)

    return run
```

```python
import jax
import jax.numpy as jnp
from jax import lax
import numpy as np
from jax.experimental import pallas as pl
from jax.experimental.pallas import tpu as pltpu
from jax.sharding import Mesh
from jax.sharding import PartitionSpec as P

HEADS = 4
KD = 512
VD = 1024
SPAN = 64
DK = 128
DV = 256


PRECISE = lax.Precision.HIGHEST
EPSILON = 1e-06
GATE_NORM = 16.0


def entering(part, axis, combine, identity, reverse):
    count = lax.axis_size(axis)
    place = lax.axis_index(axis)
    ahead = count - 1 - place if reverse else place
    gathered = jax.tree.map(lambda a: lax.all_gather(a, axis), part)
    state = jax.tree.map(lambda a, e: jnp.zeros_like(a) + jnp.asarray(e, a.dtype), part, identity)

    def one(hop, state):
        source = count - 1 - hop if reverse else hop
        return combine(
            state, jax.tree.map(lambda a: lax.dynamic_index_in_dim(a, source, 0, False), gathered)
        )

    return lax.fori_loop(0, ahead, one, state)


def product(left_side, right_side):
    return jnp.dot(left_side, right_side, preferred_element_type=jnp.float32)


def times_transpose(left_side, right_side):
    return lax.dot_general(
        left_side, right_side, (((1,), (1,)), ((), ())), preferred_element_type=jnp.float32
    )


def outer_sum(left_side, right_side):
    return lax.dot_general(
        left_side, right_side, (((0,), (0,)), ((), ())), preferred_element_type=jnp.float32
    )


def root_norm(values, gain_row):
    return (
        values * lax.rsqrt(jnp.mean(values * values, axis=-1, keepdims=True) + EPSILON) * gain_row
    )


def gated_heads(mixed_rows, gain_row, out_gate):
    heads_normed = root_norm(mixed_rows, gain_row)
    return (heads_normed * jax.nn.silu(out_gate.reshape(mixed_rows.shape))).reshape(out_gate.shape)


def silu_product(gate_rows, up_rows):
    return jax.nn.silu(gate_rows) * up_rows


def forget_log(logits):
    return jax.nn.log_sigmoid(logits) / GATE_NORM


def chain_link(earlier, later):
    return (earlier[0] * later[0], later[0][..., None] * earlier[1] + later[1])


def local_mixing(queries, key_rows, value_rows, decays, start_state):
    cumulated = jnp.cumsum(decays, axis=2)
    closing = cumulated[:, :, -1]
    causal_mask = jnp.arange(SPAN)[:, None] >= jnp.arange(SPAN)[None, :]
    differences = cumulated[:, :, :, None] - cumulated[:, :, None, :]
    differences = jnp.where(causal_mask[:, :, None, None], differences, 0.0)
    weights = jnp.exp(differences)
    scores = jnp.einsum("bntha,bnsha,bntsha->bnhts", queries, key_rows, weights, precision=PRECISE)
    scores = jnp.where(causal_mask, scores, 0.0)
    query_scaled = queries * jnp.exp(cumulated)
    key_tail = key_rows * jnp.exp(closing[:, :, None] - cumulated)
    inner = jnp.einsum("bnhts,bnshe->bnthe", scores, value_rows, precision=PRECISE)
    pieces = jnp.einsum("bnsha,bnshe->nbhae", key_tail, value_rows, precision=PRECISE)
    rates = jnp.exp(jnp.moveaxis(closing, 1, 0))

    def advance(carried, item):
        piece, rate = item
        return (rate[..., None] * carried + piece, carried)

    final_state, starts = lax.scan(advance, start_state, (pieces, rates))
    carried_part = jnp.einsum("bntha,nbhae->bnthe", query_scaled, starts, precision=PRECISE)
    return (inner + carried_part, final_state)


def wide_body(
    tokens,
    attn_gain,
    w_query,
    w_key,
    w_value,
    w_outgate,
    w_rank_in,
    w_rank_out,
    fgate_bias,
    head_gain,
    w_output,
    ffn_gain,
    w_gate,
    w_up,
    w_down,
    out_grad,
):
    seqs, tok_dev, width = tokens.shape
    blocks = tok_dev // SPAN
    count = seqs * tok_dev
    gathered = (
        lax.all_gather(w_query, "shard", axis=0, tiled=True),
        lax.all_gather(w_key, "shard", axis=0, tiled=True),
        lax.all_gather(w_value, "shard", axis=0, tiled=True),
        lax.all_gather(w_outgate, "shard", axis=0, tiled=True),
        lax.all_gather(w_rank_in, "shard", axis=0, tiled=True),
        lax.all_gather(w_rank_out, "shard", axis=0, tiled=True),
        lax.all_gather(w_output, "shard", axis=0, tiled=True),
        lax.all_gather(w_gate, "shard", axis=0, tiled=True),
        lax.all_gather(w_up, "shard", axis=0, tiled=True),
        lax.all_gather(w_down, "shard", axis=0, tiled=True),
    )
    (
        query_full,
        key_full,
        value_full,
        outgate_full,
        rank_in_full,
        rank_out_full,
        output_full,
        gate_full,
        up_full,
        down_full,
    ) = gathered
    inputs = tokens.reshape(count, width).astype(jnp.float32)
    normed, norm_back = jax.vjp(root_norm, inputs, attn_gain.astype(jnp.float32))
    normed_low = normed.astype(jnp.bfloat16)
    queries = product(normed_low, query_full).astype(jnp.bfloat16)
    key_rows = product(normed_low, key_full).astype(jnp.bfloat16)
    value_rows = product(normed_low, value_full).astype(jnp.bfloat16)
    out_gate = product(normed_low, outgate_full)
    rank_rows = product(normed_low, rank_in_full).astype(jnp.bfloat16)
    logits = times_transpose(rank_rows, rank_out_full) + fgate_bias.astype(jnp.float32)
    decays, gate_back = jax.vjp(forget_log, logits)
    shape_key = (seqs, blocks, SPAN, HEADS, DK)
    shape_value = (seqs, blocks, SPAN, HEADS, DV)
    query_blocks = queries.astype(jnp.float32).reshape(shape_key)
    key_blocks = key_rows.astype(jnp.float32).reshape(shape_key)
    value_blocks = value_rows.astype(jnp.float32).reshape(shape_value)
    decay_blocks = decays.reshape(shape_key)
    cumulated = jnp.cumsum(decay_blocks, axis=2)
    block_total = cumulated[:, :, -1]
    running = jnp.cumsum(block_total, axis=1)
    preceding = running - block_total
    device_total = running[:, -1]
    tail_keys = key_blocks * jnp.exp(
        device_total[:, None, None] - preceding[:, :, None] - cumulated
    )
    local_end = jnp.einsum("bntha,bnthe->bhae", tail_keys, value_blocks, precision=PRECISE)
    total_rate = jnp.exp(device_total)
    unit_rate = jnp.ones_like(total_rate)
    scanned = entering(
        (total_rate, local_end), "shard", chain_link, (unit_rate, jnp.zeros_like(local_end)), False
    )
    (mixed, final_state), mix_back = jax.vjp(
        local_mixing, query_blocks, key_blocks, value_blocks, decay_blocks, scanned[1]
    )
    mixed_rows = mixed.reshape(count, HEADS, DV)
    gated, gated_back = jax.vjp(gated_heads, mixed_rows, head_gain.astype(jnp.float32), out_gate)
    gated_low = gated.astype(jnp.bfloat16)
    residual = inputs + product(gated_low, output_full)
    normed_ffn, ffn_norm_back = jax.vjp(root_norm, residual, ffn_gain.astype(jnp.float32))
    ffn_input = normed_ffn.astype(jnp.bfloat16)
    gate_rows = product(ffn_input, gate_full)
    up_rows = product(ffn_input, up_full)
    hidden, act_back = jax.vjp(silu_product, gate_rows, up_rows)
    hidden_low = hidden.astype(jnp.bfloat16)
    block_out = (residual + product(hidden_low, down_full)).astype(jnp.bfloat16)
    grad_rows = out_grad.reshape(count, width)
    down_grad = outer_sum(hidden_low, grad_rows)
    hidden_grad = times_transpose(grad_rows, down_full)
    gate_grad, up_grad = act_back(hidden_grad)
    gate_grad_low = gate_grad.astype(jnp.bfloat16)
    up_grad_low = up_grad.astype(jnp.bfloat16)
    gate_w_grad = outer_sum(ffn_input, gate_grad_low)
    up_w_grad = outer_sum(ffn_input, up_grad_low)
    ffn_input_grad = times_transpose(gate_grad_low, gate_full) + times_transpose(
        up_grad_low, up_full
    )
    residual_part, ffn_gain_grad = ffn_norm_back(ffn_input_grad)
    residual_grad = grad_rows.astype(jnp.float32) + residual_part
    branch_grad = residual_grad.astype(jnp.bfloat16)
    output_w_grad = outer_sum(gated_low, branch_grad)
    gated_grad = times_transpose(branch_grad, output_full)
    mixed_grad, head_gain_grad, out_gate_grad = gated_back(gated_grad)
    mixed_grad_blocks = mixed_grad.reshape(shape_value)
    early_queries = query_blocks * jnp.exp(preceding[:, :, None] + cumulated)
    back_part = jnp.einsum("bntha,bnthe->bhae", early_queries, mixed_grad_blocks, precision=PRECISE)
    rescanned = entering(
        (total_rate, back_part), "shard", chain_link, (unit_rate, jnp.zeros_like(back_part)), True
    )
    pulled = mix_back((mixed_grad_blocks, rescanned[1]))
    query_grad_low = pulled[0].reshape(count, KD).astype(jnp.bfloat16)
    key_grad_low = pulled[1].reshape(count, KD).astype(jnp.bfloat16)
    value_grad_low = pulled[2].reshape(count, VD).astype(jnp.bfloat16)
    logit_grad = gate_back(pulled[3].reshape(count, KD))[0]
    logit_grad_low = logit_grad.astype(jnp.bfloat16)
    out_gate_low = out_gate_grad.astype(jnp.bfloat16)
    bias_grad = jnp.sum(logit_grad_low.astype(jnp.float32), axis=0)
    rank_out_grad = outer_sum(logit_grad_low, rank_rows)
    rank_grad_low = product(logit_grad_low, rank_out_full).astype(jnp.bfloat16)
    rank_in_grad = outer_sum(normed_low, rank_grad_low)
    query_w_grad = outer_sum(normed_low, query_grad_low)
    key_w_grad = outer_sum(normed_low, key_grad_low)
    value_w_grad = outer_sum(normed_low, value_grad_low)
    outgate_w_grad = outer_sum(normed_low, out_gate_low)
    normed_grad = (
        times_transpose(query_grad_low, query_full)
        + times_transpose(key_grad_low, key_full)
        + times_transpose(value_grad_low, value_full)
        + times_transpose(out_gate_low, outgate_full)
        + times_transpose(rank_grad_low, rank_in_full)
    )
    input_part, attn_gain_grad = norm_back(normed_grad)
    tokens_grad = (residual_grad + input_part).astype(jnp.bfloat16).reshape(tokens.shape)
    matrices = (
        query_w_grad,
        key_w_grad,
        value_w_grad,
        outgate_w_grad,
        rank_in_grad,
        rank_out_grad,
        output_w_grad,
        gate_w_grad,
        up_w_grad,
        down_grad,
    )
    owned = (
        lax.psum_scatter(matrices[0], "shard", scatter_dimension=0, tiled=True),
        lax.psum_scatter(matrices[1], "shard", scatter_dimension=0, tiled=True),
        lax.psum_scatter(matrices[2], "shard", scatter_dimension=0, tiled=True),
        lax.psum_scatter(matrices[3], "shard", scatter_dimension=0, tiled=True),
        lax.psum_scatter(matrices[4], "shard", scatter_dimension=0, tiled=True),
        lax.psum_scatter(matrices[5], "shard", scatter_dimension=0, tiled=True),
        lax.psum_scatter(matrices[6], "shard", scatter_dimension=0, tiled=True),
        lax.psum_scatter(matrices[7], "shard", scatter_dimension=0, tiled=True),
        lax.psum_scatter(matrices[8], "shard", scatter_dimension=0, tiled=True),
        lax.psum_scatter(matrices[9], "shard", scatter_dimension=0, tiled=True),
    )
    owned = lax.psum(
        (
            owned[0],
            owned[1],
            owned[2],
            owned[3],
            owned[4],
            owned[5],
            owned[6],
            owned[7],
            owned[8],
            owned[9],
        ),
        "rep",
    )
    small = lax.psum((attn_gain_grad, bias_grad, head_gain_grad, ffn_gain_grad), ("shard", "rep"))
    return (
        block_out.reshape(tokens.shape),
        tokens_grad,
        small[0],
        owned[0],
        owned[1],
        owned[2],
        owned[3],
        owned[4],
        owned[5],
        small[1],
        small[2],
        owned[6],
        small[3],
        owned[7],
        owned[8],
        owned[9],
    )


CHUNK = 128
LEVELS = (64, 32, 16, 8, 4, 2, 1)
PAIR = 2
AXES = ("shard", "x", "core")
BF16 = jnp.bfloat16
F32 = jnp.float32


def level_tables():
    rows = np.arange(CHUNK)
    t, u = rows[:, None], rows[None, :]
    sums = [(u <= t), (u > t)]
    masks = [(t == u)]
    for size in LEVELS:
        same = (t // (2 * size)) == (u // (2 * size))
        late_t = (t % (2 * size)) >= size
        late_u = (u % (2 * size)) >= size
        sums.append(
            same & ((late_t & late_u & (u <= t)) | (~late_t & ~late_u & (u > t)))
        )
        masks.append(same & late_t & ~late_u)
    sums = np.concatenate(sums, 0).astype(np.float32)
    masks = np.stack(masks, 0).astype(np.float32)
    upper = (u >= t).astype(np.float32)
    return (
        np.concatenate([sums, sums], 1),
        masks,
        np.concatenate([upper, upper], 1),
    )


def dot_nn(a, b):
    return lax.dot_general(a, b, (((1,), (0,)), ((), ())), preferred_element_type=F32)


def dot_nt(a, b):
    return lax.dot_general(a, b, (((1,), (1,)), ((), ())), preferred_element_type=F32)


def dot_tn(a, b):
    return lax.dot_general(a, b, (((0,), (0,)), ((), ())), preferred_element_type=F32)


def split(a):
    high = a.astype(BF16)
    return high, (a - high.astype(F32)).astype(BF16)


def fine(dot, a, b):
    ah, al = split(a)
    bh, bl = split(b)
    return dot(ah, bh) + (dot(ah, bl) + dot(al, bh))


def half_fine(dot, a, b):
    ah, al = split(a)
    return dot(ah, b) + dot(al, b)


def summed(table, values):
    high = values.astype(BF16)
    rest = (values - high.astype(F32)).astype(BF16)
    return dot_nn(table, jnp.concatenate([high, rest], 0))


def log_decay(logits):
    return (jnp.minimum(logits, 0.0) - jnp.log(1.0 + jnp.exp(-jnp.abs(logits)))) / GATE_NORM


def sigmoid(z):
    return 1.0 / (1.0 + jnp.exp(-z))


def mix_forward_kernel(
    order, q_ref, k_ref, v_ref, lg_ref, og_ref, gain_ref, sums_ref, mask_ref,
    gated_ref, mixed_ref, states_ref, state
):
    @pl.when(pl.program_id(0) == 0)
    def _():
        state[...] = jnp.zeros_like(state)

    factors = jnp.exp(summed(sums_ref[...], log_decay(lg_ref[...])))
    for head in range(PAIR):
        kc = slice(head * DK, (head + 1) * DK)
        vc = slice(head * DV, (head + 1) * DV)
        q_low, k_low, v_low = q_ref[:, kc], k_ref[:, kc], v_ref[:, vc]
        q, k = q_low.astype(F32), k_low.astype(F32)
        scores = mask_ref[0] * dot_nt(q_low, k_low)
        for level in range(len(LEVELS)):
            e = factors[(level + 2) * CHUNK : (level + 3) * CHUNK, kc]
            scores += mask_ref[level + 1] * fine(dot_nt, q * e, k * e)
        before = factors[:CHUNK, kc]
        after = factors[CHUNK : 2 * CHUNK, kc]
        carried = state[head]
        states_ref[0, head] = carried
        mixed = half_fine(dot_nn, scores, v_low) + fine(dot_nt, q * before, carried)
        k_high, k_rest = split(k * after)
        state[head] = carried * before[CHUNK - 1 :] + (
            dot_tn(v_low, k_high) + dot_tn(v_low, k_rest)
        )
        mixed_ref[:, vc] = mixed
        normed = mixed * lax.rsqrt(jnp.mean(mixed * mixed, axis=1, keepdims=True) + EPSILON)
        og = og_ref[:, vc]
        gated_ref[:, vc] = (normed * gain_ref[...] * (og * sigmoid(og))).astype(BF16)


def mix_backward_kernel(
    order, q_ref, k_ref, v_ref, lg_ref, og_ref, mixed_ref, dg_ref, states_ref, gain_ref,
    sums_ref, mask_ref, upper_ref,
    dall_ref, dlog_ref, hgain_ref, bias_ref, dstate, carry
):
    @pl.when(pl.program_id(0) == 0)
    def _():
        dstate[...] = jnp.zeros_like(dstate)
        carry[...] = jnp.zeros_like(carry)
        hgain_ref[...] = jnp.zeros_like(hgain_ref)
        bias_ref[...] = jnp.zeros_like(bias_ref)

    logits = lg_ref[...]
    factors = jnp.exp(summed(sums_ref[...], log_decay(logits)))
    gain = gain_ref[...]
    flows = []
    for head in range(PAIR):
        kc = slice(head * DK, (head + 1) * DK)
        vc = slice(head * DV, (head + 1) * DV)
        og, m, dg = og_ref[:, vc], mixed_ref[:, vc], dg_ref[:, vc]
        sig = sigmoid(og)
        r = lax.rsqrt(jnp.mean(m * m, axis=1, keepdims=True) + EPSILON)
        n = m * r
        dn = dg * (og * sig)
        hgain_ref[...] += jnp.sum(dn * n, axis=0, keepdims=True)
        u = gain * dn
        dm = r * (u - n * jnp.mean(u * n, axis=1, keepdims=True))
        dog = dg * (n * gain) * (sig * (1.0 + og * (1.0 - sig)))
        dall_ref[:, 2 * PAIR * DK + PAIR * DV + head * DV : 2 * PAIR * DK + PAIR * DV + (head + 1) * DV] = dog.astype(BF16)
        dm_low = dm.astype(BF16)
        q_low, k_low, v_low = q_ref[:, kc], k_ref[:, kc], v_ref[:, vc]
        q, k = q_low.astype(F32), k_low.astype(F32)
        dm_rest = (dm - dm_low.astype(F32)).astype(BF16)
        da = dot_nt(dm_low, v_low) + dot_nt(dm_rest, v_low)
        before = factors[:CHUNK, kc]
        after = factors[CHUNK : 2 * CHUNK, kc]
        carried = states_ref[0, head]
        ds = dstate[head]
        ds_low = ds.astype(BF16)
        q_in = (q * before).astype(BF16)
        k_out = (k * after).astype(BF16)
        scores = mask_ref[0] * dot_nt(q_low, k_low)
        part = (mask_ref[0] * da).astype(BF16)
        dq = dot_nn(part, k_low) + before * dot_nn(dm_low, carried.astype(BF16))
        dk = dot_tn(part, q_low) + after * dot_nn(v_low, ds_low)
        for level in range(len(LEVELS)):
            e = factors[(level + 2) * CHUNK : (level + 3) * CHUNK, kc]
            q_e, k_e = (q * e).astype(BF16), (k * e).astype(BF16)
            scores += mask_ref[level + 1] * dot_nt(q_e, k_e)
            part = (mask_ref[level + 1] * da).astype(BF16)
            dq += e * dot_nn(part, k_e)
            dk += e * dot_tn(part, q_e)
        dv = dot_tn(scores.astype(BF16), dm_low) + dot_nt(k_out, ds_low)
        dall_ref[:, kc] = dq.astype(BF16)
        dall_ref[:, PAIR * DK + head * DK : PAIR * DK + (head + 1) * DK] = dk.astype(BF16)
        dall_ref[:, 2 * PAIR * DK + head * DV : 2 * PAIR * DK + (head + 1) * DV] = dv.astype(BF16)
        ds = ds * before[CHUNK - 1 :] + dot_tn(dm_low, q_in)
        dstate[head] = ds
        flows.append(q * dq - k * dk)
        carried_flow = jnp.sum(carried * ds, axis=0, keepdims=True)
        flows.append(carried_flow)
    flow = jnp.concatenate([flows[0], flows[2]], 1)
    d_decay = summed(upper_ref[...], flow) + carry[...]
    carry[...] = jnp.concatenate([flows[1], flows[3]], 1)
    dlog = (d_decay * (sigmoid(-logits) * (1.0 / GATE_NORM))).astype(BF16)
    dlog_ref[...] = dlog
    bias_ref[...] += jnp.sum(dlog.astype(F32), axis=0, keepdims=True)


def mix_forward(order, q, k, v, logits, og, gain, sums, masks):
    rows = q.shape[0]
    steps = rows // CHUNK
    ck, cv = PAIR * DK, PAIR * DV

    def row_block(width):
        return pl.BlockSpec((CHUNK, width), lambda g, o: (o[g], 0))

    def whole(a):
        return pl.BlockSpec(a.shape, lambda g, o: (0,) * a.ndim)

    return pl.pallas_call(
        mix_forward_kernel,
        grid_spec=pltpu.PrefetchScalarGridSpec(
            num_scalar_prefetch=1,
            grid=(steps,),
            in_specs=[row_block(ck), row_block(ck), row_block(cv), row_block(ck), row_block(cv),
                      whole(gain), whole(sums), whole(masks)],
            out_specs=[row_block(cv), row_block(cv),
                       pl.BlockSpec((1, PAIR, DV, DK), lambda g, o: (g, 0, 0, 0))],
            scratch_shapes=[pltpu.VMEM((PAIR, DV, DK), F32)],
        ),
        out_shape=[jax.ShapeDtypeStruct((rows, cv), BF16), jax.ShapeDtypeStruct((rows, cv), F32),
                   jax.ShapeDtypeStruct((steps, PAIR, DV, DK), F32)],
        compiler_params=pltpu.CompilerParams(vmem_limit_bytes=58 * 1024 * 1024),
        cost_estimate=pl.CostEstimate(flops=1000, bytes_accessed=1000, transcendentals=0),
        name="mix_forward",
    )(order, q, k, v, logits, og, gain, sums, masks)


def mix_backward(order, q, k, v, logits, og, mixed, d_gated, states, gain, sums, masks, upper):
    rows = q.shape[0]
    steps = rows // CHUNK
    ck, cv = PAIR * DK, PAIR * DV

    def row_block(width):
        return pl.BlockSpec((CHUNK, width), lambda g, o: (o[steps - 1 - g], 0))

    def whole(a):
        return pl.BlockSpec(a.shape, lambda g, o: (0,) * a.ndim)

    return pl.pallas_call(
        mix_backward_kernel,
        grid_spec=pltpu.PrefetchScalarGridSpec(
            num_scalar_prefetch=1,
            grid=(steps,),
            in_specs=[row_block(ck), row_block(ck), row_block(cv), row_block(ck), row_block(cv),
                      row_block(cv), row_block(cv),
                      pl.BlockSpec((1, PAIR, DV, DK), lambda g, o: (steps - 1 - g, 0, 0, 0)),
                      whole(gain), whole(sums), whole(masks), whole(upper)],
            out_specs=[row_block(2 * ck + 2 * cv), row_block(ck),
                       pl.BlockSpec((1, DV), lambda g, o: (0, 0)),
                       pl.BlockSpec((1, ck), lambda g, o: (0, 0))],
            scratch_shapes=[pltpu.VMEM((PAIR, DV, DK), F32), pltpu.VMEM((1, ck), F32)],
        ),
        out_shape=[jax.ShapeDtypeStruct((rows, 2 * ck + 2 * cv), BF16), jax.ShapeDtypeStruct((rows, ck), BF16),
                   jax.ShapeDtypeStruct((1, DV), F32), jax.ShapeDtypeStruct((1, ck), F32)],
        compiler_params=pltpu.CompilerParams(vmem_limit_bytes=58 * 1024 * 1024),
        cost_estimate=pl.CostEstimate(flops=1000, bytes_accessed=1000, transcendentals=0),
        name="mix_backward",
    )(order, q, k, v, logits, og, mixed, d_gated, states, gain, sums, masks, upper)


FREE = pl.CostEstimate(flops=1000, bytes_accessed=1000, transcendentals=0)
ROOMY = pltpu.CompilerParams(vmem_limit_bytes=58 * 1024 * 1024)


def held(a):
    return pl.BlockSpec(a.shape, lambda *g: (0,) * a.ndim, pipeline_mode=pl.Buffered(1))


def tiles(rows, width):
    return pl.BlockSpec((rows, width), lambda g: (g, 0))


def attn_in_kernel(x_ref, gain_ref, w_ref, rank_ref, bias_ref, n_ref, q_ref, k_ref, v_ref, og_ref, rr_ref, lg_ref):
    ck, cv = q_ref.shape[1], v_ref.shape[1]
    x = x_ref[...].astype(F32)
    r = lax.rsqrt(jnp.mean(x * x, axis=1, keepdims=True) + EPSILON)
    n = (x * r * gain_ref[...]).astype(BF16)
    n_ref[...] = n
    q_ref[...] = dot_nn(n, w_ref[:, :ck]).astype(BF16)
    k_ref[...] = dot_nn(n, w_ref[:, ck : 2 * ck]).astype(BF16)
    v_ref[...] = dot_nn(n, w_ref[:, 2 * ck : 2 * ck + cv]).astype(BF16)
    og_ref[...] = dot_nn(n, w_ref[:, 2 * ck + cv : 2 * ck + 2 * cv])
    rank = dot_nn(n, w_ref[:, 2 * ck + 3 * cv :]).astype(BF16)
    rr_ref[...] = rank
    lg_ref[...] = dot_nt(rank, rank_ref[...]) + bias_ref[...]


def attn_in(x, gain, w, rank, bias):
    rows, ck, cv, step = x.shape[0], PAIR * DK, PAIR * DV, 256
    shapes = [(x.shape[1], BF16), (ck, BF16), (ck, BF16), (cv, BF16), (cv, F32), (128, BF16), (ck, F32)]
    return pl.pallas_call(
        attn_in_kernel,
        grid=(rows // step,),
        in_specs=[tiles(step, x.shape[1]), held(gain), held(w), held(rank), held(bias)],
        out_specs=[tiles(step, c) for c, _ in shapes],
        out_shape=[jax.ShapeDtypeStruct((rows, c), t) for c, t in shapes],
        compiler_params=ROOMY,
        cost_estimate=FREE,
        name="attn_in",
    )(x, gain, w, rank, bias)


def attn_out_kernel(x_ref, g_ref, w_ref, gain_ref, res_ref, n_ref, r_ref):
    res = x_ref[...].astype(F32) + dot_nn(g_ref[...], w_ref[...])
    r = lax.rsqrt(jnp.mean(res * res, axis=1, keepdims=True) + EPSILON)
    res_ref[...] = res
    n_ref[...] = (res * r * gain_ref[...]).astype(BF16)
    r_ref[...] = r


def attn_out(x, gated, w, gain):
    rows, width = x.shape
    step = 256
    return pl.pallas_call(
        attn_out_kernel,
        grid=(rows // step,),
        in_specs=[tiles(step, width), tiles(step, gated.shape[1]), held(w), held(gain)],
        out_specs=[tiles(step, width), tiles(step, width), tiles(step, 1)],
        out_shape=[jax.ShapeDtypeStruct((rows, width), F32), jax.ShapeDtypeStruct((rows, width), BF16),
                   jax.ShapeDtypeStruct((rows, 1), F32)],
        compiler_params=ROOMY,
        cost_estimate=FREE,
        name="attn_out",
    )(x, gated, w, gain)


def ffn_kernel(plane, n_ref, dy_ref, near_ref, far_ref, down_ref, hid_ref, near_d_ref, far_d_ref, block_ref, dn_ref):
    straight = plane[0] == 0
    n = n_ref[...]
    near = dot_nn(n, near_ref[...])
    far = dot_nn(n, far_ref[...])
    gate, up = jnp.where(straight, near, far), jnp.where(straight, far, near)
    sig = sigmoid(gate)
    act = gate * sig
    hidden = (act * up).astype(BF16)
    hid_ref[...] = hidden
    d_hidden = dot_nt(dy_ref[...], down_ref[...])
    d_gate = d_hidden * up * (sig + act * (1.0 - sig))
    d_up = d_hidden * act
    d_near = jnp.where(straight, d_gate, d_up).astype(BF16)
    d_far = jnp.where(straight, d_up, d_gate).astype(BF16)
    near_d_ref[...] = d_near
    far_d_ref[...] = d_far
    block_ref[...] = dot_nn(hidden, down_ref[...])
    dn_ref[...] = dot_nt(d_near, near_ref[...]) + dot_nt(d_far, far_ref[...])


def ffn(plane, n, dy, near, far, down):
    rows, width = n.shape
    ff, step = near.shape[1], 256

    def row(width):
        return pl.BlockSpec((step, width), lambda g, p: (g, 0))

    return pl.pallas_call(
        ffn_kernel,
        grid_spec=pltpu.PrefetchScalarGridSpec(
            num_scalar_prefetch=1,
            grid=(rows // step,),
            in_specs=[row(width), row(width), held(near), held(far), held(down)],
            out_specs=[row(ff), row(ff), row(ff), row(width), row(width)],
        ),
        out_shape=[jax.ShapeDtypeStruct((rows, ff), BF16)] * 3
        + [jax.ShapeDtypeStruct((rows, width), F32)] * 2,
        compiler_params=ROOMY,
        cost_estimate=FREE,
        name="ffn",
    )(plane, n, dy, near, far, down)


def branch_kernel(dn_ref, sw_ref, dy_ref, res_ref, r_ref, gain_ref, w_ref, d_ref, low_ref, dg_ref, fg_ref):
    step = pl.program_id(0)

    @pl.when(step == 0)
    def _():
        fg_ref[...] = jnp.zeros_like(fg_ref)

    dn = dn_ref[...] + sw_ref[...]
    res, r = res_ref[...], r_ref[...]
    n = res * r

    @pl.when(step < pl.num_programs(0) // 2)
    def _():
        fg_ref[...] += jnp.sum(dn * n, axis=0, keepdims=True)

    u = gain_ref[...] * dn
    d = dy_ref[...].astype(F32) + r * (u - n * jnp.mean(u * n, axis=1, keepdims=True))
    low = d.astype(BF16)
    d_ref[...] = d
    low_ref[...] = low
    dg_ref[...] = dot_nt(low, w_ref[...])


def branch(dn, swapped, dy, res, r, gain, w):
    rows, width = dn.shape
    step = 256
    count = rows // step
    other = pl.BlockSpec((step, width), lambda g: ((g + count // 2) % count, 0))
    full = tiles(step, width)
    return pl.pallas_call(
        branch_kernel,
        grid=(count,),
        in_specs=[full, other, full, full, tiles(step, 1), held(gain), held(w)],
        out_specs=[full, full, tiles(step, w.shape[0]), pl.BlockSpec((1, width), lambda g: (0, 0))],
        out_shape=[jax.ShapeDtypeStruct((rows, width), F32), jax.ShapeDtypeStruct((rows, width), BF16),
                   jax.ShapeDtypeStruct((rows, w.shape[0]), F32), jax.ShapeDtypeStruct((1, width), F32)],
        compiler_params=ROOMY,
        cost_estimate=FREE,
        name="branch",
    )(dn, swapped, dy, res, r, gain, w)


def outer_kernel(n_ref, d_ref, g_ref):
    g_ref[...] = dot_tn(n_ref[...], d_ref[...]).astype(BF16)


def outer(n, d, step=256):
    rows, width = n.shape
    return pl.pallas_call(
        outer_kernel,
        grid=(width // step,),
        in_specs=[pl.BlockSpec((rows, step), lambda i: (0, i)), held(d)],
        out_specs=tiles(step, d.shape[1]),
        out_shape=jax.ShapeDtypeStruct((width, d.shape[1]), BF16),
        compiler_params=ROOMY,
        cost_estimate=FREE,
        name="outer",
    )(n, d)


def device_of(shard, x, core, xs):
    return (shard * xs + x) * 2 + core


def core_swap(a):
    return lax.ppermute(a, "core", [(0, 1), (1, 0)])


def x_swap(a):
    return lax.ppermute(a, "x", [(0, 1), (1, 0)])


def ring_order(shards):
    return list(range(0, shards, 2)) + list(range(shards - 1, 0, -2))


class Ring:
    def __init__(self):
        self.shards, self.xs = lax.axis_size("shard"), lax.axis_size("x")
        self.core = lax.axis_index("core")
        cycle = ring_order(self.shards)
        spot = [cycle.index(s) for s in range(self.shards)]
        self.cycle = jnp.asarray(cycle, jnp.int32)
        self.spot = jnp.asarray(spot, jnp.int32)[lax.axis_index("shard")]
        self.sign = 1 - 2 * self.core
        self.pairs = []
        for s in range(self.shards):
            for x in range(self.xs):
                for c in range(2):
                    step = 1 if c == 0 else -1
                    to = cycle[(spot[s] + step) % self.shards]
                    self.pairs.append(
                        (device_of(s, x, c, self.xs), device_of(to, x, c, self.xs))
                    )

    def behind(self, hops):
        return self.cycle[(self.spot - self.sign * hops) % self.shards]

    def send(self, a):
        return lax.ppermute(a, AXES, self.pairs)

    def gather(self, piece, early=None):
        whole = jnp.zeros((self.shards,) + piece.shape, piece.dtype)
        pieces = [piece]
        for hops in range(self.shards - 1):
            if hops == 1 and early is not None:
                pieces[-1], early = lax.optimization_barrier((pieces[-1], early))
            pieces.append(self.send(pieces[-1]))
        for hops, a in enumerate(pieces):
            whole = lax.dynamic_update_index_in_dim(whole, a, self.behind(hops), 0)
        return whole, pieces, early

    def own(self, blocks, hops):
        return lax.dynamic_index_in_dim(blocks, self.behind(hops), 0, False)


class Gather:
    def __init__(self, ring, piece):
        self.ring, self.hops, self.last = ring, 0, piece
        self.whole = jnp.zeros((ring.shards,) + piece.shape, piece.dtype)
        self.keep(piece)

    def keep(self, piece):
        self.whole = lax.dynamic_update_index_in_dim(
            self.whole, piece, self.ring.behind(self.hops), 0
        )

    def take(self, arrived, *deps):
        self.hops += 1
        self.last = after(arrived, *deps)
        self.keep(self.last)


class Scatter:
    def __init__(self, ring, blocks):
        self.ring, self.blocks, self.hops = ring, blocks, 1
        self.moving = ring.own(blocks, 1)

    def hop(self, *deps):
        self.hops += 1
        arrived = self.ring.send(self.moving)
        mine = after(self.ring.own(self.blocks, self.hops), *deps)
        self.moving = (arrived.astype(F32) + mine.astype(F32)).astype(BF16)
        return self.moving


def after(a, *deps):
    return lax.optimization_barrier((a,) + deps)[0] if deps else a


def tree_steps():
    shards = lax.axis_size("shard")
    steps = [core_swap]
    if lax.axis_size("x") == 2:
        steps.append(x_swap)
    step = 1
    while step < shards:
        pairs = [(s, s ^ step) for s in range(shards)]
        steps.append(lambda a, pairs=pairs: lax.ppermute(a, "shard", pairs))
        step *= 2
    return steps


def by_core(mine, other, axis):
    first = lax.axis_index("core") == 0
    return jnp.concatenate(
        [jnp.where(first, mine, other), jnp.where(first, other, mine)], axis
    )


def swap_rows(a):
    half = a.shape[0] // 2
    return jnp.concatenate([a[half:], a[:half]], 0)


def core_half(a, axis):
    half = a.shape[axis] // 2
    return lax.dynamic_slice_in_dim(a, lax.axis_index("core") * half, half, axis)


def body(
    tokens,
    attn_gain,
    w_query,
    w_key,
    w_value,
    w_outgate,
    w_rank_in,
    w_rank_out,
    fgate_bias,
    head_gain,
    w_output,
    ffn_gain,
    w_gate,
    w_up,
    w_down,
    out_grad,
):
    seqs, tok_dev, width = tokens.shape
    shards = lax.axis_size("shard")
    xs = lax.axis_size("x")
    core = lax.axis_index("core")
    place = lax.axis_index("shard")
    piece = place % seqs

    def to_chip(step):
        pairs = []
        for j in range(shards):
            for x in range(xs):
                for c in range(2):
                    target = c * seqs + (step + j % seqs) % seqs
                    pairs.append(
                        (device_of(j, x, c, xs), device_of(target, x, j // seqs, xs))
                    )
        return pairs

    def rows_in(a):
        return jnp.concatenate(
            [
                lax.ppermute(
                    lax.dynamic_index_in_dim(a, (step + piece) % seqs, 0, False),
                    AXES,
                    to_chip(step),
                )
                for step in range(seqs)
            ],
            0,
        )

    def rows_out(a):
        back = [
            lax.ppermute(
                a[step * tok_dev : (step + 1) * tok_dev],
                AXES,
                [(t, s) for s, t in to_chip(step)],
            )
            for step in range(seqs)
        ]
        twice = jnp.stack(back + back, 0)
        return lax.dynamic_slice_in_dim(twice, (seqs - piece) % seqs, seqs, 0)

    counter = jnp.arange(shards, dtype=jnp.int32)
    order = ((counter // seqs) ^ core) * seqs + (piece - counter) % seqs
    order = order.astype(jnp.int32)
    sums, masks, upper = level_tables()
    sums, masks, upper = jnp.asarray(sums, BF16), jnp.asarray(masks, F32), jnp.asarray(upper, BF16)

    rank_pack = jnp.concatenate(
        [
            w_rank_in,
            jnp.pad(w_rank_out, ((0, w_rank_in.shape[0] - w_rank_out.shape[0]), (0, 0))),
            jnp.zeros((w_rank_in.shape[0], 96), BF16),
        ],
        1,
    )
    ck, cv = PAIR * DK, PAIR * DV
    packed = jnp.concatenate(
        [core_half(w, 1) for w in (w_query, w_key, w_value, w_outgate, w_output)] + [rank_pack], 1
    )
    wide = 2 * ck + 2 * cv
    own = rows_in(tokens)
    ring = Ring()
    attn_full, attn_pieces, own = ring.gather(packed, own)
    attn_full = attn_full.reshape(width, -1)
    plane = lax.axis_index("x") == 0
    gate_piece, up_piece = core_half(w_gate, 1), core_half(w_up, 1)
    near_ring = Gather(ring, after(jnp.where(plane, gate_piece, up_piece), attn_pieces[6]))
    far_ring = Gather(ring, jnp.where(plane, up_piece, gate_piece))
    down_ring = Gather(ring, after(core_half(w_down, 0), attn_pieces[6]))
    own_grad = rows_in(after(out_grad, attn_pieces[7]))

    def ffn_hop(*deps):
        down_ring.take(ring.send(down_ring.last), *deps)
        near_ring.take(ring.send(near_ring.last), *deps)
        far_ring.take(x_swap(near_ring.last))

    ffn_hop()
    x_low = jnp.concatenate([own, core_swap(own)], 0)
    attn_row = attn_gain.astype(F32)
    rank_out = attn_full[:, wide + cv + 16 : wide + cv + 32]
    rank_out = rank_out.reshape(shards, -1, 16)[:, : w_rank_out.shape[0]].reshape(-1, 16)
    rank_out = jnp.pad(core_half(rank_out, 0), ((0, 0), (0, 112)))
    bias = core_half(fgate_bias, 0).astype(F32)[None]
    normed, queries, keys, values, out_gate, rank_rows, logits = attn_in(
        x_low, attn_row[None], attn_full, rank_out, bias
    )
    gain = head_gain.astype(F32)[None]
    ffn_hop(queries)
    queries = after(queries, near_ring.last)
    gated, mixed, states = mix_forward(
        order, queries, keys, values, logits, out_gate, gain, sums, masks
    )
    ffn_hop(gated)
    gated = after(gated, near_ring.last)
    gated_full = by_core(gated, swap_rows(core_swap(gated)), 1)
    out_mine = attn_full[:, wide : wide + cv]
    w_out_full = by_core(out_mine, core_swap(out_mine), 1)
    ffn_row = ffn_gain.astype(F32)
    residual, ffn_in, r_ffn = attn_out(x_low, gated_full, w_out_full, ffn_row[None])
    ffn_hop(ffn_in)
    for _ in range(4, shards - 1):
        ffn_hop()
    cols_near = near_ring.whole.reshape(width, -1)
    cols_far = far_ring.whole.reshape(width, -1)
    down_rows = down_ring.whole

    ff_half = w_gate.shape[1] // 2
    group = shards // 2
    mine_down = lax.dynamic_slice_in_dim(down_rows, core * group, group, 0)
    send_down = lax.dynamic_slice_in_dim(down_rows, (1 - core) * group, group, 0)
    other_down = core_swap(send_down)
    w_down_half = by_core(mine_down, other_down, 1).reshape(ff_half, width)

    dy = jnp.concatenate([own_grad, core_swap(own_grad)], 0)
    turn = lax.axis_index("x")[None].astype(jnp.int32)
    hidden, d_near, d_far, block_part, dn_part = ffn(
        turn, ffn_in, dy, cols_near, cols_far, w_down_half
    )
    half_rows = x_low.shape[0] // 2
    dn_swapped = core_swap(dn_part)
    block_swapped = core_swap(block_part[half_rows:])
    far_part = outer(ffn_in, d_far)
    grad_far = x_swap(far_part)
    grad_near = outer(after(ffn_in, far_part), d_near)
    hidden = after(hidden, grad_near)
    down_grad = outer(hidden, dy, 128).reshape(group, 2, -1, width)
    mine_dg = lax.dynamic_index_in_dim(down_grad, core, 1, False)
    other_dg = core_swap(lax.dynamic_index_in_dim(down_grad, 1 - core, 1, False))
    down = Scatter(ring, by_core(mine_dg, other_dg, 0))

    d_residual, d_branch, d_gated, ffn_gain_grad = branch(
        dn_part, after(dn_swapped, down.moving), dy, residual, r_ffn, ffn_row[None],
        core_half(w_out_full, 0)
    )
    ffn_gain_grad = ffn_gain_grad[0]
    down.hop(d_gated)
    block_own = (
        residual[:half_rows] + block_part[:half_rows] + after(block_swapped, d_gated)
    ).astype(BF16)
    block_out = rows_out(block_own)
    d_all, d_logits, hgain_part, bias_part = mix_backward(
        order, queries, keys, values, logits, out_gate, mixed, after(d_gated, down.moving),
        states, gain, sums, masks, upper
    )
    down.hop(d_all)
    d_all = after(d_all, down.moving)
    out_w_grad = outer_sum(gated_full, core_half(d_branch, 1))
    qkvo_grad = outer_sum(normed, d_all)
    near_total = after(grad_near, d_all).astype(F32) + grad_far.astype(F32)
    last_grad = jnp.concatenate(
        [qkvo_grad.astype(BF16), out_w_grad.astype(BF16), near_total.astype(BF16)], 1
    )
    attn = Scatter(ring, last_grad.reshape(shards, -1, wide + cv + ff_half))
    down.hop(attn.moving)
    rank_out_grad = outer_sum(rank_rows[:, :16], d_logits)
    rank_part = product(d_logits, rank_out[:, :16])
    rank_swapped = core_swap(rank_part)
    dn_attn = times_transpose(after(d_all, down.moving), attn_full[:, :wide])
    dn_attn_swapped = core_swap(dn_attn[half_rows:])
    attn.hop(dn_attn)
    down.hop(dn_attn, attn.moving)
    dn_attn_swapped = after(dn_attn_swapped, down.moving)
    d_rank = (rank_part + swap_rows(rank_swapped)).astype(BF16)
    rank_in_grad = outer_sum(d_rank[:half_rows], normed[:half_rows])
    dn_own = (
        dn_attn[:half_rows]
        + dn_attn_swapped
        + times_transpose(d_rank[:half_rows], attn_full[:, wide + cv : wide + cv + 16])
    )
    own_in = x_low[:half_rows].astype(F32)
    own_r = lax.rsqrt(jnp.mean(own_in * own_in, axis=1, keepdims=True) + EPSILON)
    u = attn_row * dn_own
    tok_grad = (
        d_residual[:half_rows]
        + own_r * (u - own_in * (own_r * own_r) * jnp.mean(u * own_in, axis=1, keepdims=True))
    ).astype(BF16)
    attn_gain_grad = jnp.sum(dn_own * own_in * own_r, axis=0)
    attn.hop(tok_grad)
    down.hop(tok_grad, attn.moving)
    tokens_grad = rows_out(after(tok_grad, down.moving))

    first = (core == 0).astype(F32)

    def spread(a):
        return jnp.concatenate([a * first, a * (1.0 - first)], 1)

    rank_out_both = spread(rank_out_grad)
    lanes = 128

    def flat(a):
        return a.reshape(-1, lanes)

    parts = (
        attn_gain_grad[None], spread(bias_part), hgain_part, ffn_gain_grad[None],
        rank_in_grad, rank_out_both,
    )
    small = jnp.concatenate([flat(a) for a in parts], 0)
    steps = tree_steps()
    for count in range(3, shards):
        if count < 3 + len(steps):
            small = small + steps[count - 3](small)
        attn.hop(small)
        if down.hops < shards:
            down.hop(attn.moving)
            small = after(small, down.moving)
        else:
            small = after(small, attn.moving)
    for step in steps[shards - 3 :]:
        small = small + step(small)
    last_own, down_own = attn.moving, down.moving
    last_far = x_swap(last_own)
    split_at = wide + cv
    near_own, far_own = last_own[:, split_at:], last_far[:, split_at:]
    gate_own = jnp.where(plane, near_own, far_own)
    up_own = jnp.where(plane, far_own, near_own)
    pieces, at = [], 0
    for a in parts:
        size = a.size // lanes
        pieces.append(small[at : at + size].reshape(a.shape))
        at += size
    rin_rows, rout_rows = w_rank_in.shape[0], w_rank_out.shape[0]
    rank_in_own = lax.dynamic_slice_in_dim(pieces[4], place * rin_rows, rin_rows, 1).T
    rank_out_own = lax.dynamic_slice_in_dim(pieces[5].T, place * rout_rows, rout_rows, 0)

    def settle(moving):
        total = moving.astype(F32)
        if xs == 2:
            total = total + x_swap(moving).astype(F32)
        return total, core_swap(total)

    attn_mine = last_own[:, :split_at].astype(F32) + last_far[:, :split_at].astype(F32)
    attn_other = core_swap(attn_mine)

    def columns(mine, other, start, size):
        return by_core(mine[:, start : start + size], other[:, start : start + size], 1)

    return (
        block_out,
        tokens_grad,
        pieces[0][0],
        columns(attn_mine, attn_other, 0, ck),
        columns(attn_mine, attn_other, ck, ck),
        columns(attn_mine, attn_other, 2 * ck, cv),
        columns(attn_mine, attn_other, 2 * ck + cv, cv),
        rank_in_own,
        rank_out_own,
        pieces[1][0],
        pieces[2][0],
        columns(attn_mine, attn_other, wide, cv),
        pieces[3][0],
        by_core(gate_own, core_swap(gate_own), 1).astype(F32),
        by_core(up_own, core_swap(up_own), 1).astype(F32),
        by_core(*settle(down_own), 0),
    )


def solution(mesh):
    shards = mesh.shape["shard"]
    reps = mesh.shape["rep"]

    def run(*arrays):
        tokens = arrays[0]
        seqs = tokens.shape[0] // reps
        narrow = reps == 4 and shards == 2 * seqs and tokens.shape[1] // shards == CHUNK
        if narrow:
            grid = Mesh(mesh.devices.reshape(shards, reps // 2, 2), AXES)
            rep = ("x", "core")
        else:
            grid, rep = mesh, "rep"
        rows, cols = P(rep, "shard", None), P("shard", None)
        in_specs = (rows, P()) + (cols,) * 6 + (P(), P(), cols, P()) + (cols,) * 3 + (rows,)
        out_specs = (rows, rows, P()) + (cols,) * 6 + (P(), P(), cols, P()) + (cols,) * 3
        return jax.shard_map(
            body if narrow else wide_body,
            mesh=grid,
            in_specs=in_specs,
            out_specs=out_specs,
            check_vma=False,
        )(*arrays)

    return run
```

```python
import jax
import jax.numpy as jnp
from jax import lax
import numpy as np
from jax.experimental import pallas as pl
from jax.experimental.pallas import tpu as pltpu
from jax.sharding import Mesh
from jax.sharding import PartitionSpec as P

HEADS = 4
KD = 512
VD = 1024
SPAN = 64
DK = 128
DV = 256


PRECISE = lax.Precision.HIGHEST
EPSILON = 1e-06
GATE_NORM = 16.0


def entering(part, axis, combine, identity, reverse):
    count = lax.axis_size(axis)
    place = lax.axis_index(axis)
    ahead = count - 1 - place if reverse else place
    gathered = jax.tree.map(lambda a: lax.all_gather(a, axis), part)
    state = jax.tree.map(lambda a, e: jnp.zeros_like(a) + jnp.asarray(e, a.dtype), part, identity)

    def one(hop, state):
        source = count - 1 - hop if reverse else hop
        return combine(
            state, jax.tree.map(lambda a: lax.dynamic_index_in_dim(a, source, 0, False), gathered)
        )

    return lax.fori_loop(0, ahead, one, state)


def product(left_side, right_side):
    return jnp.dot(left_side, right_side, preferred_element_type=jnp.float32)


def times_transpose(left_side, right_side):
    return lax.dot_general(
        left_side, right_side, (((1,), (1,)), ((), ())), preferred_element_type=jnp.float32
    )


def outer_sum(left_side, right_side):
    return lax.dot_general(
        left_side, right_side, (((0,), (0,)), ((), ())), preferred_element_type=jnp.float32
    )


def root_norm(values, gain_row):
    return (
        values * lax.rsqrt(jnp.mean(values * values, axis=-1, keepdims=True) + EPSILON) * gain_row
    )


def gated_heads(mixed_rows, gain_row, out_gate):
    heads_normed = root_norm(mixed_rows, gain_row)
    return (heads_normed * jax.nn.silu(out_gate.reshape(mixed_rows.shape))).reshape(out_gate.shape)


def silu_product(gate_rows, up_rows):
    return jax.nn.silu(gate_rows) * up_rows


def forget_log(logits):
    return jax.nn.log_sigmoid(logits) / GATE_NORM


def chain_link(earlier, later):
    return (earlier[0] * later[0], later[0][..., None] * earlier[1] + later[1])


def local_mixing(queries, key_rows, value_rows, decays, start_state):
    cumulated = jnp.cumsum(decays, axis=2)
    closing = cumulated[:, :, -1]
    causal_mask = jnp.arange(SPAN)[:, None] >= jnp.arange(SPAN)[None, :]
    differences = cumulated[:, :, :, None] - cumulated[:, :, None, :]
    differences = jnp.where(causal_mask[:, :, None, None], differences, 0.0)
    weights = jnp.exp(differences)
    scores = jnp.einsum("bntha,bnsha,bntsha->bnhts", queries, key_rows, weights, precision=PRECISE)
    scores = jnp.where(causal_mask, scores, 0.0)
    query_scaled = queries * jnp.exp(cumulated)
    key_tail = key_rows * jnp.exp(closing[:, :, None] - cumulated)
    inner = jnp.einsum("bnhts,bnshe->bnthe", scores, value_rows, precision=PRECISE)
    pieces = jnp.einsum("bnsha,bnshe->nbhae", key_tail, value_rows, precision=PRECISE)
    rates = jnp.exp(jnp.moveaxis(closing, 1, 0))

    def advance(carried, item):
        piece, rate = item
        return (rate[..., None] * carried + piece, carried)

    final_state, starts = lax.scan(advance, start_state, (pieces, rates))
    carried_part = jnp.einsum("bntha,nbhae->bnthe", query_scaled, starts, precision=PRECISE)
    return (inner + carried_part, final_state)


def wide_body(
    tokens,
    attn_gain,
    w_query,
    w_key,
    w_value,
    w_outgate,
    w_rank_in,
    w_rank_out,
    fgate_bias,
    head_gain,
    w_output,
    ffn_gain,
    w_gate,
    w_up,
    w_down,
    out_grad,
):
    seqs, tok_dev, width = tokens.shape
    blocks = tok_dev // SPAN
    count = seqs * tok_dev
    gathered = (
        lax.all_gather(w_query, "shard", axis=0, tiled=True),
        lax.all_gather(w_key, "shard", axis=0, tiled=True),
        lax.all_gather(w_value, "shard", axis=0, tiled=True),
        lax.all_gather(w_outgate, "shard", axis=0, tiled=True),
        lax.all_gather(w_rank_in, "shard", axis=0, tiled=True),
        lax.all_gather(w_rank_out, "shard", axis=0, tiled=True),
        lax.all_gather(w_output, "shard", axis=0, tiled=True),
        lax.all_gather(w_gate, "shard", axis=0, tiled=True),
        lax.all_gather(w_up, "shard", axis=0, tiled=True),
        lax.all_gather(w_down, "shard", axis=0, tiled=True),
    )
    (
        query_full,
        key_full,
        value_full,
        outgate_full,
        rank_in_full,
        rank_out_full,
        output_full,
        gate_full,
        up_full,
        down_full,
    ) = gathered
    inputs = tokens.reshape(count, width).astype(jnp.float32)
    normed, norm_back = jax.vjp(root_norm, inputs, attn_gain.astype(jnp.float32))
    normed_low = normed.astype(jnp.bfloat16)
    queries = product(normed_low, query_full).astype(jnp.bfloat16)
    key_rows = product(normed_low, key_full).astype(jnp.bfloat16)
    value_rows = product(normed_low, value_full).astype(jnp.bfloat16)
    out_gate = product(normed_low, outgate_full)
    rank_rows = product(normed_low, rank_in_full).astype(jnp.bfloat16)
    logits = times_transpose(rank_rows, rank_out_full) + fgate_bias.astype(jnp.float32)
    decays, gate_back = jax.vjp(forget_log, logits)
    shape_key = (seqs, blocks, SPAN, HEADS, DK)
    shape_value = (seqs, blocks, SPAN, HEADS, DV)
    query_blocks = queries.astype(jnp.float32).reshape(shape_key)
    key_blocks = key_rows.astype(jnp.float32).reshape(shape_key)
    value_blocks = value_rows.astype(jnp.float32).reshape(shape_value)
    decay_blocks = decays.reshape(shape_key)
    cumulated = jnp.cumsum(decay_blocks, axis=2)
    block_total = cumulated[:, :, -1]
    running = jnp.cumsum(block_total, axis=1)
    preceding = running - block_total
    device_total = running[:, -1]
    tail_keys = key_blocks * jnp.exp(
        device_total[:, None, None] - preceding[:, :, None] - cumulated
    )
    local_end = jnp.einsum("bntha,bnthe->bhae", tail_keys, value_blocks, precision=PRECISE)
    total_rate = jnp.exp(device_total)
    unit_rate = jnp.ones_like(total_rate)
    scanned = entering(
        (total_rate, local_end), "shard", chain_link, (unit_rate, jnp.zeros_like(local_end)), False
    )
    (mixed, final_state), mix_back = jax.vjp(
        local_mixing, query_blocks, key_blocks, value_blocks, decay_blocks, scanned[1]
    )
    mixed_rows = mixed.reshape(count, HEADS, DV)
    gated, gated_back = jax.vjp(gated_heads, mixed_rows, head_gain.astype(jnp.float32), out_gate)
    gated_low = gated.astype(jnp.bfloat16)
    residual = inputs + product(gated_low, output_full)
    normed_ffn, ffn_norm_back = jax.vjp(root_norm, residual, ffn_gain.astype(jnp.float32))
    ffn_input = normed_ffn.astype(jnp.bfloat16)
    gate_rows = product(ffn_input, gate_full)
    up_rows = product(ffn_input, up_full)
    hidden, act_back = jax.vjp(silu_product, gate_rows, up_rows)
    hidden_low = hidden.astype(jnp.bfloat16)
    block_out = (residual + product(hidden_low, down_full)).astype(jnp.bfloat16)
    grad_rows = out_grad.reshape(count, width)
    down_grad = outer_sum(hidden_low, grad_rows)
    hidden_grad = times_transpose(grad_rows, down_full)
    gate_grad, up_grad = act_back(hidden_grad)
    gate_grad_low = gate_grad.astype(jnp.bfloat16)
    up_grad_low = up_grad.astype(jnp.bfloat16)
    gate_w_grad = outer_sum(ffn_input, gate_grad_low)
    up_w_grad = outer_sum(ffn_input, up_grad_low)
    ffn_input_grad = times_transpose(gate_grad_low, gate_full) + times_transpose(
        up_grad_low, up_full
    )
    residual_part, ffn_gain_grad = ffn_norm_back(ffn_input_grad)
    residual_grad = grad_rows.astype(jnp.float32) + residual_part
    branch_grad = residual_grad.astype(jnp.bfloat16)
    output_w_grad = outer_sum(gated_low, branch_grad)
    gated_grad = times_transpose(branch_grad, output_full)
    mixed_grad, head_gain_grad, out_gate_grad = gated_back(gated_grad)
    mixed_grad_blocks = mixed_grad.reshape(shape_value)
    early_queries = query_blocks * jnp.exp(preceding[:, :, None] + cumulated)
    back_part = jnp.einsum("bntha,bnthe->bhae", early_queries, mixed_grad_blocks, precision=PRECISE)
    rescanned = entering(
        (total_rate, back_part), "shard", chain_link, (unit_rate, jnp.zeros_like(back_part)), True
    )
    pulled = mix_back((mixed_grad_blocks, rescanned[1]))
    query_grad_low = pulled[0].reshape(count, KD).astype(jnp.bfloat16)
    key_grad_low = pulled[1].reshape(count, KD).astype(jnp.bfloat16)
    value_grad_low = pulled[2].reshape(count, VD).astype(jnp.bfloat16)
    logit_grad = gate_back(pulled[3].reshape(count, KD))[0]
    logit_grad_low = logit_grad.astype(jnp.bfloat16)
    out_gate_low = out_gate_grad.astype(jnp.bfloat16)
    bias_grad = jnp.sum(logit_grad_low.astype(jnp.float32), axis=0)
    rank_out_grad = outer_sum(logit_grad_low, rank_rows)
    rank_grad_low = product(logit_grad_low, rank_out_full).astype(jnp.bfloat16)
    rank_in_grad = outer_sum(normed_low, rank_grad_low)
    query_w_grad = outer_sum(normed_low, query_grad_low)
    key_w_grad = outer_sum(normed_low, key_grad_low)
    value_w_grad = outer_sum(normed_low, value_grad_low)
    outgate_w_grad = outer_sum(normed_low, out_gate_low)
    normed_grad = (
        times_transpose(query_grad_low, query_full)
        + times_transpose(key_grad_low, key_full)
        + times_transpose(value_grad_low, value_full)
        + times_transpose(out_gate_low, outgate_full)
        + times_transpose(rank_grad_low, rank_in_full)
    )
    input_part, attn_gain_grad = norm_back(normed_grad)
    tokens_grad = (residual_grad + input_part).astype(jnp.bfloat16).reshape(tokens.shape)
    matrices = (
        query_w_grad,
        key_w_grad,
        value_w_grad,
        outgate_w_grad,
        rank_in_grad,
        rank_out_grad,
        output_w_grad,
        gate_w_grad,
        up_w_grad,
        down_grad,
    )
    owned = (
        lax.psum_scatter(matrices[0], "shard", scatter_dimension=0, tiled=True),
        lax.psum_scatter(matrices[1], "shard", scatter_dimension=0, tiled=True),
        lax.psum_scatter(matrices[2], "shard", scatter_dimension=0, tiled=True),
        lax.psum_scatter(matrices[3], "shard", scatter_dimension=0, tiled=True),
        lax.psum_scatter(matrices[4], "shard", scatter_dimension=0, tiled=True),
        lax.psum_scatter(matrices[5], "shard", scatter_dimension=0, tiled=True),
        lax.psum_scatter(matrices[6], "shard", scatter_dimension=0, tiled=True),
        lax.psum_scatter(matrices[7], "shard", scatter_dimension=0, tiled=True),
        lax.psum_scatter(matrices[8], "shard", scatter_dimension=0, tiled=True),
        lax.psum_scatter(matrices[9], "shard", scatter_dimension=0, tiled=True),
    )
    owned = lax.psum(
        (
            owned[0],
            owned[1],
            owned[2],
            owned[3],
            owned[4],
            owned[5],
            owned[6],
            owned[7],
            owned[8],
            owned[9],
        ),
        "rep",
    )
    small = lax.psum((attn_gain_grad, bias_grad, head_gain_grad, ffn_gain_grad), ("shard", "rep"))
    return (
        block_out.reshape(tokens.shape),
        tokens_grad,
        small[0],
        owned[0],
        owned[1],
        owned[2],
        owned[3],
        owned[4],
        owned[5],
        small[1],
        small[2],
        owned[6],
        small[3],
        owned[7],
        owned[8],
        owned[9],
    )


CHUNK = 128
LEVELS = (64, 32, 16, 8, 4, 2, 1)
PAIR = 2
AXES = ("shard", "x", "core")
BF16 = jnp.bfloat16
F32 = jnp.float32


def level_tables():
    rows = np.arange(CHUNK)
    t, u = rows[:, None], rows[None, :]
    sums = [(u <= t), (u > t)]
    masks = [(t == u)]
    for size in LEVELS:
        same = (t // (2 * size)) == (u // (2 * size))
        late_t = (t % (2 * size)) >= size
        late_u = (u % (2 * size)) >= size
        sums.append(
            same & ((late_t & late_u & (u <= t)) | (~late_t & ~late_u & (u > t)))
        )
        masks.append(same & late_t & ~late_u)
    sums = np.concatenate(sums, 0).astype(np.float32)
    masks = np.stack(masks, 0).astype(np.float32)
    upper = (u >= t).astype(np.float32)
    return (
        np.concatenate([sums, sums], 1),
        masks,
        np.concatenate([upper, upper], 1),
    )


def dot_nn(a, b):
    return lax.dot_general(a, b, (((1,), (0,)), ((), ())), preferred_element_type=F32)


def dot_nt(a, b):
    return lax.dot_general(a, b, (((1,), (1,)), ((), ())), preferred_element_type=F32)


def dot_tn(a, b):
    return lax.dot_general(a, b, (((0,), (0,)), ((), ())), preferred_element_type=F32)


def split(a):
    high = a.astype(BF16)
    return high, (a - high.astype(F32)).astype(BF16)


def fine(dot, a, b):
    ah, al = split(a)
    bh, bl = split(b)
    return dot(ah, bh) + (dot(ah, bl) + dot(al, bh))


def half_fine(dot, a, b):
    ah, al = split(a)
    return dot(ah, b) + dot(al, b)


def summed(table, values):
    high = values.astype(BF16)
    rest = (values - high.astype(F32)).astype(BF16)
    return dot_nn(table, jnp.concatenate([high, rest], 0))


def log_decay(logits):
    return (jnp.minimum(logits, 0.0) - jnp.log(1.0 + jnp.exp(-jnp.abs(logits)))) / GATE_NORM


def sigmoid(z):
    return 1.0 / (1.0 + jnp.exp(-z))


def mix_forward_kernel(
    order, q_ref, k_ref, v_ref, lg_ref, og_ref, gain_ref, sums_ref, mask_ref,
    gated_ref, mixed_ref, states_ref, state
):
    @pl.when(pl.program_id(0) == 0)
    def _():
        state[...] = jnp.zeros_like(state)

    factors = jnp.exp(summed(sums_ref[...], log_decay(lg_ref[...])))
    for head in range(PAIR):
        kc = slice(head * DK, (head + 1) * DK)
        vc = slice(head * DV, (head + 1) * DV)
        q_low, k_low, v_low = q_ref[:, kc], k_ref[:, kc], v_ref[:, vc]
        q, k = q_low.astype(F32), k_low.astype(F32)
        scores = mask_ref[0] * dot_nt(q_low, k_low)
        for level in range(len(LEVELS)):
            e = factors[(level + 2) * CHUNK : (level + 3) * CHUNK, kc]
            scores += mask_ref[level + 1] * fine(dot_nt, q * e, k * e)
        before = factors[:CHUNK, kc]
        after = factors[CHUNK : 2 * CHUNK, kc]
        carried = state[head]
        states_ref[0, head] = carried
        mixed = half_fine(dot_nn, scores, v_low) + fine(dot_nt, q * before, carried)
        k_high, k_rest = split(k * after)
        state[head] = carried * before[CHUNK - 1 :] + (
            dot_tn(v_low, k_high) + dot_tn(v_low, k_rest)
        )
        mixed_ref[:, vc] = mixed
        normed = mixed * lax.rsqrt(jnp.mean(mixed * mixed, axis=1, keepdims=True) + EPSILON)
        og = og_ref[:, vc]
        gated_ref[:, vc] = (normed * gain_ref[...] * (og * sigmoid(og))).astype(BF16)


def mix_backward_kernel(
    order, q_ref, k_ref, v_ref, lg_ref, og_ref, mixed_ref, dg_ref, states_ref, gain_ref,
    sums_ref, mask_ref, upper_ref,
    dall_ref, dlog_ref, hgain_ref, bias_ref, dstate, carry
):
    @pl.when(pl.program_id(0) == 0)
    def _():
        dstate[...] = jnp.zeros_like(dstate)
        carry[...] = jnp.zeros_like(carry)
        hgain_ref[...] = jnp.zeros_like(hgain_ref)
        bias_ref[...] = jnp.zeros_like(bias_ref)

    logits = lg_ref[...]
    factors = jnp.exp(summed(sums_ref[...], log_decay(logits)))
    gain = gain_ref[...]
    flows = []
    for head in range(PAIR):
        kc = slice(head * DK, (head + 1) * DK)
        vc = slice(head * DV, (head + 1) * DV)
        og, m, dg = og_ref[:, vc], mixed_ref[:, vc], dg_ref[:, vc]
        sig = sigmoid(og)
        r = lax.rsqrt(jnp.mean(m * m, axis=1, keepdims=True) + EPSILON)
        n = m * r
        dn = dg * (og * sig)
        hgain_ref[...] += jnp.sum(dn * n, axis=0, keepdims=True)
        u = gain * dn
        dm = r * (u - n * jnp.mean(u * n, axis=1, keepdims=True))
        dog = dg * (n * gain) * (sig * (1.0 + og * (1.0 - sig)))
        dall_ref[:, 2 * PAIR * DK + PAIR * DV + head * DV : 2 * PAIR * DK + PAIR * DV + (head + 1) * DV] = dog.astype(BF16)
        dm_low = dm.astype(BF16)
        q_low, k_low, v_low = q_ref[:, kc], k_ref[:, kc], v_ref[:, vc]
        q, k = q_low.astype(F32), k_low.astype(F32)
        dm_rest = (dm - dm_low.astype(F32)).astype(BF16)
        da = dot_nt(dm_low, v_low) + dot_nt(dm_rest, v_low)
        before = factors[:CHUNK, kc]
        after = factors[CHUNK : 2 * CHUNK, kc]
        carried = states_ref[0, head]
        ds = dstate[head]
        ds_low = ds.astype(BF16)
        q_in = (q * before).astype(BF16)
        k_out = (k * after).astype(BF16)
        scores = mask_ref[0] * dot_nt(q_low, k_low)
        part = (mask_ref[0] * da).astype(BF16)
        dq = dot_nn(part, k_low) + before * dot_nn(dm_low, carried.astype(BF16))
        dk = dot_tn(part, q_low) + after * dot_nn(v_low, ds_low)
        for level in range(len(LEVELS)):
            e = factors[(level + 2) * CHUNK : (level + 3) * CHUNK, kc]
            q_e, k_e = (q * e).astype(BF16), (k * e).astype(BF16)
            scores += mask_ref[level + 1] * dot_nt(q_e, k_e)
            part = (mask_ref[level + 1] * da).astype(BF16)
            dq += e * dot_nn(part, k_e)
            dk += e * dot_tn(part, q_e)
        dv = dot_tn(scores.astype(BF16), dm_low) + dot_nt(k_out, ds_low)
        dall_ref[:, kc] = dq.astype(BF16)
        dall_ref[:, PAIR * DK + head * DK : PAIR * DK + (head + 1) * DK] = dk.astype(BF16)
        dall_ref[:, 2 * PAIR * DK + head * DV : 2 * PAIR * DK + (head + 1) * DV] = dv.astype(BF16)
        ds = ds * before[CHUNK - 1 :] + dot_tn(dm_low, q_in)
        dstate[head] = ds
        flows.append(q * dq - k * dk)
        carried_flow = jnp.sum(carried * ds, axis=0, keepdims=True)
        flows.append(carried_flow)
    flow = jnp.concatenate([flows[0], flows[2]], 1)
    d_decay = summed(upper_ref[...], flow) + carry[...]
    carry[...] = jnp.concatenate([flows[1], flows[3]], 1)
    dlog = (d_decay * (sigmoid(-logits) * (1.0 / GATE_NORM))).astype(BF16)
    dlog_ref[...] = dlog
    bias_ref[...] += jnp.sum(dlog.astype(F32), axis=0, keepdims=True)


def mix_forward(order, q, k, v, logits, og, gain, sums, masks):
    rows = q.shape[0]
    steps = rows // CHUNK
    ck, cv = PAIR * DK, PAIR * DV

    def row_block(width):
        return pl.BlockSpec((CHUNK, width), lambda g, o: (o[g], 0))

    def whole(a):
        return pl.BlockSpec(a.shape, lambda g, o: (0,) * a.ndim)

    return pl.pallas_call(
        mix_forward_kernel,
        grid_spec=pltpu.PrefetchScalarGridSpec(
            num_scalar_prefetch=1,
            grid=(steps,),
            in_specs=[row_block(ck), row_block(ck), row_block(cv), row_block(ck), row_block(cv),
                      whole(gain), whole(sums), whole(masks)],
            out_specs=[row_block(cv), row_block(cv),
                       pl.BlockSpec((1, PAIR, DV, DK), lambda g, o: (g, 0, 0, 0))],
            scratch_shapes=[pltpu.VMEM((PAIR, DV, DK), F32)],
        ),
        out_shape=[jax.ShapeDtypeStruct((rows, cv), BF16), jax.ShapeDtypeStruct((rows, cv), F32),
                   jax.ShapeDtypeStruct((steps, PAIR, DV, DK), F32)],
        compiler_params=pltpu.CompilerParams(vmem_limit_bytes=58 * 1024 * 1024),
        cost_estimate=pl.CostEstimate(flops=22_000_000_000, bytes_accessed=1000, transcendentals=0),
        name="mix_forward",
    )(order, q, k, v, logits, og, gain, sums, masks)


def mix_backward(order, q, k, v, logits, og, mixed, d_gated, states, gain, sums, masks, upper):
    rows = q.shape[0]
    steps = rows // CHUNK
    ck, cv = PAIR * DK, PAIR * DV

    def row_block(width):
        return pl.BlockSpec((CHUNK, width), lambda g, o: (o[steps - 1 - g], 0))

    def whole(a):
        return pl.BlockSpec(a.shape, lambda g, o: (0,) * a.ndim)

    return pl.pallas_call(
        mix_backward_kernel,
        grid_spec=pltpu.PrefetchScalarGridSpec(
            num_scalar_prefetch=1,
            grid=(steps,),
            in_specs=[row_block(ck), row_block(ck), row_block(cv), row_block(ck), row_block(cv),
                      row_block(cv), row_block(cv),
                      pl.BlockSpec((1, PAIR, DV, DK), lambda g, o: (steps - 1 - g, 0, 0, 0)),
                      whole(gain), whole(sums), whole(masks), whole(upper)],
            out_specs=[row_block(2 * ck + 2 * cv), row_block(ck),
                       pl.BlockSpec((1, DV), lambda g, o: (0, 0)),
                       pl.BlockSpec((1, ck), lambda g, o: (0, 0))],
            scratch_shapes=[pltpu.VMEM((PAIR, DV, DK), F32), pltpu.VMEM((1, ck), F32)],
        ),
        out_shape=[jax.ShapeDtypeStruct((rows, 2 * ck + 2 * cv), BF16), jax.ShapeDtypeStruct((rows, ck), BF16),
                   jax.ShapeDtypeStruct((1, DV), F32), jax.ShapeDtypeStruct((1, ck), F32)],
        compiler_params=pltpu.CompilerParams(vmem_limit_bytes=58 * 1024 * 1024),
        cost_estimate=pl.CostEstimate(flops=6_000_000_000, bytes_accessed=1000, transcendentals=0),
        name="mix_backward",
    )(order, q, k, v, logits, og, mixed, d_gated, states, gain, sums, masks, upper)


FREE = pl.CostEstimate(flops=1000, bytes_accessed=1000, transcendentals=0)
ROOMY = pltpu.CompilerParams(vmem_limit_bytes=58 * 1024 * 1024)


def held(a):
    return pl.BlockSpec(a.shape, lambda *g: (0,) * a.ndim, pipeline_mode=pl.Buffered(1))


def tiles(rows, width):
    return pl.BlockSpec((rows, width), lambda g: (g, 0))


def attn_in_kernel(x_ref, gain_ref, w_ref, rank_ref, bias_ref, n_ref, q_ref, k_ref, v_ref, og_ref, rr_ref, lg_ref):
    ck, cv = q_ref.shape[1], v_ref.shape[1]
    x = x_ref[...].astype(F32)
    r = lax.rsqrt(jnp.mean(x * x, axis=1, keepdims=True) + EPSILON)
    n = (x * r * gain_ref[...]).astype(BF16)
    n_ref[...] = n
    q_ref[...] = dot_nn(n, w_ref[:, :ck]).astype(BF16)
    k_ref[...] = dot_nn(n, w_ref[:, ck : 2 * ck]).astype(BF16)
    v_ref[...] = dot_nn(n, w_ref[:, 2 * ck : 2 * ck + cv]).astype(BF16)
    og_ref[...] = dot_nn(n, w_ref[:, 2 * ck + cv : 2 * ck + 2 * cv])
    rank = dot_nn(n, w_ref[:, 2 * ck + 3 * cv :]).astype(BF16)
    rr_ref[...] = rank
    lg_ref[...] = dot_nt(rank, rank_ref[...]) + bias_ref[...]


def attn_in(x, gain, w, rank, bias):
    rows, ck, cv, step = x.shape[0], PAIR * DK, PAIR * DV, 256
    shapes = [(x.shape[1], BF16), (ck, BF16), (ck, BF16), (cv, BF16), (cv, F32), (128, BF16), (ck, F32)]
    return pl.pallas_call(
        attn_in_kernel,
        grid=(rows // step,),
        in_specs=[tiles(step, x.shape[1]), held(gain), held(w), held(rank), held(bias)],
        out_specs=[tiles(step, c) for c, _ in shapes],
        out_shape=[jax.ShapeDtypeStruct((rows, c), t) for c, t in shapes],
        compiler_params=ROOMY,
        cost_estimate=FREE,
        name="attn_in",
    )(x, gain, w, rank, bias)


def attn_out_kernel(x_ref, g_ref, w_ref, gain_ref, res_ref, n_ref, r_ref):
    res = x_ref[...].astype(F32) + dot_nn(g_ref[...], w_ref[...])
    r = lax.rsqrt(jnp.mean(res * res, axis=1, keepdims=True) + EPSILON)
    res_ref[...] = res
    n_ref[...] = (res * r * gain_ref[...]).astype(BF16)
    r_ref[...] = r


def attn_out(x, gated, w, gain):
    rows, width = x.shape
    step = 256
    return pl.pallas_call(
        attn_out_kernel,
        grid=(rows // step,),
        in_specs=[tiles(step, width), tiles(step, gated.shape[1]), held(w), held(gain)],
        out_specs=[tiles(step, width), tiles(step, width), tiles(step, 1)],
        out_shape=[jax.ShapeDtypeStruct((rows, width), F32), jax.ShapeDtypeStruct((rows, width), BF16),
                   jax.ShapeDtypeStruct((rows, 1), F32)],
        compiler_params=ROOMY,
        cost_estimate=FREE,
        name="attn_out",
    )(x, gated, w, gain)


def ffn_kernel(plane, n_ref, dy_ref, near_ref, far_ref, down_ref, hid_ref, near_d_ref, far_d_ref, block_ref, dn_ref):
    straight = plane[0] == 0
    n = n_ref[...]
    near = dot_nn(n, near_ref[...])
    far = dot_nn(n, far_ref[...])
    gate, up = jnp.where(straight, near, far), jnp.where(straight, far, near)
    sig = sigmoid(gate)
    act = gate * sig
    hidden = (act * up).astype(BF16)
    hid_ref[...] = hidden
    d_hidden = dot_nt(dy_ref[...], down_ref[...])
    d_gate = d_hidden * up * (sig + act * (1.0 - sig))
    d_up = d_hidden * act
    d_near = jnp.where(straight, d_gate, d_up).astype(BF16)
    d_far = jnp.where(straight, d_up, d_gate).astype(BF16)
    near_d_ref[...] = d_near
    far_d_ref[...] = d_far
    block_ref[...] = dot_nn(hidden, down_ref[...])
    dn_ref[...] = dot_nt(d_near, near_ref[...]) + dot_nt(d_far, far_ref[...])


def ffn(plane, n, dy, near, far, down):
    rows, width = n.shape
    ff, step = near.shape[1], 256

    def row(width):
        return pl.BlockSpec((step, width), lambda g, p: (g, 0))

    return pl.pallas_call(
        ffn_kernel,
        grid_spec=pltpu.PrefetchScalarGridSpec(
            num_scalar_prefetch=1,
            grid=(rows // step,),
            in_specs=[row(width), row(width), held(near), held(far), held(down)],
            out_specs=[row(ff), row(ff), row(ff), row(width), row(width)],
        ),
        out_shape=[jax.ShapeDtypeStruct((rows, ff), BF16)] * 3
        + [jax.ShapeDtypeStruct((rows, width), F32)] * 2,
        compiler_params=ROOMY,
        cost_estimate=FREE,
        name="ffn",
    )(plane, n, dy, near, far, down)


def branch_kernel(dn_ref, sw_ref, dy_ref, res_ref, r_ref, gain_ref, w_ref, d_ref, low_ref, dg_ref, fg_ref):
    step = pl.program_id(0)

    @pl.when(step == 0)
    def _():
        fg_ref[...] = jnp.zeros_like(fg_ref)

    dn = dn_ref[...] + sw_ref[...]
    res, r = res_ref[...], r_ref[...]
    n = res * r

    @pl.when(step < pl.num_programs(0) // 2)
    def _():
        fg_ref[...] += jnp.sum(dn * n, axis=0, keepdims=True)

    u = gain_ref[...] * dn
    d = dy_ref[...].astype(F32) + r * (u - n * jnp.mean(u * n, axis=1, keepdims=True))
    low = d.astype(BF16)
    d_ref[...] = d
    low_ref[...] = low
    dg_ref[...] = dot_nt(low, w_ref[...])


def branch(dn, swapped, dy, res, r, gain, w):
    rows, width = dn.shape
    step = 256
    count = rows // step
    other = pl.BlockSpec((step, width), lambda g: ((g + count // 2) % count, 0))
    full = tiles(step, width)
    return pl.pallas_call(
        branch_kernel,
        grid=(count,),
        in_specs=[full, other, full, full, tiles(step, 1), held(gain), held(w)],
        out_specs=[full, full, tiles(step, w.shape[0]), pl.BlockSpec((1, width), lambda g: (0, 0))],
        out_shape=[jax.ShapeDtypeStruct((rows, width), F32), jax.ShapeDtypeStruct((rows, width), BF16),
                   jax.ShapeDtypeStruct((rows, w.shape[0]), F32), jax.ShapeDtypeStruct((1, width), F32)],
        compiler_params=ROOMY,
        cost_estimate=FREE,
        name="branch",
    )(dn, swapped, dy, res, r, gain, w)


def outer_kernel(n_ref, d_ref, g_ref):
    g_ref[...] = dot_tn(n_ref[...], d_ref[...]).astype(BF16)


def outer(n, d, step=256):
    rows, width = n.shape
    return pl.pallas_call(
        outer_kernel,
        grid=(width // step,),
        in_specs=[pl.BlockSpec((rows, step), lambda i: (0, i)), held(d)],
        out_specs=tiles(step, d.shape[1]),
        out_shape=jax.ShapeDtypeStruct((width, d.shape[1]), BF16),
        compiler_params=ROOMY,
        cost_estimate=FREE,
        name="outer",
    )(n, d)


def outer_wide_kernel(n_ref, d_ref, g_ref, turned):
    @pl.when(pl.program_id(0) == 0)
    def _():
        turned[...] = n_ref[...].T

    g_ref[...] = dot_nn(turned[...], d_ref[...]).astype(BF16)


def outer_wide(n, d):
    rows, width = n.shape
    step = 256
    column = pl.BlockSpec((rows, step), lambda i: (0, i))
    return pl.pallas_call(
        outer_wide_kernel,
        grid=(d.shape[1] // step,),
        in_specs=[held(n), column],
        out_specs=pl.BlockSpec((width, step), lambda i: (0, i)),
        out_shape=jax.ShapeDtypeStruct((width, d.shape[1]), BF16),
        scratch_shapes=[pltpu.VMEM((width, rows), BF16)],
        compiler_params=ROOMY,
        cost_estimate=FREE,
        name="outer_wide",
    )(n, d)


def device_of(shard, x, core, xs):
    return (shard * xs + x) * 2 + core


def core_swap(a):
    return lax.ppermute(a, "core", [(0, 1), (1, 0)])


def x_swap(a):
    return lax.ppermute(a, "x", [(0, 1), (1, 0)])


def ring_order(shards):
    return list(range(0, shards, 2)) + list(range(shards - 1, 0, -2))


class Ring:
    def __init__(self):
        self.shards, xs = lax.axis_size("shard"), lax.axis_size("x")
        cycle = ring_order(self.shards)
        spot = [cycle.index(s) for s in range(self.shards)]
        self.cycle = jnp.asarray(cycle, jnp.int32)
        self.spot = jnp.asarray(spot, jnp.int32)[lax.axis_index("shard")]
        self.ahead, self.back = (
            [
                (
                    device_of(s, x, c, xs),
                    device_of(cycle[(spot[s] + step) % self.shards], x, c, xs),
                )
                for s in range(self.shards)
                for x in range(xs)
                for c in range(2)
            ]
            for step in (1, -1)
        )
        self.far = self.shards // 2
        self.near = (self.shards - 1) // 2

    def at(self, offset):
        return self.cycle[(self.spot + offset) % self.shards]

    def send(self, a):
        return lax.ppermute(a, AXES, self.ahead)

    def send_back(self, a):
        return lax.ppermute(a, AXES, self.back)


class Gather:
    def __init__(self, ring, piece):
        self.ring, self.hops = ring, 0
        self.ahead = self.back = piece
        self.whole = jnp.zeros((ring.shards,) + piece.shape, piece.dtype)
        self.keep(piece, 0)

    def keep(self, piece, offset):
        self.whole = lax.dynamic_update_index_in_dim(
            self.whole, piece, self.ring.at(offset), 0
        )

    def hop(self, *deps):
        self.hops += 1
        arrived = []
        if self.hops <= self.ring.far:
            self.ahead = after(self.ring.send(self.ahead), *deps)
            self.keep(self.ahead, -self.hops)
            arrived.append((self.ahead, -self.hops))
        if self.hops <= self.ring.near:
            self.back = after(self.ring.send_back(self.back), *deps)
            self.keep(self.back, self.hops)
            arrived.append((self.back, self.hops))
        return arrived


class Scatter:
    def __init__(self, ring, blocks):
        self.ring, self.blocks, self.hops = ring, blocks, 0
        self.ahead, self.back = self.own(ring.far), self.own(-ring.near)
        self.moving = self.ahead

    def own(self, offset, *deps):
        block = lax.dynamic_index_in_dim(self.blocks, self.ring.at(offset), 0, False)
        return after(block, *deps)

    def add(self, *terms):
        total = terms[0].astype(F32)
        for term in terms[1:]:
            total = total + term.astype(F32)
        return total.astype(BF16)

    def hop(self, *deps):
        self.hops += 1
        far, near = self.ring.far - self.hops, self.ring.near - self.hops
        arrived = self.ring.send(self.ahead)
        if near >= 0:
            arrived_back = self.ring.send_back(self.back)
            if near > 0:
                self.back = self.add(arrived_back, self.own(-near, *deps))
            else:
                self.back = arrived_back
        if far > 0:
            self.ahead = self.add(arrived, self.own(far, *deps))
        else:
            self.ahead = self.add(arrived, self.back, self.own(0, *deps))
        self.moving = self.ahead
        return self.moving


def after(a, *deps):
    return lax.optimization_barrier((a,) + deps)[0] if deps else a


def tree_steps():
    shards = lax.axis_size("shard")
    steps = [core_swap]
    if lax.axis_size("x") == 2:
        steps.append(x_swap)
    step = 1
    while step < shards:
        pairs = [(s, s ^ step) for s in range(shards)]
        steps.append(lambda a, pairs=pairs: lax.ppermute(a, "shard", pairs))
        step *= 2
    return steps


def by_core(mine, other, axis):
    first = lax.axis_index("core") == 0
    return jnp.concatenate(
        [jnp.where(first, mine, other), jnp.where(first, other, mine)], axis
    )


def swap_rows(a):
    half = a.shape[0] // 2
    return jnp.concatenate([a[half:], a[:half]], 0)


def core_half(a, axis):
    half = a.shape[axis] // 2
    return lax.dynamic_slice_in_dim(a, lax.axis_index("core") * half, half, axis)


def body(
    tokens,
    attn_gain,
    w_query,
    w_key,
    w_value,
    w_outgate,
    w_rank_in,
    w_rank_out,
    fgate_bias,
    head_gain,
    w_output,
    ffn_gain,
    w_gate,
    w_up,
    w_down,
    out_grad,
):
    seqs, tok_dev, width = tokens.shape
    shards = lax.axis_size("shard")
    xs = lax.axis_size("x")
    core = lax.axis_index("core")
    place = lax.axis_index("shard")
    piece = place % seqs

    def to_chip(step):
        pairs = []
        for j in range(shards):
            for x in range(xs):
                for c in range(2):
                    target = c * seqs + (step + j % seqs) % seqs
                    pairs.append(
                        (device_of(j, x, c, xs), device_of(target, x, j // seqs, xs))
                    )
        return pairs

    def rows_in(a):
        return jnp.concatenate(
            [
                lax.ppermute(
                    lax.dynamic_index_in_dim(a, (step + piece) % seqs, 0, False),
                    AXES,
                    to_chip(step),
                )
                for step in range(seqs)
            ],
            0,
        )

    def rows_out(a):
        back = [
            lax.ppermute(
                a[step * tok_dev : (step + 1) * tok_dev],
                AXES,
                [(t, s) for s, t in to_chip(step)],
            )
            for step in range(seqs)
        ]
        out = jnp.zeros((seqs,) + back[0].shape, a.dtype)
        for step, part in enumerate(back):
            out = lax.dynamic_update_index_in_dim(out, part, (step + piece) % seqs, 0)
        return out

    counter = jnp.arange(shards, dtype=jnp.int32)
    order = ((counter // seqs) ^ core) * seqs + (piece - counter) % seqs
    order = order.astype(jnp.int32)
    sums, masks, upper = level_tables()
    sums, masks, upper = jnp.asarray(sums, BF16), jnp.asarray(masks, F32), jnp.asarray(upper, BF16)

    rank_pack = jnp.concatenate(
        [
            w_rank_in,
            jnp.pad(w_rank_out, ((0, w_rank_in.shape[0] - w_rank_out.shape[0]), (0, 0))),
            jnp.zeros((w_rank_in.shape[0], 96), BF16),
        ],
        1,
    )
    ck, cv = PAIR * DK, PAIR * DV
    packed = jnp.concatenate(
        [core_half(w, 1) for w in (w_query, w_key, w_value, w_outgate, w_output)] + [rank_pack], 1
    )
    wide = 2 * ck + 2 * cv
    own = rows_in(tokens)
    ring = Ring()
    attn_ring = Gather(ring, packed)
    attn_ring.hop()
    attn_ring.ahead, attn_ring.back, own = lax.optimization_barrier(
        (attn_ring.ahead, attn_ring.back, own)
    )
    for _ in range(1, ring.far - 1):
        attn_ring.hop()
    attn_late = attn_ring.ahead
    attn_ring.hop()
    attn_full = attn_ring.whole.reshape(width, -1)
    plane = lax.axis_index("x") == 0
    gate_piece, up_piece = core_half(w_gate, 1), core_half(w_up, 1)
    near_ring = Gather(ring, after(jnp.where(plane, gate_piece, up_piece), attn_late))
    far_ring = Gather(ring, jnp.where(plane, up_piece, gate_piece))
    down_ring = Gather(ring, after(core_half(w_down, 0), attn_late))

    def ffn_hop(*deps):
        down_ring.hop(*deps)
        for piece, offset in near_ring.hop(*deps):
            far_ring.keep(x_swap(piece), offset)

    ffn_hop()
    x_low = jnp.concatenate([own, core_swap(own)], 0)
    attn_row = attn_gain.astype(F32)
    rank_out = attn_full[:, wide + cv + 16 : wide + cv + 32]
    rank_out = rank_out.reshape(shards, -1, 16)[:, : w_rank_out.shape[0]].reshape(-1, 16)
    rank_out = jnp.pad(core_half(rank_out, 0), ((0, 0), (0, 112)))
    bias = core_half(fgate_bias, 0).astype(F32)[None]
    normed, queries, keys, values, out_gate, rank_rows, logits = attn_in(
        x_low, attn_row[None], attn_full, rank_out, bias
    )
    gain = head_gain.astype(F32)[None]
    for _ in range(1, ring.far):
        ffn_hop()
    queries = after(queries, near_ring.ahead, down_ring.ahead)
    own_grad = rows_in(after(out_grad, near_ring.ahead))
    gated, mixed, states = mix_forward(
        order, queries, keys, values, logits, out_gate, gain, sums, masks
    )
    gated_full = by_core(gated, swap_rows(core_swap(gated)), 1)
    out_mine = attn_full[:, wide : wide + cv]
    w_out_full = by_core(out_mine, core_swap(out_mine), 1)
    ffn_row = ffn_gain.astype(F32)
    residual, ffn_in, r_ffn = attn_out(x_low, gated_full, w_out_full, ffn_row[None])
    ffn_in, own_grad = lax.optimization_barrier((ffn_in, own_grad))
    dy = jnp.concatenate([own_grad, core_swap(own_grad)], 0)
    cols_near = near_ring.whole.reshape(width, -1)
    cols_far = far_ring.whole.reshape(width, -1)
    down_rows = down_ring.whole

    ff_half = w_gate.shape[1] // 2
    group = shards // 2
    mine_down = lax.dynamic_slice_in_dim(down_rows, core * group, group, 0)
    send_down = lax.dynamic_slice_in_dim(down_rows, (1 - core) * group, group, 0)
    other_down = core_swap(send_down)
    w_down_half = by_core(mine_down, other_down, 1).reshape(ff_half, width)

    turn = lax.axis_index("x")[None].astype(jnp.int32)
    hidden, d_near, d_far, block_part, dn_part = ffn(
        turn, ffn_in, dy, cols_near, cols_far, w_down_half
    )
    half_rows = x_low.shape[0] // 2
    dn_swapped = core_swap(dn_part)
    block_swapped = core_swap(block_part[half_rows:])
    far_part = outer(ffn_in, d_far)
    grad_far = x_swap(far_part)
    grad_near = outer(after(ffn_in, far_part), d_near)
    block_own = (
        residual[:half_rows] + block_part[:half_rows] + after(block_swapped, far_part)
    ).astype(BF16)
    block_out = rows_out(block_own)
    hidden = after(hidden, grad_near, block_own)
    down_grad = outer_wide(hidden, dy).reshape(group, 2, -1, width)
    mine_dg = lax.dynamic_index_in_dim(down_grad, core, 1, False)
    other_dg = core_swap(lax.dynamic_index_in_dim(down_grad, 1 - core, 1, False))
    down = Scatter(ring, by_core(mine_dg, other_dg, 0))

    d_residual, d_branch, d_gated, ffn_gain_grad = branch(
        dn_part, after(dn_swapped, down.moving), dy, residual, r_ffn, ffn_row[None],
        core_half(w_out_full, 0)
    )
    ffn_gain_grad = ffn_gain_grad[0]
    down.hop(d_gated)
    d_all, d_logits, hgain_part, bias_part = mix_backward(
        order, queries, keys, values, logits, out_gate, mixed, after(d_gated, down.moving, block_out),
        states, gain, sums, masks, upper
    )
    down.hop(d_all)
    d_all = after(d_all, down.moving)
    qkvo_grad = outer(normed, d_all)
    down.hop(qkvo_grad)
    out_w_grad = outer(after(gated_full, down.moving), core_half(d_branch, 1))
    near_total = after(grad_near, out_w_grad).astype(F32) + grad_far.astype(F32)
    last_grad = jnp.concatenate(
        [qkvo_grad, out_w_grad, near_total.astype(BF16)], 1
    )
    attn = Scatter(ring, last_grad.reshape(shards, -1, wide + cv + ff_half))
    down.hop(attn.moving)
    rank_out_grad = outer_sum(rank_rows[:, :16], d_logits)
    rank_part = product(d_logits, rank_out[:, :16])
    rank_swapped = core_swap(rank_part)
    dn_attn = times_transpose(after(d_all, down.moving), attn_full[:, :wide])
    dn_attn_swapped = core_swap(dn_attn[half_rows:])
    attn.hop(dn_attn)
    dn_attn_swapped = after(dn_attn_swapped, down.moving)
    d_rank = (rank_part + swap_rows(rank_swapped)).astype(BF16)
    rank_in_grad = outer_sum(d_rank[:half_rows], normed[:half_rows])
    dn_own = (
        dn_attn[:half_rows]
        + dn_attn_swapped
        + times_transpose(d_rank[:half_rows], attn_full[:, wide + cv : wide + cv + 16])
    )
    own_in = x_low[:half_rows].astype(F32)
    own_r = lax.rsqrt(jnp.mean(own_in * own_in, axis=1, keepdims=True) + EPSILON)
    u = attn_row * dn_own
    tok_grad = (
        d_residual[:half_rows]
        + own_r * (u - own_in * (own_r * own_r) * jnp.mean(u * own_in, axis=1, keepdims=True))
    ).astype(BF16)
    attn_gain_grad = jnp.sum(dn_own * own_in * own_r, axis=0)
    attn.hop(tok_grad)

    first = (core == 0).astype(F32)

    def spread(a):
        return jnp.concatenate([a * first, a * (1.0 - first)], 1)

    rank_out_both = spread(rank_out_grad)
    lanes = 128

    def flat(a):
        return a.reshape(-1, lanes)

    parts = (
        attn_gain_grad[None], spread(bias_part), hgain_part, ffn_gain_grad[None],
        rank_in_grad, rank_out_both,
    )
    small = jnp.concatenate([flat(a) for a in parts], 0)
    steps = tree_steps()
    small = after(small, attn.moving)
    for step in steps[:2]:
        small = small + step(small)
    for _ in range(2, ring.far - 1):
        attn.hop()
    tokens_grad = rows_out(after(tok_grad, attn.moving))
    attn.hop(small)
    small = after(small, attn.moving)
    last_own, down_own = attn.moving, down.moving
    last_far = x_swap(last_own)
    for step in steps[2:-1]:
        small = small + step(small)
    small, last_far = lax.optimization_barrier((small, last_far))
    small = small + steps[-1](small)
    split_at = wide + cv
    near_own, far_own = last_own[:, split_at:], last_far[:, split_at:]
    gate_own = jnp.where(plane, near_own, far_own)
    up_own = jnp.where(plane, far_own, near_own)
    pieces, at = [], 0
    for a in parts:
        size = a.size // lanes
        pieces.append(small[at : at + size].reshape(a.shape))
        at += size
    rin_rows, rout_rows = w_rank_in.shape[0], w_rank_out.shape[0]
    rank_in_own = lax.dynamic_slice_in_dim(pieces[4], place * rin_rows, rin_rows, 1).T
    rank_out_own = lax.dynamic_slice_in_dim(pieces[5].T, place * rout_rows, rout_rows, 0)

    def settle(moving):
        total = moving.astype(F32)
        if xs == 2:
            total = total + x_swap(moving).astype(F32)
        return total, core_swap(total)

    attn_mine = last_own[:, :split_at].astype(F32) + last_far[:, :split_at].astype(F32)
    attn_other = core_swap(attn_mine)

    def columns(mine, other, start, size):
        return by_core(mine[:, start : start + size], other[:, start : start + size], 1)

    return (
        block_out,
        tokens_grad,
        pieces[0][0],
        columns(attn_mine, attn_other, 0, ck),
        columns(attn_mine, attn_other, ck, ck),
        columns(attn_mine, attn_other, 2 * ck, cv),
        columns(attn_mine, attn_other, 2 * ck + cv, cv),
        rank_in_own,
        rank_out_own,
        pieces[1][0],
        pieces[2][0],
        columns(attn_mine, attn_other, wide, cv),
        pieces[3][0],
        by_core(gate_own, core_swap(gate_own), 1).astype(F32),
        by_core(up_own, core_swap(up_own), 1).astype(F32),
        by_core(*settle(down_own), 0),
    )


def solution(mesh):
    shards = mesh.shape["shard"]
    reps = mesh.shape["rep"]

    def run(*arrays):
        tokens = arrays[0]
        seqs = tokens.shape[0] // reps
        narrow = reps == 4 and shards == 2 * seqs and tokens.shape[1] // shards == CHUNK
        if narrow:
            grid = Mesh(mesh.devices.reshape(shards, reps // 2, 2), AXES)
            rep = ("x", "core")
        else:
            grid, rep = mesh, "rep"
        rows, cols = P(rep, "shard", None), P("shard", None)
        in_specs = (rows, P()) + (cols,) * 6 + (P(), P(), cols, P()) + (cols,) * 3 + (rows,)
        out_specs = (rows, rows, P()) + (cols,) * 6 + (P(), P(), cols, P()) + (cols,) * 3
        return jax.shard_map(
            body if narrow else wide_body,
            mesh=grid,
            in_specs=in_specs,
            out_specs=out_specs,
            check_vma=False,
        )(*arrays)

    return run
```

```python
import jax
import jax.numpy as jnp
from jax import lax
import numpy as np
from jax.experimental import pallas as pl
from jax.experimental.pallas import tpu as pltpu
from jax.sharding import Mesh
from jax.sharding import PartitionSpec as P

HEADS = 4
KD = 512
VD = 1024
SPAN = 64
DK = 128
DV = 256


PRECISE = lax.Precision.HIGHEST
EPSILON = 1e-06
GATE_NORM = 16.0


def entering(part, axis, combine, identity, reverse):
    count = lax.axis_size(axis)
    place = lax.axis_index(axis)
    ahead = count - 1 - place if reverse else place
    gathered = jax.tree.map(lambda a: lax.all_gather(a, axis), part)
    state = jax.tree.map(lambda a, e: jnp.zeros_like(a) + jnp.asarray(e, a.dtype), part, identity)

    def one(hop, state):
        source = count - 1 - hop if reverse else hop
        return combine(
            state, jax.tree.map(lambda a: lax.dynamic_index_in_dim(a, source, 0, False), gathered)
        )

    return lax.fori_loop(0, ahead, one, state)


def product(left_side, right_side):
    return jnp.dot(left_side, right_side, preferred_element_type=jnp.float32)


def times_transpose(left_side, right_side):
    return lax.dot_general(
        left_side, right_side, (((1,), (1,)), ((), ())), preferred_element_type=jnp.float32
    )


def outer_sum(left_side, right_side):
    return lax.dot_general(
        left_side, right_side, (((0,), (0,)), ((), ())), preferred_element_type=jnp.float32
    )


def root_norm(values, gain_row):
    return (
        values * lax.rsqrt(jnp.mean(values * values, axis=-1, keepdims=True) + EPSILON) * gain_row
    )


def gated_heads(mixed_rows, gain_row, out_gate):
    heads_normed = root_norm(mixed_rows, gain_row)
    return (heads_normed * jax.nn.silu(out_gate.reshape(mixed_rows.shape))).reshape(out_gate.shape)


def silu_product(gate_rows, up_rows):
    return jax.nn.silu(gate_rows) * up_rows


def forget_log(logits):
    return jax.nn.log_sigmoid(logits) / GATE_NORM


def chain_link(earlier, later):
    return (earlier[0] * later[0], later[0][..., None] * earlier[1] + later[1])


def local_mixing(queries, key_rows, value_rows, decays, start_state):
    cumulated = jnp.cumsum(decays, axis=2)
    closing = cumulated[:, :, -1]
    causal_mask = jnp.arange(SPAN)[:, None] >= jnp.arange(SPAN)[None, :]
    differences = cumulated[:, :, :, None] - cumulated[:, :, None, :]
    differences = jnp.where(causal_mask[:, :, None, None], differences, 0.0)
    weights = jnp.exp(differences)
    scores = jnp.einsum("bntha,bnsha,bntsha->bnhts", queries, key_rows, weights, precision=PRECISE)
    scores = jnp.where(causal_mask, scores, 0.0)
    query_scaled = queries * jnp.exp(cumulated)
    key_tail = key_rows * jnp.exp(closing[:, :, None] - cumulated)
    inner = jnp.einsum("bnhts,bnshe->bnthe", scores, value_rows, precision=PRECISE)
    pieces = jnp.einsum("bnsha,bnshe->nbhae", key_tail, value_rows, precision=PRECISE)
    rates = jnp.exp(jnp.moveaxis(closing, 1, 0))

    def advance(carried, item):
        piece, rate = item
        return (rate[..., None] * carried + piece, carried)

    final_state, starts = lax.scan(advance, start_state, (pieces, rates))
    carried_part = jnp.einsum("bntha,nbhae->bnthe", query_scaled, starts, precision=PRECISE)
    return (inner + carried_part, final_state)


def wide_body(
    tokens,
    attn_gain,
    w_query,
    w_key,
    w_value,
    w_outgate,
    w_rank_in,
    w_rank_out,
    fgate_bias,
    head_gain,
    w_output,
    ffn_gain,
    w_gate,
    w_up,
    w_down,
    out_grad,
):
    seqs, tok_dev, width = tokens.shape
    blocks = tok_dev // SPAN
    count = seqs * tok_dev
    gathered = (
        lax.all_gather(w_query, "shard", axis=0, tiled=True),
        lax.all_gather(w_key, "shard", axis=0, tiled=True),
        lax.all_gather(w_value, "shard", axis=0, tiled=True),
        lax.all_gather(w_outgate, "shard", axis=0, tiled=True),
        lax.all_gather(w_rank_in, "shard", axis=0, tiled=True),
        lax.all_gather(w_rank_out, "shard", axis=0, tiled=True),
        lax.all_gather(w_output, "shard", axis=0, tiled=True),
        lax.all_gather(w_gate, "shard", axis=0, tiled=True),
        lax.all_gather(w_up, "shard", axis=0, tiled=True),
        lax.all_gather(w_down, "shard", axis=0, tiled=True),
    )
    (
        query_full,
        key_full,
        value_full,
        outgate_full,
        rank_in_full,
        rank_out_full,
        output_full,
        gate_full,
        up_full,
        down_full,
    ) = gathered
    inputs = tokens.reshape(count, width).astype(jnp.float32)
    normed, norm_back = jax.vjp(root_norm, inputs, attn_gain.astype(jnp.float32))
    normed_low = normed.astype(jnp.bfloat16)
    queries = product(normed_low, query_full).astype(jnp.bfloat16)
    key_rows = product(normed_low, key_full).astype(jnp.bfloat16)
    value_rows = product(normed_low, value_full).astype(jnp.bfloat16)
    out_gate = product(normed_low, outgate_full)
    rank_rows = product(normed_low, rank_in_full).astype(jnp.bfloat16)
    logits = times_transpose(rank_rows, rank_out_full) + fgate_bias.astype(jnp.float32)
    decays, gate_back = jax.vjp(forget_log, logits)
    shape_key = (seqs, blocks, SPAN, HEADS, DK)
    shape_value = (seqs, blocks, SPAN, HEADS, DV)
    query_blocks = queries.astype(jnp.float32).reshape(shape_key)
    key_blocks = key_rows.astype(jnp.float32).reshape(shape_key)
    value_blocks = value_rows.astype(jnp.float32).reshape(shape_value)
    decay_blocks = decays.reshape(shape_key)
    cumulated = jnp.cumsum(decay_blocks, axis=2)
    block_total = cumulated[:, :, -1]
    running = jnp.cumsum(block_total, axis=1)
    preceding = running - block_total
    device_total = running[:, -1]
    tail_keys = key_blocks * jnp.exp(
        device_total[:, None, None] - preceding[:, :, None] - cumulated
    )
    local_end = jnp.einsum("bntha,bnthe->bhae", tail_keys, value_blocks, precision=PRECISE)
    total_rate = jnp.exp(device_total)
    unit_rate = jnp.ones_like(total_rate)
    scanned = entering(
        (total_rate, local_end), "shard", chain_link, (unit_rate, jnp.zeros_like(local_end)), False
    )
    (mixed, final_state), mix_back = jax.vjp(
        local_mixing, query_blocks, key_blocks, value_blocks, decay_blocks, scanned[1]
    )
    mixed_rows = mixed.reshape(count, HEADS, DV)
    gated, gated_back = jax.vjp(gated_heads, mixed_rows, head_gain.astype(jnp.float32), out_gate)
    gated_low = gated.astype(jnp.bfloat16)
    residual = inputs + product(gated_low, output_full)
    normed_ffn, ffn_norm_back = jax.vjp(root_norm, residual, ffn_gain.astype(jnp.float32))
    ffn_input = normed_ffn.astype(jnp.bfloat16)
    gate_rows = product(ffn_input, gate_full)
    up_rows = product(ffn_input, up_full)
    hidden, act_back = jax.vjp(silu_product, gate_rows, up_rows)
    hidden_low = hidden.astype(jnp.bfloat16)
    block_out = (residual + product(hidden_low, down_full)).astype(jnp.bfloat16)
    grad_rows = out_grad.reshape(count, width)
    down_grad = outer_sum(hidden_low, grad_rows)
    hidden_grad = times_transpose(grad_rows, down_full)
    gate_grad, up_grad = act_back(hidden_grad)
    gate_grad_low = gate_grad.astype(jnp.bfloat16)
    up_grad_low = up_grad.astype(jnp.bfloat16)
    gate_w_grad = outer_sum(ffn_input, gate_grad_low)
    up_w_grad = outer_sum(ffn_input, up_grad_low)
    ffn_input_grad = times_transpose(gate_grad_low, gate_full) + times_transpose(
        up_grad_low, up_full
    )
    residual_part, ffn_gain_grad = ffn_norm_back(ffn_input_grad)
    residual_grad = grad_rows.astype(jnp.float32) + residual_part
    branch_grad = residual_grad.astype(jnp.bfloat16)
    output_w_grad = outer_sum(gated_low, branch_grad)
    gated_grad = times_transpose(branch_grad, output_full)
    mixed_grad, head_gain_grad, out_gate_grad = gated_back(gated_grad)
    mixed_grad_blocks = mixed_grad.reshape(shape_value)
    early_queries = query_blocks * jnp.exp(preceding[:, :, None] + cumulated)
    back_part = jnp.einsum("bntha,bnthe->bhae", early_queries, mixed_grad_blocks, precision=PRECISE)
    rescanned = entering(
        (total_rate, back_part), "shard", chain_link, (unit_rate, jnp.zeros_like(back_part)), True
    )
    pulled = mix_back((mixed_grad_blocks, rescanned[1]))
    query_grad_low = pulled[0].reshape(count, KD).astype(jnp.bfloat16)
    key_grad_low = pulled[1].reshape(count, KD).astype(jnp.bfloat16)
    value_grad_low = pulled[2].reshape(count, VD).astype(jnp.bfloat16)
    logit_grad = gate_back(pulled[3].reshape(count, KD))[0]
    logit_grad_low = logit_grad.astype(jnp.bfloat16)
    out_gate_low = out_gate_grad.astype(jnp.bfloat16)
    bias_grad = jnp.sum(logit_grad_low.astype(jnp.float32), axis=0)
    rank_out_grad = outer_sum(logit_grad_low, rank_rows)
    rank_grad_low = product(logit_grad_low, rank_out_full).astype(jnp.bfloat16)
    rank_in_grad = outer_sum(normed_low, rank_grad_low)
    query_w_grad = outer_sum(normed_low, query_grad_low)
    key_w_grad = outer_sum(normed_low, key_grad_low)
    value_w_grad = outer_sum(normed_low, value_grad_low)
    outgate_w_grad = outer_sum(normed_low, out_gate_low)
    normed_grad = (
        times_transpose(query_grad_low, query_full)
        + times_transpose(key_grad_low, key_full)
        + times_transpose(value_grad_low, value_full)
        + times_transpose(out_gate_low, outgate_full)
        + times_transpose(rank_grad_low, rank_in_full)
    )
    input_part, attn_gain_grad = norm_back(normed_grad)
    tokens_grad = (residual_grad + input_part).astype(jnp.bfloat16).reshape(tokens.shape)
    matrices = (
        query_w_grad,
        key_w_grad,
        value_w_grad,
        outgate_w_grad,
        rank_in_grad,
        rank_out_grad,
        output_w_grad,
        gate_w_grad,
        up_w_grad,
        down_grad,
    )
    owned = (
        lax.psum_scatter(matrices[0], "shard", scatter_dimension=0, tiled=True),
        lax.psum_scatter(matrices[1], "shard", scatter_dimension=0, tiled=True),
        lax.psum_scatter(matrices[2], "shard", scatter_dimension=0, tiled=True),
        lax.psum_scatter(matrices[3], "shard", scatter_dimension=0, tiled=True),
        lax.psum_scatter(matrices[4], "shard", scatter_dimension=0, tiled=True),
        lax.psum_scatter(matrices[5], "shard", scatter_dimension=0, tiled=True),
        lax.psum_scatter(matrices[6], "shard", scatter_dimension=0, tiled=True),
        lax.psum_scatter(matrices[7], "shard", scatter_dimension=0, tiled=True),
        lax.psum_scatter(matrices[8], "shard", scatter_dimension=0, tiled=True),
        lax.psum_scatter(matrices[9], "shard", scatter_dimension=0, tiled=True),
    )
    owned = lax.psum(
        (
            owned[0],
            owned[1],
            owned[2],
            owned[3],
            owned[4],
            owned[5],
            owned[6],
            owned[7],
            owned[8],
            owned[9],
        ),
        "rep",
    )
    small = lax.psum((attn_gain_grad, bias_grad, head_gain_grad, ffn_gain_grad), ("shard", "rep"))
    return (
        block_out.reshape(tokens.shape),
        tokens_grad,
        small[0],
        owned[0],
        owned[1],
        owned[2],
        owned[3],
        owned[4],
        owned[5],
        small[1],
        small[2],
        owned[6],
        small[3],
        owned[7],
        owned[8],
        owned[9],
    )


CHUNK = 128
LEVELS = (64, 32, 16, 8, 4, 2, 1)
PAIR = 2
AXES = ("shard", "x", "core")
BF16 = jnp.bfloat16
F32 = jnp.float32


def level_tables():
    rows = np.arange(CHUNK)
    t, u = rows[:, None], rows[None, :]
    sums = [(u <= t), (u > t)]
    masks = [(t == u)]
    for size in LEVELS:
        same = (t // (2 * size)) == (u // (2 * size))
        late_t = (t % (2 * size)) >= size
        late_u = (u % (2 * size)) >= size
        sums.append(
            same & ((late_t & late_u & (u <= t)) | (~late_t & ~late_u & (u > t)))
        )
        masks.append(same & late_t & ~late_u)
    sums = np.concatenate(sums, 0).astype(np.float32)
    masks = np.stack(masks, 0).astype(np.float32)
    upper = (u >= t).astype(np.float32)
    return (
        np.concatenate([sums, sums], 1),
        masks,
        np.concatenate([upper, upper], 1),
    )


def dot_nn(a, b):
    return lax.dot_general(a, b, (((1,), (0,)), ((), ())), preferred_element_type=F32)


def dot_nt(a, b):
    return lax.dot_general(a, b, (((1,), (1,)), ((), ())), preferred_element_type=F32)


def dot_tn(a, b):
    return lax.dot_general(a, b, (((0,), (0,)), ((), ())), preferred_element_type=F32)


def split(a):
    high = a.astype(BF16)
    return high, (a - high.astype(F32)).astype(BF16)


def fine(dot, a, b):
    ah, al = split(a)
    bh, bl = split(b)
    return dot(ah, bh) + (dot(ah, bl) + dot(al, bh))


def half_fine(dot, a, b):
    ah, al = split(a)
    return dot(ah, b) + dot(al, b)


def summed(table, values):
    high = values.astype(BF16)
    rest = (values - high.astype(F32)).astype(BF16)
    return dot_nn(table, jnp.concatenate([high, rest], 0))


def log_decay(logits):
    return (jnp.minimum(logits, 0.0) - jnp.log(1.0 + jnp.exp(-jnp.abs(logits)))) / GATE_NORM


def sigmoid(z):
    return 1.0 / (1.0 + jnp.exp(-z))


def mix_forward_kernel(
    order, q_ref, k_ref, v_ref, lg_ref, og_ref, gain_ref, sums_ref, mask_ref,
    gated_ref, mixed_ref, states_ref, state
):
    @pl.when(pl.program_id(0) == 0)
    def _():
        state[...] = jnp.zeros_like(state)

    factors = jnp.exp(summed(sums_ref[...], log_decay(lg_ref[...])))
    for head in range(PAIR):
        kc = slice(head * DK, (head + 1) * DK)
        vc = slice(head * DV, (head + 1) * DV)
        q_low, k_low, v_low = q_ref[:, kc], k_ref[:, kc], v_ref[:, vc]
        q, k = q_low.astype(F32), k_low.astype(F32)
        scores = mask_ref[0] * dot_nt(q_low, k_low)
        for level in range(len(LEVELS)):
            e = factors[(level + 2) * CHUNK : (level + 3) * CHUNK, kc]
            scores += mask_ref[level + 1] * fine(dot_nt, q * e, k * e)
        before = factors[:CHUNK, kc]
        after = factors[CHUNK : 2 * CHUNK, kc]
        carried = state[head]
        states_ref[0, head] = carried
        mixed = half_fine(dot_nn, scores, v_low) + fine(dot_nt, q * before, carried)
        k_high, k_rest = split(k * after)
        state[head] = carried * before[CHUNK - 1 :] + (
            dot_tn(v_low, k_high) + dot_tn(v_low, k_rest)
        )
        mixed_ref[:, vc] = mixed
        normed = mixed * lax.rsqrt(jnp.mean(mixed * mixed, axis=1, keepdims=True) + EPSILON)
        og = og_ref[:, vc]
        gated_ref[:, vc] = (normed * gain_ref[...] * (og * sigmoid(og))).astype(BF16)


def mix_backward_kernel(
    order, q_ref, k_ref, v_ref, lg_ref, og_ref, mixed_ref, dg_ref, states_ref, gain_ref,
    sums_ref, mask_ref, upper_ref,
    dall_ref, dlog_ref, hgain_ref, bias_ref, dstate, carry
):
    @pl.when(pl.program_id(0) == 0)
    def _():
        dstate[...] = jnp.zeros_like(dstate)
        carry[...] = jnp.zeros_like(carry)
        hgain_ref[...] = jnp.zeros_like(hgain_ref)
        bias_ref[...] = jnp.zeros_like(bias_ref)

    logits = lg_ref[...]
    factors = jnp.exp(summed(sums_ref[...], log_decay(logits)))
    gain = gain_ref[...]
    flows = []
    for head in range(PAIR):
        kc = slice(head * DK, (head + 1) * DK)
        vc = slice(head * DV, (head + 1) * DV)
        og, m, dg = og_ref[:, vc], mixed_ref[:, vc], dg_ref[:, vc]
        sig = sigmoid(og)
        r = lax.rsqrt(jnp.mean(m * m, axis=1, keepdims=True) + EPSILON)
        n = m * r
        dn = dg * (og * sig)
        hgain_ref[...] += jnp.sum(dn * n, axis=0, keepdims=True)
        u = gain * dn
        dm = r * (u - n * jnp.mean(u * n, axis=1, keepdims=True))
        dog = dg * (n * gain) * (sig * (1.0 + og * (1.0 - sig)))
        dall_ref[:, 2 * PAIR * DK + PAIR * DV + head * DV : 2 * PAIR * DK + PAIR * DV + (head + 1) * DV] = dog.astype(BF16)
        dm_low = dm.astype(BF16)
        q_low, k_low, v_low = q_ref[:, kc], k_ref[:, kc], v_ref[:, vc]
        q, k = q_low.astype(F32), k_low.astype(F32)
        dm_rest = (dm - dm_low.astype(F32)).astype(BF16)
        da = dot_nt(dm_low, v_low) + dot_nt(dm_rest, v_low)
        before = factors[:CHUNK, kc]
        after = factors[CHUNK : 2 * CHUNK, kc]
        carried = states_ref[0, head]
        ds = dstate[head]
        ds_low = ds.astype(BF16)
        q_in = (q * before).astype(BF16)
        k_out = (k * after).astype(BF16)
        scores = mask_ref[0] * dot_nt(q_low, k_low)
        part = (mask_ref[0] * da).astype(BF16)
        dq = dot_nn(part, k_low) + before * dot_nn(dm_low, carried.astype(BF16))
        dk = dot_tn(part, q_low) + after * dot_nn(v_low, ds_low)
        for level in range(len(LEVELS)):
            e = factors[(level + 2) * CHUNK : (level + 3) * CHUNK, kc]
            q_e, k_e = (q * e).astype(BF16), (k * e).astype(BF16)
            scores += mask_ref[level + 1] * dot_nt(q_e, k_e)
            part = (mask_ref[level + 1] * da).astype(BF16)
            dq += e * dot_nn(part, k_e)
            dk += e * dot_tn(part, q_e)
        dv = dot_tn(scores.astype(BF16), dm_low) + dot_nt(k_out, ds_low)
        dall_ref[:, kc] = dq.astype(BF16)
        dall_ref[:, PAIR * DK + head * DK : PAIR * DK + (head + 1) * DK] = dk.astype(BF16)
        dall_ref[:, 2 * PAIR * DK + head * DV : 2 * PAIR * DK + (head + 1) * DV] = dv.astype(BF16)
        ds = ds * before[CHUNK - 1 :] + dot_tn(dm_low, q_in)
        dstate[head] = ds
        flows.append(q * dq - k * dk)
        carried_flow = jnp.sum(carried * ds, axis=0, keepdims=True)
        flows.append(carried_flow)
    flow = jnp.concatenate([flows[0], flows[2]], 1)
    d_decay = summed(upper_ref[...], flow) + carry[...]
    carry[...] = jnp.concatenate([flows[1], flows[3]], 1)
    dlog = (d_decay * (sigmoid(-logits) * (1.0 / GATE_NORM))).astype(BF16)
    dlog_ref[...] = dlog
    bias_ref[...] += jnp.sum(dlog.astype(F32), axis=0, keepdims=True)


def mix_forward(order, q, k, v, logits, og, gain, sums, masks):
    rows = q.shape[0]
    steps = rows // CHUNK
    ck, cv = PAIR * DK, PAIR * DV

    def row_block(width):
        return pl.BlockSpec((CHUNK, width), lambda g, o: (o[g], 0))

    def whole(a):
        return pl.BlockSpec(a.shape, lambda g, o: (0,) * a.ndim)

    return pl.pallas_call(
        mix_forward_kernel,
        grid_spec=pltpu.PrefetchScalarGridSpec(
            num_scalar_prefetch=1,
            grid=(steps,),
            in_specs=[row_block(ck), row_block(ck), row_block(cv), row_block(ck), row_block(cv),
                      whole(gain), whole(sums), whole(masks)],
            out_specs=[row_block(cv), row_block(cv),
                       pl.BlockSpec((1, PAIR, DV, DK), lambda g, o: (g, 0, 0, 0))],
            scratch_shapes=[pltpu.VMEM((PAIR, DV, DK), F32)],
        ),
        out_shape=[jax.ShapeDtypeStruct((rows, cv), BF16), jax.ShapeDtypeStruct((rows, cv), F32),
                   jax.ShapeDtypeStruct((steps, PAIR, DV, DK), F32)],
        compiler_params=pltpu.CompilerParams(vmem_limit_bytes=58 * 1024 * 1024),
        cost_estimate=pl.CostEstimate(flops=22_000_000_000, bytes_accessed=1000, transcendentals=0),
        name="mix_forward",
    )(order, q, k, v, logits, og, gain, sums, masks)


def mix_backward(order, q, k, v, logits, og, mixed, d_gated, states, gain, sums, masks, upper):
    rows = q.shape[0]
    steps = rows // CHUNK
    ck, cv = PAIR * DK, PAIR * DV

    def row_block(width):
        return pl.BlockSpec((CHUNK, width), lambda g, o: (o[steps - 1 - g], 0))

    def whole(a):
        return pl.BlockSpec(a.shape, lambda g, o: (0,) * a.ndim)

    return pl.pallas_call(
        mix_backward_kernel,
        grid_spec=pltpu.PrefetchScalarGridSpec(
            num_scalar_prefetch=1,
            grid=(steps,),
            in_specs=[row_block(ck), row_block(ck), row_block(cv), row_block(ck), row_block(cv),
                      row_block(cv), row_block(cv),
                      pl.BlockSpec((1, PAIR, DV, DK), lambda g, o: (steps - 1 - g, 0, 0, 0)),
                      whole(gain), whole(sums), whole(masks), whole(upper)],
            out_specs=[row_block(2 * ck + 2 * cv), row_block(ck),
                       pl.BlockSpec((1, DV), lambda g, o: (0, 0)),
                       pl.BlockSpec((1, ck), lambda g, o: (0, 0))],
            scratch_shapes=[pltpu.VMEM((PAIR, DV, DK), F32), pltpu.VMEM((1, ck), F32)],
        ),
        out_shape=[jax.ShapeDtypeStruct((rows, 2 * ck + 2 * cv), BF16), jax.ShapeDtypeStruct((rows, ck), BF16),
                   jax.ShapeDtypeStruct((1, DV), F32), jax.ShapeDtypeStruct((1, ck), F32)],
        compiler_params=pltpu.CompilerParams(vmem_limit_bytes=58 * 1024 * 1024),
        cost_estimate=pl.CostEstimate(flops=6_000_000_000, bytes_accessed=1000, transcendentals=0),
        name="mix_backward",
    )(order, q, k, v, logits, og, mixed, d_gated, states, gain, sums, masks, upper)


FREE = pl.CostEstimate(flops=1000, bytes_accessed=1000, transcendentals=0)
ROOMY = pltpu.CompilerParams(vmem_limit_bytes=58 * 1024 * 1024)


def held(a):
    return pl.BlockSpec(a.shape, lambda *g: (0,) * a.ndim, pipeline_mode=pl.Buffered(1))


def tiles(rows, width):
    return pl.BlockSpec((rows, width), lambda g: (g, 0))


def attn_in_kernel(x_ref, gain_ref, w_ref, rank_ref, bias_ref, n_ref, q_ref, k_ref, v_ref, og_ref, rr_ref, lg_ref):
    ck, cv = q_ref.shape[1], v_ref.shape[1]
    x = x_ref[...].astype(F32)
    r = lax.rsqrt(jnp.mean(x * x, axis=1, keepdims=True) + EPSILON)
    n = (x * r * gain_ref[...]).astype(BF16)
    n_ref[...] = n
    q_ref[...] = dot_nn(n, w_ref[:, :ck]).astype(BF16)
    k_ref[...] = dot_nn(n, w_ref[:, ck : 2 * ck]).astype(BF16)
    v_ref[...] = dot_nn(n, w_ref[:, 2 * ck : 2 * ck + cv]).astype(BF16)
    og_ref[...] = dot_nn(n, w_ref[:, 2 * ck + cv : 2 * ck + 2 * cv])
    rank = dot_nn(n, w_ref[:, 2 * ck + 3 * cv :]).astype(BF16)
    rr_ref[...] = rank
    lg_ref[...] = dot_nt(rank, rank_ref[...]) + bias_ref[...]


def attn_in(x, gain, w, rank, bias):
    rows, ck, cv, step = x.shape[0], PAIR * DK, PAIR * DV, 256
    shapes = [(x.shape[1], BF16), (ck, BF16), (ck, BF16), (cv, BF16), (cv, F32), (128, BF16), (ck, F32)]
    return pl.pallas_call(
        attn_in_kernel,
        grid=(rows // step,),
        in_specs=[tiles(step, x.shape[1]), held(gain), held(w), held(rank), held(bias)],
        out_specs=[tiles(step, c) for c, _ in shapes],
        out_shape=[jax.ShapeDtypeStruct((rows, c), t) for c, t in shapes],
        compiler_params=ROOMY,
        cost_estimate=FREE,
        name="attn_in",
    )(x, gain, w, rank, bias)


def attn_out_kernel(x_ref, g_ref, w_ref, gain_ref, res_ref, n_ref, r_ref):
    res = x_ref[...].astype(F32) + dot_nn(g_ref[...], w_ref[...])
    r = lax.rsqrt(jnp.mean(res * res, axis=1, keepdims=True) + EPSILON)
    res_ref[...] = res
    n_ref[...] = (res * r * gain_ref[...]).astype(BF16)
    r_ref[...] = r


def attn_out(x, gated, w, gain):
    rows, width = x.shape
    step = 256
    return pl.pallas_call(
        attn_out_kernel,
        grid=(rows // step,),
        in_specs=[tiles(step, width), tiles(step, gated.shape[1]), held(w), held(gain)],
        out_specs=[tiles(step, width), tiles(step, width), tiles(step, 1)],
        out_shape=[jax.ShapeDtypeStruct((rows, width), F32), jax.ShapeDtypeStruct((rows, width), BF16),
                   jax.ShapeDtypeStruct((rows, 1), F32)],
        compiler_params=ROOMY,
        cost_estimate=FREE,
        name="attn_out",
    )(x, gated, w, gain)


def ffn_kernel(plane, n_ref, dy_ref, near_ref, far_ref, down_ref, hid_ref, near_d_ref, far_d_ref, mine_ref, other_ref, dn_ref):
    straight = plane[0] == 0
    n = n_ref[...]
    near = dot_nn(n, near_ref[...])
    far = dot_nn(n, far_ref[...])
    gate, up = jnp.where(straight, near, far), jnp.where(straight, far, near)
    sig = sigmoid(gate)
    act = gate * sig
    hidden = (act * up).astype(BF16)
    hid_ref[...] = hidden
    d_hidden = dot_nt(dy_ref[...], down_ref[...])
    d_gate = d_hidden * up * (sig + act * (1.0 - sig))
    d_up = d_hidden * act
    d_near = jnp.where(straight, d_gate, d_up).astype(BF16)
    d_far = jnp.where(straight, d_up, d_gate).astype(BF16)
    near_d_ref[...] = d_near
    far_d_ref[...] = d_far
    block = dot_nn(hidden, down_ref[...])
    first = pl.program_id(0) < pl.num_programs(0) // 2

    @pl.when(first)
    def _():
        mine_ref[...] = block

    @pl.when(jnp.logical_not(first))
    def _():
        other_ref[...] = block

    dn_ref[...] = dot_nt(d_near, near_ref[...]) + dot_nt(d_far, far_ref[...])


def ffn(plane, n, dy, near, far, down):
    rows, width = n.shape
    ff, step = near.shape[1], 256

    def row(width):
        return pl.BlockSpec((step, width), lambda g, p: (g, 0))

    half = rows // step // 2
    early = pl.BlockSpec((step, width), lambda g, p: (jnp.minimum(g, half - 1), 0))
    late = pl.BlockSpec((step, width), lambda g, p: (jnp.maximum(g - half, 0), 0))
    return pl.pallas_call(
        ffn_kernel,
        grid_spec=pltpu.PrefetchScalarGridSpec(
            num_scalar_prefetch=1,
            grid=(rows // step,),
            in_specs=[row(width), row(width), held(near), held(far), held(down)],
            out_specs=[row(ff), row(ff), row(ff), early, late, row(width)],
        ),
        out_shape=[jax.ShapeDtypeStruct((rows, ff), BF16)] * 3
        + [jax.ShapeDtypeStruct((rows // 2, width), F32)] * 2
        + [jax.ShapeDtypeStruct((rows, width), F32)],
        compiler_params=ROOMY,
        cost_estimate=FREE,
        name="ffn",
    )(plane, n, dy, near, far, down)


def branch_kernel(dn_ref, sw_ref, dy_ref, res_ref, r_ref, gain_ref, w_ref, d_ref, low_ref, dg_ref, fg_ref):
    step = pl.program_id(0)

    @pl.when(step == 0)
    def _():
        fg_ref[...] = jnp.zeros_like(fg_ref)

    dn = dn_ref[...] + sw_ref[...]
    res, r = res_ref[...], r_ref[...]
    n = res * r

    @pl.when(step < pl.num_programs(0) // 2)
    def _():
        fg_ref[...] += jnp.sum(dn * n, axis=0, keepdims=True)

    u = gain_ref[...] * dn
    d = dy_ref[...].astype(F32) + r * (u - n * jnp.mean(u * n, axis=1, keepdims=True))
    low = d.astype(BF16)
    d_ref[...] = d
    low_ref[...] = low
    dg_ref[...] = dot_nt(low, w_ref[...])


def branch(dn, swapped, dy, res, r, gain, w):
    rows, width = dn.shape
    step = 256
    count = rows // step
    other = pl.BlockSpec((step, width), lambda g: ((g + count // 2) % count, 0))
    full = tiles(step, width)
    return pl.pallas_call(
        branch_kernel,
        grid=(count,),
        in_specs=[full, other, full, full, tiles(step, 1), held(gain), held(w)],
        out_specs=[full, full, tiles(step, w.shape[0]), pl.BlockSpec((1, width), lambda g: (0, 0))],
        out_shape=[jax.ShapeDtypeStruct((rows, width), F32), jax.ShapeDtypeStruct((rows, width), BF16),
                   jax.ShapeDtypeStruct((rows, w.shape[0]), F32), jax.ShapeDtypeStruct((1, width), F32)],
        compiler_params=ROOMY,
        cost_estimate=FREE,
        name="branch",
    )(dn, swapped, dy, res, r, gain, w)


def outer_kernel(n_ref, d_ref, g_ref):
    g_ref[...] = dot_tn(n_ref[...], d_ref[...]).astype(BF16)


def outer(n, d, step=256):
    rows, width = n.shape
    return pl.pallas_call(
        outer_kernel,
        grid=(width // step,),
        in_specs=[pl.BlockSpec((rows, step), lambda i: (0, i)), held(d)],
        out_specs=tiles(step, d.shape[1]),
        out_shape=jax.ShapeDtypeStruct((width, d.shape[1]), BF16),
        compiler_params=ROOMY,
        cost_estimate=FREE,
        name="outer",
    )(n, d)


def outer_wide_kernel(n_ref, d_ref, g_ref, turned):
    @pl.when(pl.program_id(0) == 0)
    def _():
        turned[...] = n_ref[...].T

    g_ref[...] = dot_nn(turned[...], d_ref[...]).astype(BF16)


def outer_wide(n, d):
    rows, width = n.shape
    step = 256
    column = pl.BlockSpec((rows, step), lambda i: (0, i))
    return pl.pallas_call(
        outer_wide_kernel,
        grid=(d.shape[1] // step,),
        in_specs=[held(n), column],
        out_specs=pl.BlockSpec((width, step), lambda i: (0, i)),
        out_shape=jax.ShapeDtypeStruct((width, d.shape[1]), BF16),
        scratch_shapes=[pltpu.VMEM((width, rows), BF16)],
        compiler_params=ROOMY,
        cost_estimate=FREE,
        name="outer_wide",
    )(n, d)


def device_of(shard, x, core, xs):
    return (shard * xs + x) * 2 + core


def core_swap(a):
    return lax.ppermute(a, "core", [(0, 1), (1, 0)])


def x_swap(a):
    return lax.ppermute(a, "x", [(0, 1), (1, 0)])


def ring_order(shards):
    return list(range(0, shards, 2)) + list(range(shards - 1, 0, -2))


class Ring:
    def __init__(self):
        self.shards, xs = lax.axis_size("shard"), lax.axis_size("x")
        cycle = ring_order(self.shards)
        spot = [cycle.index(s) for s in range(self.shards)]
        self.cycle = jnp.asarray(cycle, jnp.int32)
        self.spot = jnp.asarray(spot, jnp.int32)[lax.axis_index("shard")]
        self.ahead, self.back = (
            [
                (
                    device_of(s, x, c, xs),
                    device_of(cycle[(spot[s] + step) % self.shards], x, c, xs),
                )
                for s in range(self.shards)
                for x in range(xs)
                for c in range(2)
            ]
            for step in (1, -1)
        )
        self.far = self.shards // 2
        self.near = (self.shards - 1) // 2

    def at(self, offset):
        return self.cycle[(self.spot + offset) % self.shards]

    def send(self, a):
        return lax.ppermute(a, AXES, self.ahead)

    def send_back(self, a):
        return lax.ppermute(a, AXES, self.back)


class Gather:
    def __init__(self, ring, piece):
        self.ring, self.hops = ring, 0
        self.ahead = self.back = piece
        self.whole = jnp.zeros((ring.shards,) + piece.shape, piece.dtype)
        self.keep(piece, 0)

    def keep(self, piece, offset):
        self.whole = lax.dynamic_update_index_in_dim(
            self.whole, piece, self.ring.at(offset), 0
        )

    def hop(self, *deps):
        self.hops += 1
        arrived = []
        if self.hops <= self.ring.far:
            self.ahead = after(self.ring.send(self.ahead), *deps)
            self.keep(self.ahead, -self.hops)
            arrived.append((self.ahead, -self.hops))
        if self.hops <= self.ring.near:
            self.back = after(self.ring.send_back(self.back), *deps)
            self.keep(self.back, self.hops)
            arrived.append((self.back, self.hops))
        return arrived


class Scatter:
    def __init__(self, ring, blocks):
        self.ring, self.blocks, self.hops = ring, blocks, 0
        self.ahead, self.back = self.own(ring.far), self.own(-ring.near)
        self.moving = self.ahead

    def own(self, offset, *deps):
        block = lax.dynamic_index_in_dim(self.blocks, self.ring.at(offset), 0, False)
        return after(block, *deps)

    def add(self, *terms):
        total = terms[0].astype(F32)
        for term in terms[1:]:
            total = total + term.astype(F32)
        return total.astype(BF16)

    def hop(self, *deps):
        self.hops += 1
        far, near = self.ring.far - self.hops, self.ring.near - self.hops
        arrived = self.ring.send(self.ahead)
        if near >= 0:
            arrived_back = self.ring.send_back(self.back)
            if near > 0:
                self.back = self.add(arrived_back, self.own(-near, *deps))
            else:
                self.back = arrived_back
        if far > 0:
            self.ahead = self.add(arrived, self.own(far, *deps))
        else:
            self.ahead = self.add(arrived, self.back, self.own(0, *deps))
        self.moving = self.ahead
        return self.moving


def after(a, *deps):
    return lax.optimization_barrier((a,) + deps)[0] if deps else a


def tree_steps():
    shards = lax.axis_size("shard")
    steps = [core_swap]
    if lax.axis_size("x") == 2:
        steps.append(x_swap)
    step = 1
    while step < shards:
        pairs = [(s, s ^ step) for s in range(shards)]
        steps.append(lambda a, pairs=pairs: lax.ppermute(a, "shard", pairs))
        step *= 2
    return steps


def by_core(mine, other, axis):
    first = lax.axis_index("core") == 0
    return jnp.concatenate(
        [jnp.where(first, mine, other), jnp.where(first, other, mine)], axis
    )


def swap_rows(a):
    half = a.shape[0] // 2
    return jnp.concatenate([a[half:], a[:half]], 0)


def core_half(a, axis):
    half = a.shape[axis] // 2
    return lax.dynamic_slice_in_dim(a, lax.axis_index("core") * half, half, axis)


def body(
    tokens,
    attn_gain,
    w_query,
    w_key,
    w_value,
    w_outgate,
    w_rank_in,
    w_rank_out,
    fgate_bias,
    head_gain,
    w_output,
    ffn_gain,
    w_gate,
    w_up,
    w_down,
    out_grad,
):
    seqs, tok_dev, width = tokens.shape
    shards = lax.axis_size("shard")
    xs = lax.axis_size("x")
    core = lax.axis_index("core")
    place = lax.axis_index("shard")
    piece = place % seqs

    def to_chip(step):
        pairs = []
        for j in range(shards):
            for x in range(xs):
                for c in range(2):
                    target = c * seqs + (step + j % seqs) % seqs
                    pairs.append(
                        (device_of(j, x, c, xs), device_of(target, x, j // seqs, xs))
                    )
        return pairs

    def rows_in(a):
        return jnp.concatenate(
            [
                lax.ppermute(
                    lax.dynamic_index_in_dim(a, (step + piece) % seqs, 0, False),
                    AXES,
                    to_chip(step),
                )
                for step in range(seqs)
            ],
            0,
        )

    def rows_out(a):
        back = [
            lax.ppermute(
                a[step * tok_dev : (step + 1) * tok_dev],
                AXES,
                [(t, s) for s, t in to_chip(step)],
            )
            for step in range(seqs)
        ]
        out = jnp.zeros((seqs,) + back[0].shape, a.dtype)
        for step, part in enumerate(back):
            out = lax.dynamic_update_index_in_dim(out, part, (step + piece) % seqs, 0)
        return out

    counter = jnp.arange(shards, dtype=jnp.int32)
    order = ((counter // seqs) ^ core) * seqs + (piece - counter) % seqs
    order = order.astype(jnp.int32)
    sums, masks, upper = level_tables()
    sums, masks, upper = jnp.asarray(sums, BF16), jnp.asarray(masks, F32), jnp.asarray(upper, BF16)

    rank_pack = jnp.concatenate(
        [
            w_rank_in,
            jnp.pad(w_rank_out, ((0, w_rank_in.shape[0] - w_rank_out.shape[0]), (0, 0))),
            jnp.zeros((w_rank_in.shape[0], 96), BF16),
        ],
        1,
    )
    ck, cv = PAIR * DK, PAIR * DV
    packed = jnp.concatenate(
        [core_half(w, 1) for w in (w_query, w_key, w_value, w_outgate, w_output)] + [rank_pack], 1
    )
    wide = 2 * ck + 2 * cv
    own = rows_in(tokens)
    ring = Ring()
    attn_ring = Gather(ring, packed)
    attn_ring.hop()
    attn_ring.ahead, attn_ring.back, own = lax.optimization_barrier(
        (attn_ring.ahead, attn_ring.back, own)
    )
    for _ in range(1, ring.far - 1):
        attn_ring.hop()
    attn_late = attn_ring.ahead
    attn_ring.hop()
    attn_full = attn_ring.whole.reshape(width, -1)
    plane = lax.axis_index("x") == 0
    gate_piece, up_piece = core_half(w_gate, 1), core_half(w_up, 1)
    near_ring = Gather(ring, after(jnp.where(plane, gate_piece, up_piece), attn_late))
    far_ring = Gather(ring, jnp.where(plane, up_piece, gate_piece))
    down_ring = Gather(ring, after(core_half(w_down, 0), attn_late))

    def ffn_hop(*deps):
        down_ring.hop(*deps)
        for piece, offset in near_ring.hop(*deps):
            far_ring.keep(x_swap(piece), offset)

    ffn_hop()
    x_low = jnp.concatenate([own, core_swap(own)], 0)
    attn_row = attn_gain.astype(F32)
    rank_out = attn_full[:, wide + cv + 16 : wide + cv + 32]
    rank_out = rank_out.reshape(shards, -1, 16)[:, : w_rank_out.shape[0]].reshape(-1, 16)
    rank_out = jnp.pad(core_half(rank_out, 0), ((0, 0), (0, 112)))
    bias = core_half(fgate_bias, 0).astype(F32)[None]
    normed, queries, keys, values, out_gate, rank_rows, logits = attn_in(
        x_low, attn_row[None], attn_full, rank_out, bias
    )
    gain = head_gain.astype(F32)[None]
    for _ in range(1, ring.far):
        ffn_hop()
    out_mine = attn_full[:, wide : wide + cv]
    w_out_full = by_core(out_mine, core_swap(out_mine), 1)
    queries = after(queries, near_ring.ahead, down_ring.ahead, w_out_full)
    own_grad = rows_in(after(out_grad, near_ring.ahead))
    gated, mixed, states = mix_forward(
        order, queries, keys, values, logits, out_gate, gain, sums, masks
    )
    gated_full = by_core(gated, swap_rows(core_swap(gated)), 1)
    ffn_row = ffn_gain.astype(F32)
    residual, ffn_in, r_ffn = attn_out(x_low, gated_full, w_out_full, ffn_row[None])
    ffn_in, own_grad = lax.optimization_barrier((ffn_in, own_grad))
    dy = jnp.concatenate([own_grad, core_swap(own_grad)], 0)
    cols_near = near_ring.whole.reshape(width, -1)
    cols_far = far_ring.whole.reshape(width, -1)
    down_rows = down_ring.whole

    ff_half = w_gate.shape[1] // 2
    group = shards // 2
    mine_down = lax.dynamic_slice_in_dim(down_rows, core * group, group, 0)
    send_down = lax.dynamic_slice_in_dim(down_rows, (1 - core) * group, group, 0)
    other_down = core_swap(send_down)
    w_down_half = by_core(mine_down, other_down, 1).reshape(ff_half, width)

    turn = lax.axis_index("x")[None].astype(jnp.int32)
    hidden, d_near, d_far, block_mine, block_other, dn_part = ffn(
        turn, ffn_in, dy, cols_near, cols_far, w_down_half
    )
    half_rows = x_low.shape[0] // 2
    dn_swapped = core_swap(dn_part)
    block_swapped = core_swap(block_other)
    far_part = outer_sum(ffn_in, d_far).astype(BF16)
    grad_far = x_swap(far_part)
    grad_near = outer_sum(after(ffn_in, far_part), d_near).astype(BF16)
    block_own = (
        residual[:half_rows] + block_mine + after(block_swapped, far_part)
    ).astype(BF16)
    block_out = rows_out(block_own)
    hidden = after(hidden, grad_near, block_own)
    down_grad = outer_sum(hidden, dy).astype(BF16).reshape(group, 2, -1, width)
    mine_dg = lax.dynamic_index_in_dim(down_grad, core, 1, False)
    other_dg = core_swap(lax.dynamic_index_in_dim(down_grad, 1 - core, 1, False))
    down = Scatter(ring, by_core(mine_dg, other_dg, 0))

    d_residual, d_branch, d_gated, ffn_gain_grad = branch(
        dn_part, after(dn_swapped, down.moving), dy, residual, r_ffn, ffn_row[None],
        core_half(w_out_full, 0)
    )
    ffn_gain_grad = ffn_gain_grad[0]
    down.hop(d_gated)
    d_all, d_logits, hgain_part, bias_part = mix_backward(
        order, queries, keys, values, logits, out_gate, mixed, after(d_gated, down.moving, block_out),
        states, gain, sums, masks, upper
    )
    down.hop(d_all)
    d_all = after(d_all, down.moving)
    qkvo_grad = outer_sum(normed, d_all).astype(BF16)
    down.hop(qkvo_grad)
    out_w_grad = outer_sum(after(gated_full, down.moving), core_half(d_branch, 1)).astype(BF16)
    near_total = after(grad_near, out_w_grad).astype(F32) + grad_far.astype(F32)
    last_grad = jnp.concatenate(
        [qkvo_grad, out_w_grad, near_total.astype(BF16)], 1
    )
    attn = Scatter(ring, last_grad.reshape(shards, -1, wide + cv + ff_half))
    down.hop(attn.moving)
    rank_out_grad = outer_sum(rank_rows[:, :16], d_logits)
    rank_part = product(d_logits, rank_out[:, :16])
    rank_swapped = core_swap(rank_part)
    dn_attn = times_transpose(after(d_all, down.moving), attn_full[:, :wide])
    dn_attn_swapped = core_swap(dn_attn[half_rows:])
    attn.hop(dn_attn)
    dn_attn_swapped = after(dn_attn_swapped, down.moving)
    d_rank = (rank_part + swap_rows(rank_swapped)).astype(BF16)
    rank_in_grad = outer_sum(d_rank[:half_rows], normed[:half_rows])
    dn_own = (
        dn_attn[:half_rows]
        + dn_attn_swapped
        + times_transpose(d_rank[:half_rows], attn_full[:, wide + cv : wide + cv + 16])
    )
    own_in = x_low[:half_rows].astype(F32)
    own_r = lax.rsqrt(jnp.mean(own_in * own_in, axis=1, keepdims=True) + EPSILON)
    u = attn_row * dn_own
    tok_grad = (
        d_residual[:half_rows]
        + own_r * (u - own_in * (own_r * own_r) * jnp.mean(u * own_in, axis=1, keepdims=True))
    ).astype(BF16)
    attn_gain_grad = jnp.sum(dn_own * own_in * own_r, axis=0)
    attn.hop(tok_grad)

    first = (core == 0).astype(F32)

    def spread(a):
        return jnp.concatenate([a * first, a * (1.0 - first)], 1)

    rank_out_both = spread(rank_out_grad)
    lanes = 128

    def flat(a):
        return a.reshape(-1, lanes)

    parts = (
        attn_gain_grad[None], spread(bias_part), hgain_part, ffn_gain_grad[None],
        rank_in_grad, rank_out_both,
    )
    small = jnp.concatenate([flat(a) for a in parts], 0)
    steps = tree_steps()
    small = after(small, attn.moving)
    for step in steps[:2]:
        small = small + step(small)
    for _ in range(2, ring.far - 1):
        attn.hop()
    tokens_grad = rows_out(after(tok_grad, attn.moving))
    attn.hop(small)
    small = after(small, attn.moving)
    last_own, down_own = attn.moving, down.moving
    last_far = x_swap(last_own)
    for step in steps[2:-1]:
        small = small + step(small)
    small, last_far = lax.optimization_barrier((small, last_far))
    small = small + steps[-1](small)
    split_at = wide + cv
    near_own, far_own = last_own[:, split_at:], last_far[:, split_at:]
    gate_own = jnp.where(plane, near_own, far_own)
    up_own = jnp.where(plane, far_own, near_own)
    pieces, at = [], 0
    for a in parts:
        size = a.size // lanes
        pieces.append(small[at : at + size].reshape(a.shape))
        at += size
    rin_rows, rout_rows = w_rank_in.shape[0], w_rank_out.shape[0]
    rank_in_own = lax.dynamic_slice_in_dim(pieces[4], place * rin_rows, rin_rows, 1).T
    rank_out_own = lax.dynamic_slice_in_dim(pieces[5].T, place * rout_rows, rout_rows, 0)

    def settle(moving):
        total = moving.astype(F32)
        if xs == 2:
            total = total + x_swap(moving).astype(F32)
        return total, core_swap(total)

    attn_mine = last_own[:, :split_at].astype(F32) + last_far[:, :split_at].astype(F32)
    attn_other = core_swap(attn_mine)

    def columns(mine, other, start, size):
        return by_core(mine[:, start : start + size], other[:, start : start + size], 1)

    return (
        block_out,
        tokens_grad,
        pieces[0][0],
        columns(attn_mine, attn_other, 0, ck),
        columns(attn_mine, attn_other, ck, ck),
        columns(attn_mine, attn_other, 2 * ck, cv),
        columns(attn_mine, attn_other, 2 * ck + cv, cv),
        rank_in_own,
        rank_out_own,
        pieces[1][0],
        pieces[2][0],
        columns(attn_mine, attn_other, wide, cv),
        pieces[3][0],
        by_core(gate_own, core_swap(gate_own), 1).astype(F32),
        by_core(up_own, core_swap(up_own), 1).astype(F32),
        by_core(*settle(down_own), 0),
    )


def solution(mesh):
    shards = mesh.shape["shard"]
    reps = mesh.shape["rep"]

    def run(*arrays):
        tokens = arrays[0]
        seqs = tokens.shape[0] // reps
        narrow = reps == 4 and shards == 2 * seqs and tokens.shape[1] // shards == CHUNK
        if narrow:
            grid = Mesh(mesh.devices.reshape(shards, reps // 2, 2), AXES)
            rep = ("x", "core")
        else:
            grid, rep = mesh, "rep"
        rows, cols = P(rep, "shard", None), P("shard", None)
        in_specs = (rows, P()) + (cols,) * 6 + (P(), P(), cols, P()) + (cols,) * 3 + (rows,)
        out_specs = (rows, rows, P()) + (cols,) * 6 + (P(), P(), cols, P()) + (cols,) * 3
        return jax.shard_map(
            body if narrow else wide_body,
            mesh=grid,
            in_specs=in_specs,
            out_specs=out_specs,
            check_vma=False,
        )(*arrays)

    return run
```
